32 devices in a mesh: dp: 8 (over z, x), mp: 4 (over y, core).
Axes of the slice: x: 2, y: 2, z: 4, core: 2. Of those that a mesh axis runs over, the one named last changes fastest.
Arguments:
- tokens: float32 [2048, 1024], P('dp'), may hold values from -6 to 6
- w_qkv: bfloat16 [1024, 3072], P('dp', 'mp'), may hold values from -0.1875 to 0.1875
- w_out: bfloat16 [1024, 1024], P('mp', 'dp'), may hold values from -4 to 4
- w_up: bfloat16 [1024, 4096], P('dp', 'mp'), may hold values from -0.1875 to 0.1875
- w_down: bfloat16 [4096, 1024], P('mp', 'dp'), may hold values from -0.09375 to 0.09375
- ln1_gain: bfloat16 [1024], P('dp'), may hold values from 0.5 to 1.5
- ln1_bias: bfloat16 [1024], P('dp'), may hold values from -3 to 3
- ln2_gain: bfloat16 [1024], P('dp'), may hold values from 0.5 to 1.5
- ln2_bias: bfloat16 [1024], P('dp'), may hold values from -3 to 3
- scene_lengths: int32 [8], replicated, may hold values from 1 to 1792, as said below
- grad_out: float32 [2048, 1024], P('dp'), may hold values from -6 to 6
Outputs:
- result: float32 [2048, 1024], P('dp')
- grad_tokens: float32 [2048, 1024], P('dp')
- grad_w_qkv: float32 [1024, 3072], P('dp', 'mp')
- grad_w_out: float32 [1024, 1024], P('mp', 'dp')
- grad_w_up: float32 [1024, 4096], P('dp', 'mp')
- grad_w_down: float32 [4096, 1024], P('mp', 'dp')
- grad_ln1_gain: float32 [1024], P('dp')
- grad_ln1_bias: float32 [1024], P('dp')
- grad_ln2_gain: float32 [1024], P('dp')
- grad_ln2_bias: float32 [1024], P('dp')
The draws below stay inside these ranges and needn't reach their ends.
Inputs may be any that keep to these rules, and one draw needn't show every extreme that they name: `scene_lengths`: the lengths sum to 2048; one scene, at a place drawn from the seed, has exactly 1792 tokens, and the other scenes together hold 256 tokens.
All inputs are finite; a program needn't handle non-finite values.
Results may differ from the reference program's by a relative error of at most 0.017.
Values may be sent and summed in bfloat16 or wider, within the bound.
A program may use at most 128 MiB of HBM per device.

```python
import jax
import jax.numpy as jnp
from jax import lax

D = 1024
HEADS = 16
HEAD_DIM = 64
FF = 4096
TOK_DEV = 256
SCENES = 8
TOKENS = 2048
SCENE_MOST = 1792


def draw_scene_lengths(key, part):
    key = jax.random.fold_in(key, 11)
    key_cuts, key_place = jax.random.split(key)
    shuffled = jax.random.permutation(key_cuts, TOK_DEV - 1).astype(jnp.int32) + 1
    cuts = jnp.sort(shuffled[:SCENES - 2])
    bounds = jnp.concatenate([jnp.zeros((1,), jnp.int32), cuts, jnp.full((1,), TOK_DEV, jnp.int32)])
    shorter = (bounds[1:] - bounds[:-1]).astype(jnp.int32)
    place = jax.random.randint(key_place, (), 0, SCENES).astype(jnp.int32)
    slots = jnp.arange(SCENES, dtype=jnp.int32)
    before = shorter[jnp.clip(slots, 0, SCENES - 2)]
    after = shorter[jnp.clip(slots - 1, 0, SCENES - 2)]
    longest = jnp.full((SCENES,), TOKENS - TOK_DEV, jnp.int32)
    return jnp.where(slots < place, before, jnp.where(slots == place, longest, after)).astype(jnp.int32)


def steps_of(rng, extent, cuts, low, largest):
    factor_of, own = 1.0, jax.random.fold_in(rng, 6)
    for dim, blocks in cuts:
        heights = jnp.exp(jax.random.uniform(jax.random.fold_in(own, dim), (blocks,), jnp.float32, low / len(cuts), largest / len(cuts)))
        factor_of = factor_of * jnp.repeat(heights, extent[dim] // blocks).reshape([-1 if axis == dim else 1 for axis in range(len(extent))])
    return factor_of


def bell_draw(own_key, shape, deviation, reach, cuts=(), kind=jnp.bfloat16):
    level = steps_of(own_key, shape, cuts, -0.22, 0.18) if cuts else 1.0
    values = jax.random.normal(own_key, shape, jnp.float32) * deviation * level
    return jnp.minimum(jnp.maximum(values, -reach), reach).astype(kind)


def setup_inputs(seed: int = 0) -> dict:
    seeds = jax.random.split(jax.random.key(seed), 12)
    tokens = bell_draw(seeds[0], (TOKENS, D), 1.0, 6.0, ((0, 8),), jnp.float32)
    w_qkv = bell_draw(seeds[1], (D, 3 * D), D ** -0.5, 0.1875, ((0, 8), (1, 4)))
    w_out = bell_draw(seeds[2], (D, D), 2 ** -0.5, 4.0, ((0, 4), (1, 8)))
    w_up = bell_draw(seeds[3], (D, FF), D ** -0.5, 0.1875, ((0, 8), (1, 4)))
    w_down = bell_draw(seeds[4], (FF, D), FF ** -0.5, 0.09375, ((0, 4), (1, 8)))
    ln1_gain = jnp.clip(1.0 + 0.1 * jax.random.normal(seeds[5], (D,), jnp.float32), 0.5, 1.5).astype(jnp.bfloat16)
    ln1_bias = bell_draw(seeds[6], (D,), 0.5, 3.0, ((0, 8),))
    ln2_gain = jnp.clip(1.0 + 0.1 * jax.random.normal(seeds[7], (D,), jnp.float32), 0.5, 1.5).astype(jnp.bfloat16)
    ln2_bias = bell_draw(seeds[8], (D,), 0.5, 3.0, ((0, 8),))
    scene_lengths = draw_scene_lengths(jax.random.fold_in(seeds[11], 71), 0)
    grad_out = bell_draw(seeds[10], (TOKENS, D), 1.0, 6.0, ((0, 8),), jnp.float32)
    return dict(tokens=tokens, w_qkv=w_qkv, w_out=w_out, w_up=w_up, w_down=w_down, ln1_gain=ln1_gain, ln1_bias=ln1_bias, ln2_gain=ln2_gain, ln2_bias=ln2_bias, scene_lengths=scene_lengths, grad_out=grad_out)


@jax.custom_vjp
def low(v):
    return lax.optimization_barrier(v.astype(jnp.bfloat16)).astype(jnp.float32)

@jax.custom_vjp
def low_back(v):
    return v

def low_keep(v):
    return (low(v), None)

def low_pass(kept, grad):
    return (grad,)

def back_keep(v):
    return (v, None)

def back_low(kept, grad):
    return (low(grad),)
low.defvjp(low_keep, low_pass)
low_back.defvjp(back_keep, back_low)
highest = lax.Precision.HIGHEST

def layer_norm(values, gain, bias):
    center = values - lax.optimization_barrier(jnp.mean(values, axis=-1, keepdims=True))
    inverse = lax.rsqrt(lax.optimization_barrier(jnp.mean(center * center, axis=-1, keepdims=True)) + 1e-05)
    return center * inverse * gain + bias

def scene_index(positions, scene_ends):
    return lax.optimization_barrier(jnp.sum((positions[:, None] >= scene_ends[None, :]).astype(jnp.int32), axis=1))

def reference(tokens, w_qkv, w_out, w_up, w_down, ln1_gain, ln1_bias, ln2_gain, ln2_bias, scene_lengths, grad_out):
    block_rows = min(512, TOKENS)
    window = min(TOKENS, block_rows + 2 * SCENE_MOST)
    scene_ends = jnp.cumsum(scene_lengths).astype(jnp.int32)
    scene_ids = scene_index(jnp.arange(TOKENS, dtype=jnp.int32), scene_ends)
    score_scale = HEAD_DIM ** (-0.5)

    def attention(query, keys, values):

        def one_block(block_index):
            first = (block_index * block_rows).astype(jnp.int32)
            start = jnp.clip(first - SCENE_MOST, 0, TOKENS - window).astype(jnp.int32)
            query_block = lax.dynamic_slice_in_dim(query, first, block_rows, 0)
            key_window = lax.dynamic_slice_in_dim(keys, start, window, 0)
            value_window = lax.dynamic_slice_in_dim(values, start, window, 0)
            query_scene = lax.dynamic_slice_in_dim(scene_ids, first, block_rows, 0)
            key_scene = lax.dynamic_slice_in_dim(scene_ids, start, window, 0)
            scores = low_back(jnp.einsum('qhd,khd->hqk', query_block, key_window, precision=highest) * score_scale)
            same = query_scene[:, None] == key_scene[None, :]
            masked = jnp.where(same[None], scores, -1e+30)
            top = lax.optimization_barrier(jnp.max(masked, axis=-1, keepdims=True))
            expo = jnp.where(same[None], jnp.exp(masked - top), 0.0)
            prob = expo / lax.optimization_barrier(jnp.sum(expo, axis=-1, keepdims=True))
            return jnp.einsum('hqk,khd->qhd', prob, value_window, precision=highest)
        pieces = lax.map(jax.checkpoint(one_block), jnp.arange(TOKENS // block_rows, dtype=jnp.int32))
        return pieces.reshape(TOKENS, HEADS * HEAD_DIM)

    def forward(inputs, weight_qkv, weight_out, weight_up, weight_down, gain_one, bias_one, gain_two, bias_two):
        hidden_one = low(layer_norm(inputs, gain_one, bias_one))
        mixed = low(low_back(jnp.dot(hidden_one, weight_qkv, precision=highest)))
        split = mixed.reshape(TOKENS, HEADS, 3, HEAD_DIM)
        attended = low(low_back(attention(split[:, :, 0], split[:, :, 1], split[:, :, 2])))
        middle = inputs + low_back(jnp.dot(attended, weight_out, precision=highest))
        hidden_two = low(layer_norm(middle, gain_two, bias_two))
        inner = low_back(jnp.dot(hidden_two, weight_up, precision=highest))
        active = low(jax.nn.gelu(inner))
        return middle + low_back(jnp.dot(active, weight_down, precision=highest))
    floats = (tokens, w_qkv.astype(jnp.float32), w_out.astype(jnp.float32), w_up.astype(jnp.float32), w_down.astype(jnp.float32), ln1_gain.astype(jnp.float32), ln1_bias.astype(jnp.float32), ln2_gain.astype(jnp.float32), ln2_bias.astype(jnp.float32))
    result, pull_back = jax.vjp(forward, *floats)
    grads = pull_back(grad_out)
    return (result, grads[0], grads[1], grads[2], grads[3], grads[4], grads[5], grads[6], grads[7], grads[8])
```

```python
import functools

import jax
import jax.numpy as jnp
from jax import lax
from jax.experimental import pallas as pl
from jax.experimental.pallas import tpu as pltpu
from jax.sharding import PartitionSpec as P

HEAD_DIM = 64
LANES = 128
FAR = -1e30
MESH = pl.DeviceIdType.MESH
bf16 = jnp.bfloat16
f32 = jnp.float32


def nn(a, b):
    return lax.dot_general(a, b, (((1,), (0,)), ((), ())), preferred_element_type=f32)


def nt(a, b):
    return lax.dot_general(a, b, (((1,), (1,)), ((), ())), preferred_element_type=f32)


class Plan:
    def __init__(self, tokens, w_qkv, w_up, scenes, dp, mp):
        self.R, self.M = dp, mp
        self.tl, self.D = tokens.shape
        self.rb = self.D // dp
        self.L = dp // 2
        self.H = w_qkv.shape[1] // (3 * HEAD_DIM)
        self.g = dp // self.H
        self.U = w_up.shape[1]
        self.rm = self.tl // mp
        self.HF = self.H * HEAD_DIM
        self.scenes = scenes.shape[0]
        self.NQ = self.H * self.tl
        self.keep = dp * self.tl <= 4096
        widths = (LANES, 3 * self.HF, self.HF, self.U, self.U)
        self.cols = []
        start = 0
        for width in widths:
            self.cols.append((start, width))
            start += width
        self.WC = start
        self.gw = (self.U, self.U, self.HF, LANES, 3 * self.HF, LANES)


def kernel(p, names, *refs):
    r = dict(zip(names, refs))
    R, M, L, H, g = p.R, p.M, p.L, p.H, p.g
    tl, D, rb, rm, U, HF, NQ = p.tl, p.D, p.rb, p.rm, p.U, p.HF, p.NQ
    half = tl // 2
    d = lax.axis_index("dp")
    m = lax.axis_index("mp")
    z, x = d // 2, lax.rem(d, 2)
    dh, di = d // g, lax.rem(d, g)
    sent = []

    def add(a, k, n):
        return lax.rem(a + k, n)

    def copy(src, dst, name, index, peer):
        return pltpu.make_async_remote_copy(
            src_ref=src,
            dst_ref=dst,
            send_sem=r[name + "_s"].at[index],
            recv_sem=r[name + "_r"].at[index],
            device_id=peer,
            device_id_type=MESH,
        )

    def send(src, dst, name, index, peer):
        one = copy(src, dst, name, index, peer)
        one.start()
        sent.append(one)

    def arrive(dst, name, index, peer):
        copy(dst, dst, name, index, peer).wait_recv()

    pair = (d + 1 - 2 * x, m)

    def line(k):
        return (add(z, k, L) * 2 + x, m)

    def row_peer(k):
        return (d, add(m, k, M))

    W = r["W"]
    local = [
        pltpu.make_async_copy(r["tokens"], r["tok"], r["loc"].at[0]),
        pltpu.make_async_copy(r["grad_out"], r["go"], r["loc"].at[1]),
        pltpu.make_async_copy(r["wblk"], W.at[d], r["loc"].at[2]),
    ]
    for one in local:
        one.start()

    barrier = pltpu.get_barrier_semaphore()
    for k in range(1, R):
        pl.semaphore_signal(barrier, 1, device_id=(add(d, k, R), m), device_id_type=MESH)
    for k in range(1, M):
        pl.semaphore_signal(barrier, 1, device_id=row_peer(k), device_id_type=MESH)
    pl.semaphore_wait(barrier, R - 1 + M - 1)

    def wcols(b, s):
        c0, width = p.cols[s]
        return W.at[b, :, pl.ds(c0, width)]

    def weights_start(s):
        for k in range(1, L):
            send(wcols(d, s), wcols(d, s), "wz", (s, k - 1), line(k))
        send(wcols(d, s), wcols(d, s), "wx", (s, 0), pair)

    def weights_relay(s):
        for k in range(1, L):
            b = add(z, L - k, L) * 2 + x
            arrive(wcols(b, s), "wz", (s, k - 1), line(L - k))
            send(wcols(b, s), wcols(b, s), "wx", (s, k), pair)

    def weights_end(s):
        for k in range(L):
            b = add(z, L - k, L) * 2 + 1 - x
            arrive(wcols(b, s), "wx", (s, k), pair)

    def weight(s, first=0, width=None):
        c0, full = p.cols[s]
        width = full if width is None else width
        return W[:, :, pl.ds(c0 + first, width)].reshape(D, width)

    local[2].wait()
    for s in range(5):
        weights_start(s)
    local[0].wait()
    local[1].wait()

    def transposed(src_ref, dst_ref, rows, chunk):
        for c in range(rows // chunk):
            part = src_ref[pl.ds(c * chunk, chunk), :].astype(f32)
            dst_ref[:, :, :, pl.ds(c * chunk, chunk)] = (
                part.T.astype(bf16).reshape(L, 2, rb, chunk)
            )

    outlow = r["outlow"]
    outlow[...] = r["go"][...].astype(bf16)

    weights_relay(0)
    weights_end(0)
    lnp = r["lnp"]
    lnp[...] = weight(0).astype(f32).T[0:8, :]
    gain1, bias1, gain2, bias2 = (lnp[pl.ds(k, 1), :] for k in range(4))

    def norm(values):
        center = values - jnp.mean(values, axis=-1, keepdims=True)
        inverse = lax.rsqrt(jnp.mean(center * center, axis=-1, keepdims=True) + 1e-05)
        return center * inverse, inverse

    def norm_back(upstream, normed, inverse, gain):
        scaled = upstream * gain
        return inverse * (
            scaled
            - jnp.mean(scaled, axis=-1, keepdims=True)
            - normed * jnp.mean(scaled * normed, axis=-1, keepdims=True)
        )

    h1 = r["h1"]

    @pl.loop(0, tl // 32)
    def _(c):
        rows = pl.ds(pl.multiple_of(c * 32, 32), 32)
        n1, _ = norm(r["tok"][rows, :])
        h1[rows, :] = (n1 * gain1 + bias1).astype(bf16)

    weights_relay(1)
    weights_end(1)

    lane = lax.broadcasted_iota(jnp.int32, (1, LANES), 1)
    low = lane < HEAD_DIM

    def swap(v):
        return pltpu.roll(v, HEAD_DIM, 1)

    qs, kvs, qin, KV = r["qs"], r["kvs"], r["qin"], r["KV"]
    for t in range(H // 2):
        mixed = nn(h1[...], weight(1, 6 * HEAD_DIM * t, 6 * HEAD_DIM))
        t0, t1, t2 = (mixed[:, k * LANES : (k + 1) * LANES] for k in range(3))
        q_even, q_odd = t0 * 0.125, swap(t1) * 0.125
        for h, q in ((2 * t, q_even), (2 * t + 1, q_odd)):
            qs[h] = jnp.where(low, q[:half], swap(q[half:])).astype(bf16)
        kvs[2 * t] = jnp.where(low, swap(t0), swap(t1)).astype(bf16)
        kvs[2 * t + 1] = t2.astype(bf16)

    def head_dev(h, member):
        return (h * g + member, m)

    for k in range(1, H):
        h = add(dh, k, H)
        peer = head_dev(h, di)
        send(kvs.at[h], KV.at[d], "kv", k, peer)
        send(qs.at[h], qin.at[dh], "q", k, peer)
    KV[d] = kvs[dh]
    qin[dh] = qs[dh]
    for k in range(H):
        j = add(dh, H - k, H)
        own = j * g + di
        if k:
            arrive(KV.at[own], "kv", k, head_dev(j, di))
        for q in range(1, g):
            send(KV.at[own], KV.at[own], "kvx", (k, q - 1), head_dev(dh, add(di, q, g)))
    for k in range(1, H):
        j = add(dh, H - k, H)
        arrive(qin.at[j], "q", k, head_dev(j, di))
    for k in range(H):
        j = add(dh, H - k, H)
        for q in range(1, g):
            member = add(di, g - q, g)
            arrive(KV.at[j * g + member], "kvx", (k, q - 1), head_dev(dh, member))

    qall, KVT = r["qall"], r["KVT"]
    for j in range(H):
        packed = qin[j].astype(f32)
        qall[pl.ds(j * tl, half), :] = jnp.where(low, packed, 0.0).astype(bf16)
        qall[pl.ds(j * tl + half, half), :] = jnp.where(low, swap(packed), 0.0).astype(bf16)

    ends = []
    total = 0
    for k in range(p.scenes):
        total = total + r["scene"][k]
        ends.append(total)

    def scene_of(pos):
        count = jnp.zeros(pos.shape, jnp.int32)
        for end in ends:
            count = count + (pos >= end).astype(jnp.int32)
        return count

    token_lane = lax.broadcasted_iota(jnp.int32, (1, tl), 1)
    q_scene = jnp.concatenate(
        [scene_of((j * g + di) * tl + token_lane) for j in range(H)], axis=1
    )
    token_row = lax.broadcasted_iota(jnp.int32, (tl, 1), 0)

    def masked_scores(o):
        scores = nt(KV[o], qall[...])
        return jnp.where(scene_of(o * tl + token_row) == q_scene, scores, FAR)

    unit = (
        lax.broadcasted_iota(jnp.int32, (LANES, LANES), 0)
        == lax.broadcasted_iota(jnp.int32, (LANES, LANES), 1)
    ).astype(bf16)

    top8, sum8, acc = r["top8"], r["sum8"], r["acc"]
    top8[...] = jnp.full((8, NQ), FAR, f32)
    sum8[...] = jnp.zeros((8, NQ), f32)
    acc[...] = jnp.zeros((LANES, NQ), f32)

    @pl.loop(0, R)
    def _(o):
        KVT[o] = nt(unit, KV[o]).astype(bf16)
        top8[...] = jnp.maximum(
            top8[...], jnp.max(masked_scores(o).reshape(tl // 8, 8, NQ), axis=0)
        )

    top = r["top"]
    top[...] = jnp.max(top8[...], axis=0, keepdims=True)

    @pl.loop(0, R)
    def _(o):
        expo = jnp.exp(masked_scores(o) - top[...])
        sum8[...] += jnp.sum(expo.reshape(tl // 8, 8, NQ), axis=0)
        low_expo = expo.astype(bf16)
        if p.keep:
            r["prob"][o] = low_expo
        acc[...] += nn(KVT[o], low_expo)

    scale_row = 1.0 / jnp.sum(sum8[...], axis=0, keepdims=True)
    inv = r["inv"]
    inv[...] = scale_row
    attf, atts, attT = r["attf"], r["atts"], r["attT"]
    attf[...] = acc[pl.ds(HEAD_DIM, HEAD_DIM), :] * scale_row
    for j in range(H):
        atts[j] = attf[:, pl.ds(j * tl, tl)].astype(bf16)
    for k in range(1, H):
        j = add(dh, k, H)
        send(atts.at[j], attT.at[dh], "att", k, head_dev(j, di))
    attT[dh] = atts[dh]
    for k in range(1, H):
        h = add(dh, H - k, H)
        arrive(attT.at[h], "att", k, head_dev(h, di))
    att = r["att"]
    att[...] = attT[...].reshape(HF, tl).astype(f32).T.astype(bf16)

    rs_send, rs_recv = r["rs_send"], r["rs_recv"]

    def rows_send(n, values):
        rs_send[n] = values.astype(bf16).reshape(M, rm, D)
        for k in range(1, M):
            send(rs_send.at[n, add(m, k, M)], rs_recv.at[n, k - 1], "rs", (n, k - 1), row_peer(k))

    def rows_sum(n):
        value = rs_send[n, m].astype(f32)
        for k in range(1, M):
            arrive(rs_recv.at[n, k - 1], "rs", (n, k - 1), row_peer(M - k))
            value = value + rs_recv[n, k - 1].astype(f32)
        return value

    def gather_send(n, ref):
        for k in range(1, M):
            send(ref.at[m], ref.at[m], "ag", (n, k - 1), row_peer(k))

    def gather_end(n, ref):
        for k in range(1, M):
            b = add(m, M - k, M)
            arrive(ref.at[b], "ag", (n, k - 1), row_peer(M - k))

    weights_relay(2)
    weights_end(2)
    rows_send(0, nt(att[...], weight(2)))
    transposed(r["go"], r["outT"], tl, LANES)
    transposed(h1, r["h1T"], tl, LANES)

    own_rows = pl.ds(pl.multiple_of(m * rm, rm), rm)
    mid, n2, r2, h2 = r["mid"], r["n2"], r["r2"], r["h2"]
    middle = r["tok"][own_rows, :] + rows_sum(0)
    mid[...] = middle
    normed, inverse = norm(middle)
    n2[...] = normed
    r2[...] = jnp.broadcast_to(inverse, (rm, LANES))
    h2[m] = (normed * gain2 + bias2).astype(bf16)
    gather_send(0, h2)
    weights_relay(3)
    weights_relay(4)
    weights_end(3)
    weights_end(4)
    gather_end(0, h2)

    active, il = r["active"], r["il"]
    c_one, c_two = 0.7978845608028654, 0.044715
    step = 256
    for c in range(U // step):
        inner = nn(h2[...].reshape(tl, D), weight(3, c * step, step))
        dact = nn(outlow[...], weight(4, c * step, step))
        square = inner * inner
        t = jnp.tanh(c_one * inner * (1.0 + c_two * square))
        cdf = 0.5 * (1.0 + t)
        active[:, pl.ds(c * step, step)] = (inner * cdf).astype(bf16)
        slope = cdf + 0.5 * inner * (1.0 - t * t) * (c_one + 3.0 * c_one * c_two * square)
        il[:, pl.ds(c * step, step)] = (dact * slope).astype(bf16)

    rows_send(1, nt(il[...], weight(3)))
    rows_send(2, nt(active[...], weight(4)))

    def grad_x(s, others):
        value = others()
        width = p.gw[s]
        r["gxs%d" % s][...] = value.astype(bf16).reshape(L, rb, width)
        for k in range(L):
            l = add(z, k, L)
            send(r["gxs%d" % s].at[l], r["gxr%d" % s].at[l], "gx", (s, k), pair)

    def grad_z(s, mine, out):
        for k in [*range(1, L), 0]:
            l = add(z, k, L)
            arrive(r["gxr%d" % s].at[l], "gx", (s, k), pair)
            value = mine(l) + r["gxr%d" % s][l].astype(f32)
            if k:
                r["gzs%d" % s][k - 1] = value.astype(bf16)
                send(r["gzs%d" % s].at[k - 1], r["gzr%d" % s].at[k - 1], "gz", (s, k - 1), line(k))
            else:
                out[...] = value

    def grad_end(s, out):
        for k in range(1, L):
            arrive(r["gzr%d" % s].at[k - 1], "gz", (s, k - 1), line(L - k))
            out[...] += r["gzr%d" % s][k - 1].astype(f32)

    def others(lhs, rhs):
        return lambda: nn(lhs[:, 1 - x].reshape(L * rb, tl), rhs[...])

    def mine(lhs, rhs):
        return lambda l: nn(lhs[l, x], rhs[...])

    outT, h1T, h2T, midT = r["outT"], r["h1T"], r["h2T"], r["midT"]
    for k in range(M // 2):
        part = h2[pl.ds(2 * k, 2)].reshape(2 * rm, D).astype(f32)
        h2T[:, :, :, pl.ds(2 * k * rm, 2 * rm)] = part.T.astype(bf16).reshape(L, 2, rb, 2 * rm)

    grad_x(0, others(outT, active))
    grad_x(1, others(h2T, il))

    back2 = rows_sum(1)
    gm, ml = r["gm"], r["ml"]
    grad_middle = r["go"][own_rows, :] + norm_back(back2, n2[...], r2[:, 0:1], gain2)
    gm[...] = grad_middle
    ml[m] = grad_middle.astype(bf16)
    gather_send(1, ml)

    col = lax.broadcasted_iota(jnp.int32, (rm, LANES), 1)

    def norm_columns(upstream, normed, c):
        gain_part = (upstream * normed).T.astype(bf16)
        bias_part = upstream.T.astype(bf16)
        value = nn(gain_part, (col == c).astype(bf16)) + nn(bias_part, (col == c + 1).astype(bf16))
        return value.reshape(L, 2, rb, LANES)

    ln2c, ln1c = r["ln2c"], r["ln1c"]
    ln2c[...] = norm_columns(back2, n2[...], 0)

    gather_end(1, ml)
    midlow = ml[...].reshape(tl, D)

    gs, gin, gall = r["gs"], r["gin"], r["gall"]
    gatt = nn(midlow, weight(2))
    for h in range(H):
        tile = gatt[:, (h // 2) * LANES : (h // 2 + 1) * LANES]
        even = h % 2 == 0
        first = tile[:half] if even else swap(tile[:half])
        second = swap(tile[half:]) if even else tile[half:]
        gs[h] = jnp.where(low, first, second).astype(bf16)
    for k in range(1, H):
        h = add(dh, k, H)
        send(gs.at[h], gin.at[dh], "ga", k, head_dev(h, di))
    gin[dh] = gs[dh]

    for k in range(M // 2):
        part = ml[pl.ds(2 * k, 2)].reshape(2 * rm, D).astype(f32)
        midT[:, :, :, pl.ds(2 * k * rm, 2 * rm)] = part.T.astype(bf16).reshape(L, 2, rb, 2 * rm)
    grad_x(2, others(midT, att))
    grad_x(3, lambda: ln2c[:, 1 - x].reshape(L * rb, LANES))
    for k in range(1, H):
        j = add(dh, H - k, H)
        arrive(gin.at[j], "ga", k, head_dev(j, di))

    inv_col = jnp.broadcast_to(inv[...], (LANES, NQ)).T
    shift_parts = []
    for j in range(H):
        packed = gin[j].astype(f32)
        top_half = jnp.where(low, 0.0, swap(packed))
        bottom = jnp.where(low, 0.0, packed)
        ga = jnp.concatenate([top_half, bottom], axis=0)
        gaT = ga.T[HEAD_DIM:, :]
        shift_parts.append(
            jnp.sum(gaT * attf[:, pl.ds(j * tl, tl)], axis=0, keepdims=True)
            * inv[:, pl.ds(j * tl, tl)]
        )
        gall[pl.ds(j * tl, tl), :] = (ga * inv_col[j * tl : (j + 1) * tl]).astype(bf16)
    shift = r["shift"]
    shift[...] = jnp.concatenate(shift_parts, axis=1)

    acc[...] = jnp.zeros((LANES, NQ), f32)
    dkvs, dkv_in = r["dkvs"], r["dkv_in"]

    for k in [*range(1, R), 0]:
        o = add(d, k, R)
        prob = r["prob"][o] if p.keep else jnp.exp(masked_scores(o) - top[...]).astype(bf16)
        dprob = nt(KV[o], gall[...])
        dscore = (prob.astype(f32) * (dprob - shift[...])).astype(bf16)
        acc[...] += nn(KVT[o], dscore)
        dkv = nn(dscore, qall[...]) + nn(prob, gall[...])
        if k:
            dkvs[k] = dkv.astype(bf16)
            send(dkvs.at[k], dkv_in.at[d], "dkv", k, (o, m))
        else:
            dkv_in[d] = dkv.astype(bf16)

    dqs, dqT = r["dqs"], r["dqT"]
    for j in range(H):
        dqs[j] = (acc[pl.ds(0, HEAD_DIM), pl.ds(j * tl, tl)] * 0.125).astype(bf16)
    for k in range(1, H):
        j = add(dh, k, H)
        send(dqs.at[j], dqT.at[dh], "dq", k, head_dev(j, di))
    dqT[dh] = dqs[dh]

    res = r["res"]
    res[m] = (mid[...] + rows_sum(2)).astype(bf16)
    gather_send(2, res)

    grad_z(0, mine(outT, active), r["o_down"])
    grad_z(1, mine(h2T, il), r["o_up"])
    grad_z(2, mine(midT, att), r["o_out"])
    lnsum = r["lnsum"]
    grad_z(3, lambda l: ln2c[l, x], lnsum.at[0])

    for k in range(1, H):
        h = add(dh, H - k, H)
        arrive(dqT.at[h], "dq", k, head_dev(h, di))
    for k in range(1, R):
        o = add(d, R - k, R)
        arrive(dkv_in.at[o], "dkv", k, (o, m))

    gmix = r["gmix"]
    dq = dqT[...].reshape(HF, tl).astype(f32).T

    def head_sum(h):
        value = dkv_in[h * g].astype(f32)
        for q in range(1, g):
            value = value + dkv_in[h * g + q].astype(f32)
        return value

    for t in range(H // 2):
        both = dq[:, t * LANES : (t + 1) * LANES]
        even = swap(head_sum(2 * t))
        base = 6 * HEAD_DIM * t
        gmix[:, pl.ds(base, LANES)] = jnp.where(low, both, even).astype(bf16)
        gmix[:, pl.ds(base + LANES, LANES)] = jnp.where(low, even, both).astype(bf16)
        gmix[:, pl.ds(base + 2 * LANES, LANES)] = head_sum(2 * t + 1).astype(bf16)

    grad_x(4, others(h1T, gmix))
    rows_send(3, nt(gmix[...], weight(1)))

    back1 = rows_sum(3)
    n1, r1 = norm(r["tok"][own_rows, :])
    gt = r["gt"]
    gt[m] = (gm[...] + norm_back(back1, n1, r1, gain1)).astype(bf16)
    gather_send(3, gt)
    ln1c[...] = norm_columns(back1, n1, 2)
    grad_x(5, lambda: ln1c[:, 1 - x].reshape(L * rb, LANES))
    grad_z(5, lambda l: ln1c[l, x], lnsum.at[1])
    grad_z(4, mine(h1T, gmix), r["o_qkv"])

    grad_end(3, lnsum.at[0])
    grad_end(5, lnsum.at[1])
    lnx = r["lnx"]
    both = lnsum[0] + lnsum[1]
    if rb < LANES:
        both = jnp.concatenate([both, jnp.zeros((LANES - rb, LANES), f32)], axis=0)
    lnx[m] = both.T[0:8, :]
    for k in range(1, M):
        send(lnx.at[m], lnx.at[m], "ln", k - 1, row_peer(k))

    gather_end(2, res)
    r["o_result"][...] = res[...].reshape(tl, D).astype(f32)
    grad_end(0, r["o_down"])
    grad_end(1, r["o_up"])
    grad_end(2, r["o_out"])
    gather_end(3, gt)
    r["o_tokens"][...] = gt[...].reshape(tl, D).astype(f32)
    for k in range(1, M):
        arrive(lnx.at[add(m, M - k, M)], "ln", k - 1, row_peer(M - k))
    value = lnx[0]
    for k in range(1, M):
        value = value + lnx[k]
    r["o_ln"][...] = value
    grad_end(4, r["o_qkv"])
    for one in sent:
        one.wait_send()


def layer(p, tokens, grad_out, wblk, scene):
    R, M, L, H, g = p.R, p.M, p.L, p.H, p.g
    tl, D, rb, rm, U, HF, NQ = p.tl, p.D, p.rb, p.rm, p.U, p.HF, p.NQ
    half = tl // 2
    ins = {"tokens": tokens, "grad_out": grad_out, "wblk": wblk, "scene": scene}
    outs = {
        "o_result": (tl, D),
        "o_tokens": (tl, D),
        "o_qkv": (rb, 3 * HF),
        "o_out": (rb, HF),
        "o_up": (rb, U),
        "o_down": (rb, U),
        "o_ln": (8, max(rb, LANES)),
    }
    v = pltpu.VMEM
    scratch = {
        "W": v((R, rb, p.WC), bf16),
        "tok": v((tl, D), f32),
        "go": v((tl, D), f32),
        "outlow": v((tl, D), bf16),
        "lnp": v((8, D), f32),
        "h1": v((tl, D), bf16),
        "qs": v((H, half, LANES), bf16),
        "kvs": v((H, tl, LANES), bf16),
        "qin": v((H, half, LANES), bf16),
        "KV": v((R, tl, LANES), bf16),
        "KVT": v((R, LANES, tl), bf16),
        "qall": v((NQ, LANES), bf16),
        "top8": v((8, NQ), f32),
        "sum8": v((8, NQ), f32),
        "top": v((1, NQ), f32),
        "inv": v((1, NQ), f32),
        "shift": v((1, NQ), f32),
        "acc": v((LANES, NQ), f32),
        "attf": v((HEAD_DIM, NQ), f32),
        "atts": v((H, HEAD_DIM, tl), bf16),
        "attT": v((H, HEAD_DIM, tl), bf16),
        "att": v((tl, HF), bf16),
        "rs_send": v((4, M, rm, D), bf16),
        "rs_recv": v((4, M - 1, rm, D), bf16),
        "mid": v((rm, D), f32),
        "n2": v((rm, D), f32),
        "r2": v((rm, LANES), f32),
        "h2": v((M, rm, D), bf16),
        "active": v((tl, U), bf16),
        "il": v((tl, U), bf16),
        "outT": v((L, 2, rb, tl), bf16),
        "h1T": v((L, 2, rb, tl), bf16),
        "h2T": v((L, 2, rb, tl), bf16),
        "midT": v((L, 2, rb, tl), bf16),
        "gm": v((rm, D), f32),
        "ml": v((M, rm, D), bf16),
        "ln2c": v((L, 2, rb, LANES), f32),
        "ln1c": v((L, 2, rb, LANES), f32),
        "lnsum": v((2, rb, LANES), f32),
        "lnx": v((M, 8, max(rb, LANES)), f32),
        "gs": v((H, half, LANES), bf16),
        "gin": v((H, half, LANES), bf16),
        "gall": v((NQ, LANES), bf16),
        "dkvs": v((R, tl, LANES), bf16),
        "dkv_in": v((R, tl, LANES), bf16),
        "dqs": v((H, HEAD_DIM, tl), bf16),
        "dqT": v((H, HEAD_DIM, tl), bf16),
        "gmix": v((tl, 3 * HF), bf16),
        "res": v((M, rm, D), bf16),
        "gt": v((M, rm, D), bf16),
    }
    if p.keep:
        scratch["prob"] = v((R, tl, NQ), bf16)
    for s, width in enumerate(p.gw):
        scratch["gxs%d" % s] = v((L, rb, width), bf16)
        scratch["gxr%d" % s] = v((L, rb, width), bf16)
        scratch["gzs%d" % s] = v((L - 1, rb, width), bf16)
        scratch["gzr%d" % s] = v((L - 1, rb, width), bf16)
    sems = {
        "wz": (5, L - 1),
        "wx": (5, L),
        "kv": (H,),
        "q": (H,),
        "kvx": (H, max(g - 1, 1)),
        "att": (H,),
        "rs": (4, M - 1),
        "ag": (4, M - 1),
        "gx": (6, L),
        "gz": (6, L - 1),
        "ga": (H,),
        "dkv": (R,),
        "dq": (H,),
        "ln": (M - 1,),
    }
    for name, shape in sems.items():
        scratch[name + "_s"] = pltpu.SemaphoreType.DMA(shape)
        scratch[name + "_r"] = pltpu.SemaphoreType.DMA(shape)
    scratch["loc"] = pltpu.SemaphoreType.DMA((3,))
    names = (*ins, *outs, *scratch)
    any_spec = pl.BlockSpec(memory_space=pl.ANY)
    flops = 6 * tl * D * p.WC + 14 * NQ * R * tl * HEAD_DIM
    return pl.pallas_call(
        functools.partial(kernel, p, names),
        out_shape=[jax.ShapeDtypeStruct(shape, f32) for shape in outs.values()],
        in_specs=[any_spec, any_spec, any_spec, pl.BlockSpec(memory_space=pltpu.SMEM)],
        out_specs=[pl.BlockSpec(memory_space=pltpu.VMEM)] * len(outs),
        scratch_shapes=list(scratch.values()),
        compiler_params=pltpu.CompilerParams(
            collective_id=0, has_side_effects=True, vmem_limit_bytes=60 << 20
        ),
        cost_estimate=pl.CostEstimate(flops=flops, bytes_accessed=8 << 20, transcendentals=NQ * R * tl),
        name="layer",
    )(*ins.values())


def on_device(
    tokens,
    w_qkv,
    w_out,
    w_up,
    w_down,
    ln1_gain,
    ln1_bias,
    ln2_gain,
    ln2_bias,
    scene_lengths,
    grad_out,
):
    p = Plan(tokens, w_qkv, w_up, scene_lengths, lax.axis_size("dp"), lax.axis_size("mp"))
    vectors = jnp.stack([ln1_gain, ln1_bias, ln2_gain, ln2_bias], axis=1)
    vectors = jnp.pad(vectors, ((0, 0), (0, LANES - 4)))
    wblk = jnp.concatenate([vectors, w_qkv, w_out.T, w_up, w_down.T], axis=1)
    result, grad_tokens, qkv, out, up, down, ln = layer(p, tokens, grad_out, wblk, scene_lengths)
    rb = p.rb
    return (
        result,
        grad_tokens,
        qkv,
        out.T,
        up,
        down.T,
        ln[2, :rb],
        ln[3, :rb],
        ln[0, :rb],
        ln[1, :rb],
    )


def solution(mesh):
    weights = (P("dp", "mp"), P("mp", "dp"), P("dp", "mp"), P("mp", "dp"))
    rows = P("dp", None)
    vector = P("dp")
    return jax.shard_map(
        on_device,
        mesh=mesh,
        in_specs=(rows, *weights, vector, vector, vector, vector, P(), rows),
        out_specs=(rows, rows, *weights, vector, vector, vector, vector),
        check_vma=False,
    )
```

```python
import functools

import jax
import jax.numpy as jnp
from jax import lax
from jax.experimental import pallas as pl
from jax.experimental.pallas import tpu as pltpu
from jax.sharding import PartitionSpec as P

HEAD_DIM = 64
LANES = 128
FAR = -1e30
MESH = pl.DeviceIdType.MESH
bf16 = jnp.bfloat16
f32 = jnp.float32


def nn(a, b):
    return lax.dot_general(a, b, (((1,), (0,)), ((), ())), preferred_element_type=f32)


def nt(a, b):
    return lax.dot_general(a, b, (((1,), (1,)), ((), ())), preferred_element_type=f32)


def tn(a, b):
    return lax.dot_general(a, b, (((0,), (0,)), ((), ())), preferred_element_type=f32)


class Plan:
    def __init__(self, tokens, w_qkv, w_up, scenes, dp, mp):
        self.R, self.M = dp, mp
        self.tl, self.D = tokens.shape
        self.rb = self.D // dp
        self.L = dp // 2
        self.H = w_qkv.shape[1] // (3 * HEAD_DIM)
        self.g = dp // self.H
        self.U = w_up.shape[1]
        self.rm = self.tl // mp
        self.HF = self.H * HEAD_DIM
        self.scenes = scenes.shape[0]
        self.NQ = self.H * self.tl
        self.keep = dp * self.tl <= 4096
        self.whole_lanes = self.rb % LANES == 0
        widths = (3 * self.HF, self.HF, self.U, self.U)
        self.cols = []
        start = 0
        for width in widths:
            self.cols.append((start, width))
            start += width
        self.WC = start
        far, near = dp // 2, dp - 1 - dp // 2
        self.far = far
        self.streams = []
        for s, width in enumerate(widths):
            half = width // 2
            for first, way in ((0, 1), (half, -1)):
                self.streams.append((s, first, half, way, far))
                self.streams.append((s, first, half, -way, near))


def kernel(p, names, *refs):
    r = dict(zip(names, refs))
    R, M, L, H, g = p.R, p.M, p.L, p.H, p.g
    tl, D, rb, rm, U, HF, NQ = p.tl, p.D, p.rb, p.rm, p.U, p.HF, p.NQ
    half = tl // 2
    d = lax.axis_index("dp")
    m = lax.axis_index("mp")
    z, x = d // 2, lax.rem(d, 2)
    dh, di = d // g, lax.rem(d, g)
    sent = []

    def add(a, k, n):
        return lax.rem(a + k, n)

    def copy(src, dst, name, index, peer):
        return pltpu.make_async_remote_copy(
            src_ref=src,
            dst_ref=dst,
            send_sem=r[name + "_s"].at[index],
            recv_sem=r[name + "_r"].at[index],
            device_id=peer,
            device_id_type=MESH,
        )

    def send(src, dst, name, index, peer):
        one = copy(src, dst, name, index, peer)
        one.start()
        sent.append(one)

    def arrive(dst, name, index, peer):
        copy(dst, dst, name, index, peer).wait_recv()

    pair = (d + 1 - 2 * x, m)

    def line(k):
        return (add(z, k, L) * 2 + x, m)

    def row_peer(k):
        return (d, add(m, k, M))

    pos = z + x * (R - 1 - 2 * z)

    def ring(q):
        q = lax.rem(q + 2 * R, R)
        far = q // L
        return 2 * q * (1 - far) + (2 * (R - 1 - q) + 1) * far

    W = r["W"]

    def wcols(b, c0, width):
        return W.at[b, :, pl.ds(c0, width)]

    local = []
    for n, (src, dst) in enumerate(
        [
            (r["w_qkv"], wcols(d, *p.cols[0])),
            (r["tokens"], r["tok"]),
            (r["w_up"], wcols(d, *p.cols[2])),
            (r["w_out"], r["raw_out"] if p.whole_lanes else wcols(d, *p.cols[1])),
            (r["w_down"], r["raw_down"] if p.whole_lanes else wcols(d, *p.cols[3])),
            (r["grad_out"], r["go"]),
        ]
    ):
        one = pltpu.make_async_copy(src, dst, r["loc"].at[n])
        one.start()
        local.append(one)

    barrier = pltpu.get_barrier_semaphore()
    greeted = [(ring(pos + 1), m), (ring(pos - 1), m)] + [row_peer(k) for k in range(1, M)]
    for peer in greeted:
        pl.semaphore_signal(barrier, 1, device_id=peer, device_id_type=MESH)

    def norm(values):
        center = values - jnp.mean(values, axis=-1, keepdims=True)
        inverse = lax.rsqrt(jnp.mean(center * center, axis=-1, keepdims=True) + 1e-05)
        return center * inverse, inverse

    local[1].wait()
    h1f = r["h1f"]

    @pl.loop(0, tl // 32)
    def _(c):
        rows = pl.ds(pl.multiple_of(c * 32, 32), 32)
        h1f[rows, :] = norm(r["tok"][rows, :])[0]

    local[0].wait()
    pl.semaphore_wait(barrier, len(greeted))

    class Queue:
        def __init__(self):
            self.steps = []

        def add(self, streams, start):
            for stream in streams:
                self.steps += [(start + t, run) for t, run in enumerate(stream)]
            self.steps.sort(key=lambda one: one[0])

        def run(self, place):
            while self.steps and self.steps[0][0] <= place:
                self.steps.pop(0)[1]()

    def gather_steps(block, name, index, way, hops):
        onward, before = (ring(pos + way), m), (ring(pos - way), m)

        def step(t):
            def run():
                here = block(ring(pos - way * t))
                if t:
                    arrive(here, name, (*index, t - 1), before)
                if t < hops:
                    send(here, here, name, (*index, t), onward)

            return run

        return [step(t) for t in range(hops + 1)]

    def gather_streams(segment):
        return [
            gather_steps(
                lambda b, s=s, first=first, width=width: wcols(b, p.cols[s][0] + first, width),
                "wg",
                (n,),
                way,
                hops,
            )
            for n, (s, first, width, way, hops) in enumerate(p.streams)
            if s == segment
        ]

    def weight(s, first=0, width=None):
        c0, full = p.cols[s]
        width = full if width is None else width
        return W[:, :, pl.ds(c0 + first, width)].reshape(D, width)

    gathers = Queue()
    lnp = r["lnp"]
    if p.whole_lanes:
        lnall = r["lnall"]
        lnall[d] = r["ln_in"][...]
        for k, (way, hops) in enumerate(((1, p.far), (-1, R - 1 - p.far))):
            gathers.add([gather_steps(lambda b: lnall.at[b], "lg", (k,), way, hops)], 0)
    else:
        lnp[...] = r["ln_in"][...].astype(f32)[0:8, :]
    gathers.add(gather_streams(0), 0)
    gathers.run(0)

    for n in range(2, 6):
        local[n].wait()
    if p.whole_lanes:
        for raw, (c0, width) in ((r["raw_out"], p.cols[1]), (r["raw_down"], p.cols[3])):
            W[d, :, pl.ds(c0, width)] = raw[...].astype(f32).T.astype(bf16)

    outlow = r["outlow"]
    outlow[...] = r["go"][...].astype(bf16)

    gathers.run(R)
    if p.whole_lanes:
        for b in range(R):
            lnp[:, pl.ds(b * rb, rb)] = lnall[b].astype(f32)[0:8, :]
    gain1, bias1, gain2, bias2 = (lnp[pl.ds(k, 1), :] for k in range(4))

    def norm_back(upstream, normed, inverse, gain):
        scaled = upstream * gain
        return inverse * (
            scaled
            - jnp.mean(scaled, axis=-1, keepdims=True)
            - normed * jnp.mean(scaled * normed, axis=-1, keepdims=True)
        )

    h1 = r["h1"]

    h1[...] = (h1f[...] * gain1 + bias1).astype(bf16)
    lane = lax.broadcasted_iota(jnp.int32, (1, LANES), 1)
    low = lane < HEAD_DIM

    def swap(v):
        return pltpu.roll(v, HEAD_DIM, 1)

    qs, kvs, qin, KV = r["qs"], r["kvs"], r["qin"], r["KV"]
    for t in range(H // 2):
        mixed = nn(h1[...], weight(0, 6 * HEAD_DIM * t, 6 * HEAD_DIM))
        t0, t1, t2 = (mixed[:, k * LANES : (k + 1) * LANES] for k in range(3))
        q_even, q_odd = t0 * 0.125, swap(t1) * 0.125
        for h, q in ((2 * t, q_even), (2 * t + 1, q_odd)):
            qs[h] = jnp.where(low, q[:half], swap(q[half:])).astype(bf16)
        kvs[2 * t] = jnp.where(low, swap(t0), swap(t1)).astype(bf16)
        kvs[2 * t + 1] = t2.astype(bf16)

    def head_dev(h, member):
        return (h * g + member, m)

    for k in range(1, H):
        h = add(dh, k, H)
        peer = head_dev(h, di)
        send(kvs.at[h], KV.at[d], "kv", k, peer)
        send(qs.at[h], qin.at[dh], "q", k, peer)
    gathers.add(gather_streams(1), 0)
    gathers.add(gather_streams(2), 0.5)
    gathers.add(gather_streams(3), 3)
    gathers.run(0.5)
    KV[d] = kvs[dh]
    qin[dh] = qs[dh]
    for k in range(H):
        j = add(dh, H - k, H)
        own = j * g + di
        if k:
            arrive(KV.at[own], "kv", k, head_dev(j, di))
        for q in range(1, g):
            send(KV.at[own], KV.at[own], "kvx", (k, q - 1), head_dev(dh, add(di, q, g)))
    for k in range(1, H):
        j = add(dh, H - k, H)
        arrive(qin.at[j], "q", k, head_dev(j, di))
    for k in range(H):
        j = add(dh, H - k, H)
        for q in range(1, g):
            member = add(di, g - q, g)
            arrive(KV.at[j * g + member], "kvx", (k, q - 1), head_dev(dh, member))

    gathers.run(1.5)

    qall, KVT = r["qall"], r["KVT"]
    for j in range(H):
        packed = qin[j].astype(f32)
        qall[pl.ds(j * tl, half), :] = jnp.where(low, packed, 0.0).astype(bf16)
        qall[pl.ds(j * tl + half, half), :] = jnp.where(low, swap(packed), 0.0).astype(bf16)

    ends = []
    total = 0
    for k in range(p.scenes):
        total = total + r["scene"][k]
        ends.append(total)

    def scene_of(pos):
        count = jnp.zeros(pos.shape, jnp.int32)
        for end in ends:
            count = count + (pos >= end).astype(jnp.int32)
        return count

    token_lane = lax.broadcasted_iota(jnp.int32, (1, tl), 1)
    q_scene = jnp.concatenate(
        [scene_of((j * g + di) * tl + token_lane) for j in range(H)], axis=1
    )
    token_row = lax.broadcasted_iota(jnp.int32, (tl, 1), 0)

    def masked_scores(o):
        scores = nt(KV[o], qall[...])
        return jnp.where(scene_of(o * tl + token_row) == q_scene, scores, FAR)

    unit = (
        lax.broadcasted_iota(jnp.int32, (LANES, LANES), 0)
        == lax.broadcasted_iota(jnp.int32, (LANES, LANES), 1)
    ).astype(bf16)

    top8, sum8, acc = r["top8"], r["sum8"], r["acc"]
    top8[...] = jnp.full((8, NQ), FAR, f32)
    sum8[...] = jnp.zeros((8, NQ), f32)
    acc[...] = jnp.zeros((LANES, NQ), f32)

    def maxima(o):
        KVT[o] = nt(unit, KV[o]).astype(bf16)
        top8[...] = jnp.maximum(
            top8[...], jnp.max(masked_scores(o).reshape(tl // 8, 8, NQ), axis=0)
        )

    pl.loop(0, R)(maxima)
    gathers.run(2.5)

    top = r["top"]
    top[...] = jnp.max(top8[...], axis=0, keepdims=True)

    def exponentials(o):
        expo = jnp.exp(masked_scores(o) - top[...])
        sum8[...] += jnp.sum(expo.reshape(tl // 8, 8, NQ), axis=0)
        low_expo = expo.astype(bf16)
        if p.keep:
            r["prob"][o] = low_expo
        acc[...] += nn(KVT[o], low_expo)

    pl.loop(0, R // 2)(exponentials)
    gathers.run(3)
    pl.loop(R // 2, R)(exponentials)

    scale_row = 1.0 / jnp.sum(sum8[...], axis=0, keepdims=True)
    inv = r["inv"]
    inv[...] = scale_row
    attf, atts, attT = r["attf"], r["atts"], r["attT"]
    attf[...] = acc[pl.ds(HEAD_DIM, HEAD_DIM), :] * scale_row
    for j in range(H):
        atts[j] = attf[:, pl.ds(j * tl, tl)].astype(bf16)
    for k in range(1, H):
        j = add(dh, k, H)
        send(atts.at[j], attT.at[dh], "att", k, head_dev(j, di))
    attT[dh] = atts[dh]
    gathers.run(3.5)
    for k in range(1, H):
        h = add(dh, H - k, H)
        arrive(attT.at[h], "att", k, head_dev(h, di))
    att = r["att"]
    att[...] = attT[...].reshape(HF, tl).astype(f32).T.astype(bf16)

    rs_send, rs_recv = r["rs_send"], r["rs_recv"]

    def rows_send(n, values):
        rs_send[n] = values.astype(bf16).reshape(M, rm, D)
        for k in range(1, M):
            send(rs_send.at[n, add(m, k, M)], rs_recv.at[n, k - 1], "rs", (n, k - 1), row_peer(k))

    def rows_sum(n):
        value = rs_send[n, m].astype(f32)
        for k in range(1, M):
            arrive(rs_recv.at[n, k - 1], "rs", (n, k - 1), row_peer(M - k))
            value = value + rs_recv[n, k - 1].astype(f32)
        return value

    def gather_send(n, ref):
        for k in range(1, M):
            send(ref.at[m], ref.at[m], "ag", (n, k - 1), row_peer(k))

    def gather_end(n, ref):
        for k in range(1, M):
            b = add(m, M - k, M)
            arrive(ref.at[b], "ag", (n, k - 1), row_peer(M - k))

    gathers.run(4)
    rows_send(0, nt(att[...], weight(1)))
    gathers.run(4.5)
    own_rows = pl.ds(pl.multiple_of(m * rm, rm), rm)
    mid, n2, r2, h2 = r["mid"], r["n2"], r["r2"], r["h2"]
    middle = r["tok"][own_rows, :] + rows_sum(0)
    mid[...] = middle
    normed, inverse = norm(middle)
    n2[...] = normed
    r2[...] = jnp.broadcast_to(inverse, (rm, LANES))
    h2[m] = (normed * gain2 + bias2).astype(bf16)
    gather_send(0, h2)
    gathers.run(5)
    gather_end(0, h2)

    active, il, slope = r["active"], r["il"], r["slope"]
    c_one, c_two = 0.7978845608028654, 0.044715
    step = 256
    for c in range(U // step):
        inner = nn(h2[...].reshape(tl, D), weight(2, c * step, step))
        square = inner * inner
        t = jnp.tanh(c_one * inner * (1.0 + c_two * square))
        cdf = 0.5 * (1.0 + t)
        active[:, pl.ds(c * step, step)] = (inner * cdf).astype(bf16)
        slope[:, pl.ds(c * step, step)] = cdf + 0.5 * inner * (1.0 - t * t) * (
            c_one + 3.0 * c_one * c_two * square
        )
    sums = Queue()

    def grad_part(s, lhs, rhs):
        c0, width = p.cols[s]
        G = r["G"]
        piece = 256 if width % 256 == 0 else LANES
        for c in range(width // piece):
            value = tn(lhs, rhs[:, pl.ds(c * piece, piece)]).astype(bf16)
            G[:, :, pl.ds(c0 + c * piece, piece)] = value.reshape(R, rb, piece)

    def sum_steps(n, stream, out):
        s, first, width, way, hops = stream
        columns = pl.ds(p.cols[s][0] + first, width)
        G, came = r["G"], r["came%d" % n]
        onward, before = (ring(pos + way), m), (ring(pos - way), m)

        def step(t):
            def run():
                b = ring(pos + way * (hops - t))
                if t:
                    arrive(came.at[t - 1], "gg", (n, t - 1), before)
                if t == hops:
                    rest = G[b, :, columns] if hops < p.far else out[:, pl.ds(first, width)]
                    out[:, pl.ds(first, width)] = rest.astype(f32) + came[t - 1].astype(f32)
                    return
                if t:
                    value = G[b, :, columns].astype(f32) + came[t - 1].astype(f32)
                    G[b, :, columns] = value.astype(bf16)
                send(G.at[b, :, columns], came.at[t], "gg", (n, t), onward)

            return run

        return [step(t) for t in range(hops + 1)]

    def sum_streams(segment, out):
        return [
            sum_steps(n, stream, out) for n, stream in enumerate(p.streams) if stream[0] == segment
        ]

    grad_part(3, outlow[...], active)
    sums.add(sum_streams(3, r["o_down"]), 0)
    sums.run(0)
    gathers.run(R)
    for c in range(U // step):
        dact = nn(outlow[...], weight(3, c * step, step))
        il[:, pl.ds(c * step, step)] = (dact * slope[:, pl.ds(c * step, step)]).astype(bf16)
    rows_send(1, nt(il[...], weight(2)))

    grad_part(2, h2[...].reshape(tl, D), il)
    sums.add(sum_streams(2, r["o_up"]), 1)
    sums.run(1)
    rows_send(2, nt(active[...], weight(3)))
    back2 = rows_sum(1)
    gm, ml = r["gm"], r["ml"]
    grad_middle = r["go"][own_rows, :] + norm_back(back2, n2[...], r2[:, 0:1], gain2)
    gm[...] = grad_middle
    ml[m] = grad_middle.astype(bf16)
    gather_send(1, ml)

    sums.run(2)
    ln2g, ln2b = r["ln2g"], r["ln2b"]
    ln2g[...] = jnp.sum(back2 * n2[...], axis=0, keepdims=True)
    ln2b[...] = jnp.sum(back2, axis=0, keepdims=True)

    gather_end(1, ml)
    midlow = ml[...].reshape(tl, D)

    gs, gin, gall = r["gs"], r["gin"], r["gall"]
    gatt = nn(midlow, weight(1))
    for h in range(H):
        tile = gatt[:, (h // 2) * LANES : (h // 2 + 1) * LANES]
        even = h % 2 == 0
        first = tile[:half] if even else swap(tile[:half])
        second = swap(tile[half:]) if even else tile[half:]
        gs[h] = jnp.where(low, first, second).astype(bf16)
    for k in range(1, H):
        h = add(dh, k, H)
        send(gs.at[h], gin.at[dh], "ga", k, head_dev(h, di))
    gin[dh] = gs[dh]

    grad_part(1, midlow, att)
    sums.add(sum_streams(1, r["o_out"]), 2.5)
    sums.run(2.5)
    for k in range(1, H):
        j = add(dh, H - k, H)
        arrive(gin.at[j], "ga", k, head_dev(j, di))

    inv_col = jnp.broadcast_to(inv[...], (LANES, NQ)).T
    shift_parts = []
    for j in range(H):
        packed = gin[j].astype(f32)
        top_half = jnp.where(low, 0.0, swap(packed))
        bottom = jnp.where(low, 0.0, packed)
        ga = jnp.concatenate([top_half, bottom], axis=0)
        gaT = ga.T[HEAD_DIM:, :]
        shift_parts.append(
            jnp.sum(gaT * attf[:, pl.ds(j * tl, tl)], axis=0, keepdims=True)
            * inv[:, pl.ds(j * tl, tl)]
        )
        gall[pl.ds(j * tl, tl), :] = (ga * inv_col[j * tl : (j + 1) * tl]).astype(bf16)
    shift = r["shift"]
    shift[...] = jnp.concatenate(shift_parts, axis=1)

    acc[...] = jnp.zeros((LANES, NQ), f32)
    dkvs, dkvx, dkv_in = r["dkvs"], r["dkvx"], r["dkv_in"]

    def key_grads(o):
        prob = r["prob"][o] if p.keep else jnp.exp(masked_scores(o) - top[...]).astype(bf16)
        dprob = nt(KV[o], gall[...])
        dscore = (prob.astype(f32) * (dprob - shift[...])).astype(bf16)
        acc[...] += nn(KVT[o], dscore)
        return nn(dscore, qall[...]) + nn(prob, gall[...])

    for q in range(1, g):
        member = add(di, q, g)
        for k in range(H):
            j = add(dh, k, H)
            dkvs[q, k] = key_grads(j * g + member).astype(bf16)
            send(dkvs.at[q, k], dkvx.at[q - 1, k], "dkvx", (q - 1, k), head_dev(dh, member))
        sums.run(2.5 + q)
    for k in [*range(1, H), 0]:
        j = add(dh, k, H)
        dkv = key_grads(j * g + di)
        for q in range(1, g):
            arrive(dkvx.at[q - 1, k], "dkvx", (q - 1, k), head_dev(dh, add(di, g - q, g)))
            dkv = dkv + dkvx[q - 1, k].astype(f32)
        if k:
            dkvs[0, k] = dkv.astype(bf16)
            send(dkvs.at[0, k], dkv_in.at[dh], "dkv", k, head_dev(j, di))
        else:
            dkv_in[dh] = dkv.astype(bf16)

    dqs, dqT = r["dqs"], r["dqT"]
    for j in range(H):
        dqs[j] = (acc[pl.ds(0, HEAD_DIM), pl.ds(j * tl, tl)] * 0.125).astype(bf16)
    for k in range(1, H):
        j = add(dh, k, H)
        send(dqs.at[j], dqT.at[dh], "dq", k, head_dev(j, di))
    dqT[dh] = dqs[dh]
    sums.run(4)

    res = r["res"]
    res[m] = (mid[...] + rows_sum(2)).astype(bf16)
    gather_send(2, res)

    sums.run(5)
    for k in range(1, H):
        h = add(dh, H - k, H)
        arrive(dqT.at[h], "dq", k, head_dev(h, di))
        arrive(dkv_in.at[h], "dkv", k, head_dev(h, di))

    gmix = r["gmix"]
    dq = dqT[...].reshape(HF, tl).astype(f32).T

    def head_sum(h):
        return dkv_in[h].astype(f32)

    for t in range(H // 2):
        both = dq[:, t * LANES : (t + 1) * LANES]
        even = swap(head_sum(2 * t))
        base = 6 * HEAD_DIM * t
        gmix[:, pl.ds(base, LANES)] = jnp.where(low, both, even).astype(bf16)
        gmix[:, pl.ds(base + LANES, LANES)] = jnp.where(low, even, both).astype(bf16)
        gmix[:, pl.ds(base + 2 * LANES, LANES)] = head_sum(2 * t + 1).astype(bf16)

    grad_part(0, h1[...], gmix)
    sums.add(sum_streams(0, r["o_qkv"]), 10)
    sums.run(10)
    rows_send(3, nt(gmix[...], weight(0)))
    sums.run(11)
    back1 = rows_sum(3)
    n1, r1 = norm(r["tok"][own_rows, :])
    gt = r["gt"]
    gt[m] = (gm[...] + norm_back(back1, n1, r1, gain1)).astype(bf16)
    gather_send(3, gt)
    ln_rows = jnp.concatenate(
        [
            jnp.sum(back1 * n1, axis=0, keepdims=True),
            jnp.sum(back1, axis=0, keepdims=True),
            ln2g[...],
            ln2b[...],
            jnp.zeros((4, D), f32),
        ],
        axis=0,
    )
    lnrow, lnr_in = r["lnrow"], r["lnr_in"]
    for b in range(D // LANES):
        lnrow[b] = ln_rows[:, b * LANES : (b + 1) * LANES]

    def lane_block(b):
        return b * rb // LANES

    for k in range(1, R):
        o = add(d, k, R)
        send(lnrow.at[lane_block(o)], lnr_in.at[d], "lr", k - 1, (o, m))
    lnr_in[d] = lnrow[lane_block(d)]
    sums.run(12)
    for k in range(1, R):
        o = add(d, R - k, R)
        arrive(lnr_in.at[o], "lr", k - 1, (o, m))
    value = lnr_in[0]
    for b in range(1, R):
        value = value + lnr_in[b]
    lnx = r["lnx"]
    lnx[m] = value
    for k in range(1, M):
        send(lnx.at[m], lnx.at[m], "ln", k - 1, row_peer(k))
    sums.run(10 + R)

    gather_end(2, res)
    r["o_result"][...] = res[...].reshape(tl, D)
    gather_end(3, gt)
    r["o_tokens"][...] = gt[...].reshape(tl, D)
    for k in range(1, M):
        arrive(lnx.at[add(m, M - k, M)], "ln", k - 1, row_peer(M - k))
    value = lnx[0]
    for k in range(1, M):
        value = value + lnx[k]
    r["o_ln"][...] = value
    for one in sent:
        one.wait_send()


def layer(p, tokens, grad_out, w_qkv, w_out, w_up, w_down, ln_in, scene):
    R, M, L, H, g = p.R, p.M, p.L, p.H, p.g
    tl, D, rb, rm, U, HF, NQ = p.tl, p.D, p.rb, p.rm, p.U, p.HF, p.NQ
    half = tl // 2
    ins = {
        "tokens": tokens,
        "grad_out": grad_out,
        "w_qkv": w_qkv,
        "w_out": w_out,
        "w_up": w_up,
        "w_down": w_down,
        "ln_in": ln_in,
        "scene": scene,
    }
    outs = {
        "o_result": ((tl, D), bf16),
        "o_tokens": ((tl, D), bf16),
        "o_qkv": ((rb, 3 * HF), f32),
        "o_out": ((rb, HF), f32),
        "o_up": ((rb, U), f32),
        "o_down": ((rb, U), f32),
        "o_ln": ((8, LANES), f32),
    }
    v = pltpu.VMEM
    scratch = {
        "W": v((R, rb, p.WC), bf16),
        "tok": v((tl, D), f32),
        "go": v((tl, D), f32),
        "outlow": v((tl, D), bf16),
        "lnp": v((8, D), f32),
        "h1": v((tl, D), bf16),
        "h1f": v((tl, D), f32),
        "slope": v((tl, U), f32),
        "qs": v((H, half, LANES), bf16),
        "kvs": v((H, tl, LANES), bf16),
        "qin": v((H, half, LANES), bf16),
        "KV": v((R, tl, LANES), bf16),
        "KVT": v((R, LANES, tl), bf16),
        "qall": v((NQ, LANES), bf16),
        "top8": v((8, NQ), f32),
        "sum8": v((8, NQ), f32),
        "top": v((1, NQ), f32),
        "inv": v((1, NQ), f32),
        "shift": v((1, NQ), f32),
        "acc": v((LANES, NQ), f32),
        "attf": v((HEAD_DIM, NQ), f32),
        "atts": v((H, HEAD_DIM, tl), bf16),
        "attT": v((H, HEAD_DIM, tl), bf16),
        "att": v((tl, HF), bf16),
        "rs_send": v((4, M, rm, D), bf16),
        "rs_recv": v((4, M - 1, rm, D), bf16),
        "mid": v((rm, D), f32),
        "n2": v((rm, D), f32),
        "r2": v((rm, LANES), f32),
        "h2": v((M, rm, D), bf16),
        "active": v((tl, U), bf16),
        "il": v((tl, U), bf16),
        "gm": v((rm, D), f32),
        "ml": v((M, rm, D), bf16),
        "ln2g": v((1, D), f32),
        "ln2b": v((1, D), f32),
        "lnrow": v((D // LANES, 8, LANES), f32),
        "lnr_in": v((R, 8, LANES), f32),
        "lnx": v((M, 8, LANES), f32),
        "G": v((R, rb, p.WC), bf16),
        "gs": v((H, half, LANES), bf16),
        "gin": v((H, half, LANES), bf16),
        "gall": v((NQ, LANES), bf16),
        "dkvs": v((g, H, tl, LANES), bf16),
        "dkvx": v((max(g - 1, 1), H, tl, LANES), bf16),
        "dkv_in": v((H, tl, LANES), bf16),
        "dqs": v((H, HEAD_DIM, tl), bf16),
        "dqT": v((H, HEAD_DIM, tl), bf16),
        "gmix": v((tl, 3 * HF), bf16),
        "res": v((M, rm, D), bf16),
        "gt": v((M, rm, D), bf16),
    }
    if p.keep:
        scratch["prob"] = v((R, tl, NQ), bf16)
    if p.whole_lanes:
        scratch["raw_out"] = v((HF, rb), bf16)
        scratch["raw_down"] = v((U, rb), bf16)
        scratch["lnall"] = v((R, 16, rb), bf16)
    for n, (_, _, width, _, hops) in enumerate(p.streams):
        scratch["came%d" % n] = v((hops, rb, width), bf16)
    sems = {
        "wg": (len(p.streams), p.far),
        "gg": (len(p.streams), p.far),
        "lg": (2, p.far),
        "lr": (R - 1,),
        "kv": (H,),
        "q": (H,),
        "kvx": (H, max(g - 1, 1)),
        "att": (H,),
        "rs": (4, M - 1),
        "ag": (4, M - 1),
        "ga": (H,),
        "dkv": (H,),
        "dkvx": (max(g - 1, 1), H),
        "dq": (H,),
        "ln": (M - 1,),
    }
    for name, shape in sems.items():
        scratch[name + "_s"] = pltpu.SemaphoreType.DMA(shape)
        scratch[name + "_r"] = pltpu.SemaphoreType.DMA(shape)
    scratch["loc"] = pltpu.SemaphoreType.DMA((6,))
    names = (*ins, *outs, *scratch)
    any_spec = pl.BlockSpec(memory_space=pl.ANY)
    flops = 6 * tl * D * p.WC + 14 * NQ * R * tl * HEAD_DIM
    return pl.pallas_call(
        functools.partial(kernel, p, names),
        out_shape=[jax.ShapeDtypeStruct(*one) for one in outs.values()],
        in_specs=[any_spec] * 6 + [pl.BlockSpec(memory_space=pltpu.VMEM), pl.BlockSpec(memory_space=pltpu.SMEM)],
        out_specs=[pl.BlockSpec(memory_space=pltpu.VMEM)] * len(outs),
        scratch_shapes=list(scratch.values()),
        compiler_params=pltpu.CompilerParams(
            collective_id=0, has_side_effects=True, vmem_limit_bytes=60 << 20
        ),
        cost_estimate=pl.CostEstimate(flops=flops, bytes_accessed=8 << 20, transcendentals=NQ * R * tl),
        name="layer",
    )(*ins.values())


def finish_kernel(*refs):
    hbm, outs, held, sem = refs[:7], refs[7:17], refs[17:24], refs[24]
    copies = [pltpu.make_async_copy(hbm[k], held[k], sem.at[k]) for k in range(7)]
    for one in copies:
        one.start()
    for one in copies:
        one.wait()
    result, tokens, qkv, out, up, down, ln = held
    o_result, o_tokens, o_qkv, o_out, o_up, o_down = outs[:6]
    o_result[...] = result[...].astype(f32)
    o_tokens[...] = tokens[...].astype(f32)
    o_qkv[...] = qkv[...]
    o_out[...] = out[...].T
    o_up[...] = up[...]
    o_down[...] = down[...].T
    for k in range(4):
        outs[6 + k][...] = ln[k, :]


def finish(p, parts):
    tl, D, rb, U, HF = p.tl, p.D, p.rb, p.U, p.HF
    shapes = [(tl, D), (tl, D), (rb, 3 * HF), (HF, rb), (rb, U), (U, rb)] + [(rb,)] * 4
    spec = pl.BlockSpec(memory_space=pltpu.VMEM)
    return pl.pallas_call(
        finish_kernel,
        out_shape=[jax.ShapeDtypeStruct(shape, f32) for shape in shapes],
        in_specs=[pl.BlockSpec(memory_space=pl.ANY)] * 7,
        out_specs=[spec] * 10,
        scratch_shapes=[pltpu.VMEM(one.shape, one.dtype) for one in parts]
        + [pltpu.SemaphoreType.DMA((7,))],
        compiler_params=pltpu.CompilerParams(vmem_limit_bytes=32 << 20),
        cost_estimate=pl.CostEstimate(flops=0, bytes_accessed=6 << 20, transcendentals=0),
        name="finish",
    )(*parts)


def on_device(
    tokens,
    w_qkv,
    w_out,
    w_up,
    w_down,
    ln1_gain,
    ln1_bias,
    ln2_gain,
    ln2_bias,
    scene_lengths,
    grad_out,
):
    p = Plan(tokens, w_qkv, w_up, scene_lengths, lax.axis_size("dp"), lax.axis_size("mp"))
    rb, D = p.rb, p.D
    vectors = jnp.stack([ln1_gain, ln1_bias, ln2_gain, ln2_bias])
    if not p.whole_lanes:
        vectors = lax.all_gather(vectors, "dp", axis=1, tiled=True)
        w_out, w_down = w_out.T, w_down.T
    vectors = jnp.pad(vectors, ((0, 12), (0, 0)))
    parts = layer(p, tokens, grad_out, w_qkv, w_out, w_up, w_down, vectors, scene_lengths)
    if p.whole_lanes:
        return finish(p, parts)
    result, grad_tokens, qkv, out, up, down, ln = parts
    first = lax.axis_index("dp") * rb % LANES
    ln = lax.dynamic_slice_in_dim(ln, first, rb, 1)
    return (
        result.astype(f32),
        grad_tokens.astype(f32),
        qkv,
        out.T,
        up,
        down.T,
        ln[0],
        ln[1],
        ln[2],
        ln[3],
    )


def solution(mesh):
    weights = (P("dp", "mp"), P("mp", "dp"), P("dp", "mp"), P("mp", "dp"))
    rows = P("dp", None)
    vector = P("dp")
    return jax.shard_map(
        on_device,
        mesh=mesh,
        in_specs=(rows, *weights, vector, vector, vector, vector, P(), rows),
        out_specs=(rows, rows, *weights, vector, vector, vector, vector),
        check_vma=False,
    )
```

```python
import functools

import jax
import jax.numpy as jnp
from jax import lax
from jax.experimental import pallas as pl
from jax.experimental.pallas import tpu as pltpu
from jax.sharding import PartitionSpec as P

HEAD_DIM = 64
LANES = 128
FAR = -1e30
MESH = pl.DeviceIdType.MESH
PT = {
    "o0": 3.3,
    "op": 0.7,
    "u0": 3.4,
    "d0": 4.9,
    "g1": 4.1,
    "g2": 3.8,
    "g3": 2.6,
    "g4": [4.6, 5.1],
    "g5": [5.1, 5.6],
    "g6": 5.6,
    "g7": 5.4,
    "g8": 6.6,
    "g9": 6.9,
    "su": 0.5,
    "s1": 0.8,
    "s2": 1.3,
    "s3": 1.8,
    "so": 2.2,
    "sop": 0.86,
    "s4": 2.5,
    "s4b": [1.8],
    "s5": 3.6,
    "s5b": [3.3],
    "s6": 4.3,
    "s7": 4.8,
    "sq": 4.7,
    "sqp": 0.8,
    "up": 1.0,
    "dp": 0.74,
    "sdp": 1.0,
    "sup": 1.2,
    "s8": 5.3,
    "s9": 6.3,
    "s10": 7.3,
}
bf16 = jnp.bfloat16
f32 = jnp.float32


def nn(a, b):
    return lax.dot_general(a, b, (((1,), (0,)), ((), ())), preferred_element_type=f32)


def nt(a, b):
    return lax.dot_general(a, b, (((1,), (1,)), ((), ())), preferred_element_type=f32)


def tn(a, b):
    return lax.dot_general(a, b, (((0,), (0,)), ((), ())), preferred_element_type=f32)


class Plan:
    def __init__(self, tokens, w_qkv, w_up, scenes, dp, mp):
        self.R, self.M = dp, mp
        self.tl, self.D = tokens.shape
        self.rb = self.D // dp
        self.L = dp // 2
        self.H = w_qkv.shape[1] // (3 * HEAD_DIM)
        self.g = dp // self.H
        self.U = w_up.shape[1]
        self.rm = self.tl // mp
        self.HF = self.H * HEAD_DIM
        self.scenes = scenes.shape[0]
        self.NQ = self.H * self.tl
        self.keep = dp * self.tl <= 4096
        self.whole_lanes = self.rb % LANES == 0
        widths = (3 * self.HF, self.HF, self.U, self.U)
        self.cols = []
        start = 0
        for width in widths:
            self.cols.append((start, width))
            start += width
        self.WC = start
        far, near = dp // 2, dp - 1 - dp // 2
        self.far = far
        self.streams = []
        for s, width in enumerate(widths):
            half = width // 2
            for first, way in ((0, 1), (half, -1)):
                self.streams.append((s, first, half, way, far))
                self.streams.append((s, first, half, -way, near))


def kernel(p, names, *refs):
    r = dict(zip(names, refs))
    R, M, L, H, g = p.R, p.M, p.L, p.H, p.g
    tl, D, rb, rm, U, HF, NQ = p.tl, p.D, p.rb, p.rm, p.U, p.HF, p.NQ
    half = tl // 2
    d = lax.axis_index("dp")
    m = lax.axis_index("mp")
    z, x = d // 2, lax.rem(d, 2)
    dh, di = d // g, lax.rem(d, g)
    sent = []

    def add(a, k, n):
        return lax.rem(a + k, n)

    def copy(src, dst, name, index, peer):
        return pltpu.make_async_remote_copy(
            src_ref=src,
            dst_ref=dst,
            send_sem=r[name + "_s"].at[index],
            recv_sem=r[name + "_r"].at[index],
            device_id=peer,
            device_id_type=MESH,
        )

    def send(src, dst, name, index, peer):
        one = copy(src, dst, name, index, peer)
        one.start()
        sent.append(one)

    def arrive(dst, name, index, peer):
        copy(dst, dst, name, index, peer).wait_recv()

    pair = (d + 1 - 2 * x, m)

    def line(k):
        return (add(z, k, L) * 2 + x, m)

    def row_peer(k):
        return (d, add(m, k, M))

    pos = z + x * (R - 1 - 2 * z)

    def ring(q):
        q = lax.rem(q + 2 * R, R)
        far = q // L
        return 2 * q * (1 - far) + (2 * (R - 1 - q) + 1) * far

    W = r["W"]

    def wcols(b, c0, width):
        return W.at[b, :, pl.ds(c0, width)]

    local = []
    for n, (src, dst) in enumerate(
        [
            (r["w_qkv"], wcols(d, *p.cols[0])),
            (r["tokens"], r["tok"]),
            (r["w_up"], wcols(d, *p.cols[2])),
            (r["w_out"], r["raw_out"] if p.whole_lanes else wcols(d, *p.cols[1])),
            (r["w_down"], r["raw_down"] if p.whole_lanes else wcols(d, *p.cols[3])),
            (r["grad_out"], r["go"]),
        ]
    ):
        one = pltpu.make_async_copy(src, dst, r["loc"].at[n])
        one.start()
        local.append(one)

    barrier = pltpu.get_barrier_semaphore()
    greeted = [(ring(pos + 1), m), (ring(pos - 1), m)] + [row_peer(k) for k in range(1, M)]
    for peer in greeted:
        pl.semaphore_signal(barrier, 1, device_id=peer, device_id_type=MESH)

    def norm(values):
        center = values - jnp.mean(values, axis=-1, keepdims=True)
        inverse = lax.rsqrt(jnp.mean(center * center, axis=-1, keepdims=True) + 1e-05)
        return center * inverse, inverse

    local[0].wait()
    pl.semaphore_wait(barrier, len(greeted))

    class Queue:
        def __init__(self):
            self.steps = []

        def add(self, tag, streams, start, pace=1.0):
            for stream in streams:
                self.steps += [(start + pace * t, tag, run) for t, run in enumerate(stream)]
            self.steps.sort(key=lambda one: one[0])

        def run(self, place):
            while self.steps and self.steps[0][0] <= place:
                self.steps.pop(0)[2]()

        def need(self, tag):
            while any(one[1] == tag for one in self.steps):
                self.steps.pop(0)[2]()

    def gather_steps(block, name, index, way, hops):
        onward, before = (ring(pos + way), m), (ring(pos - way), m)

        def step(t):
            def run():
                here = block(ring(pos - way * t))
                if t:
                    arrive(here, name, (*index, t - 1), before)
                if t < hops:
                    send(here, here, name, (*index, t), onward)

            return run

        return [step(t) for t in range(hops + 1)]

    def gather_streams(segment):
        return [
            gather_steps(
                lambda b, s=s, first=first, width=width: wcols(b, p.cols[s][0] + first, width),
                "wg",
                (n,),
                way,
                hops,
            )
            for n, (s, first, width, way, hops) in enumerate(p.streams)
            if s == segment
        ]

    def weight(s, first=0, width=None):
        c0, full = p.cols[s]
        width = full if width is None else width
        return W[:, :, pl.ds(c0 + first, width)].reshape(D, width)

    gathers = Queue()
    lnp = r["lnp"]
    if p.whole_lanes:
        lnall = r["lnall"]
        lnall[d] = r["ln_in"][...]
        for k, (way, hops) in enumerate(((1, p.far), (-1, R - 1 - p.far))):
            gathers.add(0, [gather_steps(lambda b: lnall.at[b], "lg", (k,), way, hops)], 0)
    else:
        lnp[...] = r["ln_in"][...].astype(f32)[0:8, :]
    gathers.add(0, gather_streams(0), 0)
    gathers.add(1, gather_streams(1), PT["o0"], PT["op"])
    gathers.add(2, gather_streams(2), PT["u0"], PT["up"])
    gathers.add(3, gather_streams(3), PT["d0"], PT["dp"])
    gathers.run(0)
    local[1].wait()
    h1f = r["h1f"]

    @pl.loop(0, tl // 32)
    def _(c):
        rows = pl.ds(pl.multiple_of(c * 32, 32), 32)
        h1f[rows, :] = norm(r["tok"][rows, :])[0]
    for n in range(2, 6):
        local[n].wait()
    if p.whole_lanes:
        for raw, (c0, width) in ((r["raw_out"], p.cols[1]), (r["raw_down"], p.cols[3])):
            W[d, :, pl.ds(c0, width)] = raw[...].astype(f32).T.astype(bf16)

    outlow = r["outlow"]
    outlow[...] = r["go"][...].astype(bf16)

    gathers.need(0)
    if p.whole_lanes:
        for b in range(R):
            lnp[:, pl.ds(b * rb, rb)] = lnall[b].astype(f32)[0:8, :]
    gain1, bias1, gain2, bias2 = (lnp[pl.ds(k, 1), :] for k in range(4))

    def norm_back(upstream, normed, inverse, gain):
        scaled = upstream * gain
        return inverse * (
            scaled
            - jnp.mean(scaled, axis=-1, keepdims=True)
            - normed * jnp.mean(scaled * normed, axis=-1, keepdims=True)
        )

    h1 = r["h1"]

    h1[...] = (h1f[...] * gain1 + bias1).astype(bf16)
    lane = lax.broadcasted_iota(jnp.int32, (1, LANES), 1)
    low = lane < HEAD_DIM

    def swap(v):
        return pltpu.roll(v, HEAD_DIM, 1)

    qs, kvs, qin, KV = r["qs"], r["kvs"], r["qin"], r["KV"]
    for t in range(H // 2):
        mixed = nn(h1[...], weight(0, 6 * HEAD_DIM * t, 6 * HEAD_DIM))
        t0, t1, t2 = (mixed[:, k * LANES : (k + 1) * LANES] for k in range(3))
        q_even, q_odd = t0 * 0.125, swap(t1) * 0.125
        for h, q in ((2 * t, q_even), (2 * t + 1, q_odd)):
            qs[h] = jnp.where(low, q[:half], swap(q[half:])).astype(bf16)
        kvs[2 * t] = jnp.where(low, swap(t0), swap(t1)).astype(bf16)
        kvs[2 * t + 1] = t2.astype(bf16)

    def head_dev(h, member):
        return (h * g + member, m)

    for k in range(1, H):
        h = add(dh, k, H)
        peer = head_dev(h, di)
        send(kvs.at[h], KV.at[d], "kv", k, peer)
        send(qs.at[h], qin.at[dh], "q", k, peer)
    gathers.run(PT["g1"])
    KV[d] = kvs[dh]
    qin[dh] = qs[dh]
    for k in range(H):
        j = add(dh, H - k, H)
        own = j * g + di
        if k:
            arrive(KV.at[own], "kv", k, head_dev(j, di))
        for q in range(1, g):
            send(KV.at[own], KV.at[own], "kvx", (k, q - 1), head_dev(dh, add(di, q, g)))
    gathers.run(PT["g2"])
    for k in range(1, H):
        j = add(dh, H - k, H)
        arrive(qin.at[j], "q", k, head_dev(j, di))
    for k in range(H):
        j = add(dh, H - k, H)
        for q in range(1, g):
            member = add(di, g - q, g)
            arrive(KV.at[j * g + member], "kvx", (k, q - 1), head_dev(dh, member))

    gathers.run(PT["g3"])

    qall, KVT = r["qall"], r["KVT"]
    for j in range(H):
        packed = qin[j].astype(f32)
        qall[pl.ds(j * tl, half), :] = jnp.where(low, packed, 0.0).astype(bf16)
        qall[pl.ds(j * tl + half, half), :] = jnp.where(low, swap(packed), 0.0).astype(bf16)

    ends = []
    total = 0
    for k in range(p.scenes):
        total = total + r["scene"][k]
        ends.append(total)

    def scene_of(pos):
        count = jnp.zeros(pos.shape, jnp.int32)
        for end in ends:
            count = count + (pos >= end).astype(jnp.int32)
        return count

    token_lane = lax.broadcasted_iota(jnp.int32, (1, tl), 1)
    q_scene = jnp.concatenate(
        [scene_of((j * g + di) * tl + token_lane) for j in range(H)], axis=1
    )
    token_row = lax.broadcasted_iota(jnp.int32, (tl, 1), 0)

    def masked_scores(o):
        scores = nt(KV[o], qall[...])
        return jnp.where(scene_of(o * tl + token_row) == q_scene, scores, FAR)

    unit = (
        lax.broadcasted_iota(jnp.int32, (LANES, LANES), 0)
        == lax.broadcasted_iota(jnp.int32, (LANES, LANES), 1)
    ).astype(bf16)

    top8, sum8, acc = r["top8"], r["sum8"], r["acc"]
    top8[...] = jnp.full((8, NQ), FAR, f32)
    sum8[...] = jnp.zeros((8, NQ), f32)
    acc[...] = jnp.zeros((LANES, NQ), f32)

    def maxima(o):
        KVT[o] = nt(unit, KV[o]).astype(bf16)
        top8[...] = jnp.maximum(
            top8[...], jnp.max(masked_scores(o).reshape(tl // 8, 8, NQ), axis=0)
        )

    pieces = 8 if R % 8 == 0 else 1

    def in_pieces(body, places):
        for c in range(pieces):
            pl.loop(c * R // pieces, (c + 1) * R // pieces)(body)
            gathers.run(places[c * len(places) // pieces])

    in_pieces(maxima, PT["g4"])

    top = r["top"]
    top[...] = jnp.max(top8[...], axis=0, keepdims=True)

    def exponentials(o):
        expo = jnp.exp(masked_scores(o) - top[...])
        sum8[...] += jnp.sum(expo.reshape(tl // 8, 8, NQ), axis=0)
        low_expo = expo.astype(bf16)
        if p.keep:
            r["prob"][o] = low_expo
        acc[...] += nn(KVT[o], low_expo)

    in_pieces(exponentials, PT["g5"])

    scale_row = 1.0 / jnp.sum(sum8[...], axis=0, keepdims=True)
    inv = r["inv"]
    inv[...] = scale_row
    attf, atts, attT = r["attf"], r["atts"], r["attT"]
    attf[...] = acc[pl.ds(HEAD_DIM, HEAD_DIM), :] * scale_row
    for j in range(H):
        atts[j] = attf[:, pl.ds(j * tl, tl)].astype(bf16)
    for k in range(1, H):
        j = add(dh, k, H)
        send(atts.at[j], attT.at[dh], "att", k, head_dev(j, di))
    attT[dh] = atts[dh]
    gathers.run(PT["g6"])
    for k in range(1, H):
        h = add(dh, H - k, H)
        arrive(attT.at[h], "att", k, head_dev(h, di))
    att = r["att"]
    att[...] = attT[...].reshape(HF, tl).astype(f32).T.astype(bf16)

    rs_send, rs_recv = r["rs_send"], r["rs_recv"]

    def rows_send(n, values):
        rs_send[n] = values.astype(bf16).reshape(M, rm, D)
        for k in range(1, M):
            send(rs_send.at[n, add(m, k, M)], rs_recv.at[n, k - 1], "rs", (n, k - 1), row_peer(k))

    def rows_sum(n):
        value = rs_send[n, m].astype(f32)
        for k in range(1, M):
            arrive(rs_recv.at[n, k - 1], "rs", (n, k - 1), row_peer(M - k))
            value = value + rs_recv[n, k - 1].astype(f32)
        return value

    def gather_send(n, ref):
        for k in range(1, M):
            send(ref.at[m], ref.at[m], "ag", (n, k - 1), row_peer(k))

    def gather_end(n, ref):
        for k in range(1, M):
            b = add(m, M - k, M)
            arrive(ref.at[b], "ag", (n, k - 1), row_peer(M - k))

    gathers.run(PT["g7"])
    gathers.need(1)
    rows_send(0, nt(att[...], weight(1)))
    gathers.run(PT["g8"])
    own_rows = pl.ds(pl.multiple_of(m * rm, rm), rm)
    mid, n2, r2, h2 = r["mid"], r["n2"], r["r2"], r["h2"]
    middle = r["tok"][own_rows, :] + rows_sum(0)
    mid[...] = middle
    normed, inverse = norm(middle)
    n2[...] = normed
    r2[...] = jnp.broadcast_to(inverse, (rm, LANES))
    h2[m] = (normed * gain2 + bias2).astype(bf16)
    gather_send(0, h2)
    gathers.run(PT["g9"])
    gathers.need(2)
    gather_end(0, h2)

    active, il, slope = r["active"], r["il"], r["slope"]
    c_one, c_two = 0.7978845608028654, 0.044715
    step = 256
    for c in range(U // step):
        inner = nn(h2[...].reshape(tl, D), weight(2, c * step, step))
        square = inner * inner
        t = jnp.tanh(c_one * inner * (1.0 + c_two * square))
        cdf = 0.5 * (1.0 + t)
        active[:, pl.ds(c * step, step)] = (inner * cdf).astype(bf16)
        slope[:, pl.ds(c * step, step)] = cdf + 0.5 * inner * (1.0 - t * t) * (
            c_one + 3.0 * c_one * c_two * square
        )
    sums = Queue()

    def grad_part(s, lhs, rhs):
        c0, width = p.cols[s]
        G = r["G"]
        piece = 256 if width % 256 == 0 else LANES
        for c in range(width // piece):
            value = tn(lhs, rhs[:, pl.ds(c * piece, piece)]).astype(bf16)
            G[:, :, pl.ds(c0 + c * piece, piece)] = value.reshape(R, rb, piece)

    leaving = []

    def leave(value, out):
        one = pltpu.make_async_copy(value, out, r["out"].at[len(leaving)])
        one.start()
        leaving.append(one)

    def sum_steps(n, stream, name):
        held, out = r["v" + name], r[name]
        s, first, width, way, hops = stream
        columns = pl.ds(p.cols[s][0] + first, width)
        G, came = r["G"], r["came%d" % n]
        onward, before = (ring(pos + way), m), (ring(pos - way), m)

        def step(t):
            def run():
                b = ring(pos + way * (hops - t))
                if t:
                    arrive(came.at[t - 1], "gg", (n, t - 1), before)
                if t == hops:
                    mine = pl.ds(first, width)
                    rest = G[b, :, columns] if hops < p.far else held[:, mine]
                    held[:, mine] = rest.astype(f32) + came[t - 1].astype(f32)
                    if hops == p.far:
                        if p.whole_lanes:
                            leave(held.at[:, mine], out.at[:, mine])
                        elif way < 0:
                            leave(held, out)
                    return
                if t:
                    value = G[b, :, columns].astype(f32) + came[t - 1].astype(f32)
                    G[b, :, columns] = value.astype(bf16)
                send(G.at[b, :, columns], came.at[t], "gg", (n, t), onward)

            return run

        return [step(t) for t in range(hops + 1)]

    def sum_streams(segment, name):
        return [
            sum_steps(n, stream, name) for n, stream in enumerate(p.streams) if stream[0] == segment
        ]

    grad_part(3, outlow[...], active)
    sums.add(3, sum_streams(3, "o_down"), 0, PT["sdp"])
    sums.run(0)
    gathers.need(3)
    for c in range(U // step):
        dact = nn(outlow[...], weight(3, c * step, step))
        il[:, pl.ds(c * step, step)] = (dact * slope[:, pl.ds(c * step, step)]).astype(bf16)
    rows_send(1, nt(il[...], weight(2)))

    grad_part(2, h2[...].reshape(tl, D), il)
    sums.add(2, sum_streams(2, "o_up"), PT["su"], PT["sup"])
    sums.run(PT["s1"])
    rows_send(2, nt(active[...], weight(3)))
    sums.run(PT["s2"])
    back2 = rows_sum(1)
    gm, ml = r["gm"], r["ml"]
    grad_middle = r["go"][own_rows, :] + norm_back(back2, n2[...], r2[:, 0:1], gain2)
    gm[...] = grad_middle
    ml[m] = grad_middle.astype(bf16)
    gather_send(1, ml)

    sums.run(PT["s3"])
    ln2g, ln2b = r["ln2g"], r["ln2b"]
    ln2g[...] = jnp.sum(back2 * n2[...], axis=0, keepdims=True)
    ln2b[...] = jnp.sum(back2, axis=0, keepdims=True)

    gather_end(1, ml)
    midlow = ml[...].reshape(tl, D)

    gs, gin, gall = r["gs"], r["gin"], r["gall"]
    gatt = nn(midlow, weight(1))
    for h in range(H):
        tile = gatt[:, (h // 2) * LANES : (h // 2 + 1) * LANES]
        even = h % 2 == 0
        first = tile[:half] if even else swap(tile[:half])
        second = swap(tile[half:]) if even else tile[half:]
        gs[h] = jnp.where(low, first, second).astype(bf16)
    for k in range(1, H):
        h = add(dh, k, H)
        send(gs.at[h], gin.at[dh], "ga", k, head_dev(h, di))
    gin[dh] = gs[dh]

    grad_part(1, midlow, att)
    sums.add(1, sum_streams(1, "o_out"), PT["so"], PT["sop"])
    sums.run(PT["s4"])
    for k in range(1, H):
        j = add(dh, H - k, H)
        arrive(gin.at[j], "ga", k, head_dev(j, di))

    inv_col = jnp.broadcast_to(inv[...], (LANES, NQ)).T
    shift_parts = []
    for j in range(H):
        packed = gin[j].astype(f32)
        top_half = jnp.where(low, 0.0, swap(packed))
        bottom = jnp.where(low, 0.0, packed)
        ga = jnp.concatenate([top_half, bottom], axis=0)
        gaT = ga.T[HEAD_DIM:, :]
        shift_parts.append(
            jnp.sum(gaT * attf[:, pl.ds(j * tl, tl)], axis=0, keepdims=True)
            * inv[:, pl.ds(j * tl, tl)]
        )
        gall[pl.ds(j * tl, tl), :] = (ga * inv_col[j * tl : (j + 1) * tl]).astype(bf16)
    shift = r["shift"]
    shift[...] = jnp.concatenate(shift_parts, axis=1)

    acc[...] = jnp.zeros((LANES, NQ), f32)
    dkvs, dkvx, dkv_in = r["dkvs"], r["dkvx"], r["dkv_in"]

    def key_grads(o):
        prob = r["prob"][o] if p.keep else jnp.exp(masked_scores(o) - top[...]).astype(bf16)
        dprob = nt(KV[o], gall[...])
        dscore = (prob.astype(f32) * (dprob - shift[...])).astype(bf16)
        acc[...] += nn(KVT[o], dscore)
        return nn(dscore, qall[...]) + nn(prob, gall[...])

    for q in range(1, g):
        member = add(di, q, g)
        for k in range(H):
            j = add(dh, k, H)
            dkvs[q, k] = key_grads(j * g + member).astype(bf16)
            send(dkvs.at[q, k], dkvx.at[q - 1, k], "dkvx", (q - 1, k), head_dev(dh, member))
            sums.run(PT["s4b"][k * len(PT["s4b"]) // H])
        sums.run(PT["s5"])
    for k in [*range(1, H), 0]:
        j = add(dh, k, H)
        dkv = key_grads(j * g + di)
        for q in range(1, g):
            arrive(dkvx.at[q - 1, k], "dkvx", (q - 1, k), head_dev(dh, add(di, g - q, g)))
            dkv = dkv + dkvx[q - 1, k].astype(f32)
        if k:
            dkvs[0, k] = dkv.astype(bf16)
            send(dkvs.at[0, k], dkv_in.at[dh], "dkv", k, head_dev(j, di))
        else:
            dkv_in[dh] = dkv.astype(bf16)
        sums.run(PT["s5b"][k * len(PT["s5b"]) // H])

    dqs, dqT = r["dqs"], r["dqT"]
    for j in range(H):
        dqs[j] = (acc[pl.ds(0, HEAD_DIM), pl.ds(j * tl, tl)] * 0.125).astype(bf16)
    for k in range(1, H):
        j = add(dh, k, H)
        send(dqs.at[j], dqT.at[dh], "dq", k, head_dev(j, di))
    dqT[dh] = dqs[dh]
    sums.run(PT["s6"])

    res = r["res"]
    res[m] = (mid[...] + rows_sum(2)).astype(bf16)
    gather_send(2, res)

    sums.run(PT["s7"])
    for k in range(1, H):
        h = add(dh, H - k, H)
        arrive(dqT.at[h], "dq", k, head_dev(h, di))
        arrive(dkv_in.at[h], "dkv", k, head_dev(h, di))

    gmix = r["gmix"]
    dq = dqT[...].reshape(HF, tl).astype(f32).T

    def head_sum(h):
        return dkv_in[h].astype(f32)

    for t in range(H // 2):
        both = dq[:, t * LANES : (t + 1) * LANES]
        even = swap(head_sum(2 * t))
        base = 6 * HEAD_DIM * t
        gmix[:, pl.ds(base, LANES)] = jnp.where(low, both, even).astype(bf16)
        gmix[:, pl.ds(base + LANES, LANES)] = jnp.where(low, even, both).astype(bf16)
        gmix[:, pl.ds(base + 2 * LANES, LANES)] = head_sum(2 * t + 1).astype(bf16)

    grad_part(0, h1[...], gmix)
    sums.add(0, sum_streams(0, "o_qkv"), PT["sq"], PT["sqp"])
    sums.run(PT["s8"])
    rows_send(3, nt(gmix[...], weight(0)))
    sums.run(PT["s9"])
    back1 = rows_sum(3)
    n1, r1 = norm(r["tok"][own_rows, :])
    gt = r["gt"]
    gt[m] = (gm[...] + norm_back(back1, n1, r1, gain1)).astype(bf16)
    gather_send(3, gt)
    ln_rows = jnp.concatenate(
        [
            jnp.sum(back1 * n1, axis=0, keepdims=True),
            jnp.sum(back1, axis=0, keepdims=True),
            ln2g[...],
            ln2b[...],
            jnp.zeros((4, D), f32),
        ],
        axis=0,
    )
    lnrow, lnr_in = r["lnrow"], r["lnr_in"]
    for b in range(D // LANES):
        lnrow[b] = ln_rows[:, b * LANES : (b + 1) * LANES]

    def lane_block(b):
        return b * rb // LANES

    for k in range(1, R):
        o = add(d, k, R)
        send(lnrow.at[lane_block(o)], lnr_in.at[d], "lr", k - 1, (o, m))
    lnr_in[d] = lnrow[lane_block(d)]
    sums.run(PT["s10"])
    for k in range(1, R):
        o = add(d, R - k, R)
        arrive(lnr_in.at[o], "lr", k - 1, (o, m))
    value = lnr_in[0]
    for b in range(1, R):
        value = value + lnr_in[b]
    gather_end(2, res)
    leave(res, r["o_result"])
    lnx = r["lnx"]
    lnx[m] = value
    for k in range(1, M):
        send(lnx.at[m], lnx.at[m], "ln", k - 1, row_peer(k))
    sums.run(100)

    gather_end(3, gt)
    leave(gt, r["o_tokens"])
    for k in range(1, M):
        arrive(lnx.at[add(m, M - k, M)], "ln", k - 1, row_peer(M - k))
    value = lnx[0]
    for k in range(1, M):
        value = value + lnx[k]
    r["o_ln"][...] = value
    for one in leaving:
        one.wait()
    for one in sent:
        one.wait_send()


def layer(p, tokens, grad_out, w_qkv, w_out, w_up, w_down, ln_in, scene):
    R, M, L, H, g = p.R, p.M, p.L, p.H, p.g
    tl, D, rb, rm, U, HF, NQ = p.tl, p.D, p.rb, p.rm, p.U, p.HF, p.NQ
    half = tl // 2
    ins = {
        "tokens": tokens,
        "grad_out": grad_out,
        "w_qkv": w_qkv,
        "w_out": w_out,
        "w_up": w_up,
        "w_down": w_down,
        "ln_in": ln_in,
        "scene": scene,
    }
    outs = {
        "o_result": ((M, rm, D), bf16),
        "o_tokens": ((M, rm, D), bf16),
        "o_qkv": ((rb, 3 * HF), f32),
        "o_out": ((rb, HF), f32),
        "o_up": ((rb, U), f32),
        "o_down": ((rb, U), f32),
        "o_ln": ((8, LANES), f32),
    }
    v = pltpu.VMEM
    space = pl.BlockSpec(memory_space=pltpu.HBM)
    out_specs = [space] * 6 + [pl.BlockSpec(memory_space=pltpu.VMEM)]
    scratch = {
        "vo_qkv": v((rb, 3 * HF), f32),
        "vo_out": v((rb, HF), f32),
        "vo_up": v((rb, U), f32),
        "vo_down": v((rb, U), f32),
        "W": v((R, rb, p.WC), bf16),
        "tok": v((tl, D), f32),
        "go": v((tl, D), f32),
        "outlow": v((tl, D), bf16),
        "lnp": v((8, D), f32),
        "h1": v((tl, D), bf16),
        "h1f": v((tl, D), f32),
        "slope": v((tl, U), f32),
        "qs": v((H, half, LANES), bf16),
        "kvs": v((H, tl, LANES), bf16),
        "qin": v((H, half, LANES), bf16),
        "KV": v((R, tl, LANES), bf16),
        "KVT": v((R, LANES, tl), bf16),
        "qall": v((NQ, LANES), bf16),
        "top8": v((8, NQ), f32),
        "sum8": v((8, NQ), f32),
        "top": v((1, NQ), f32),
        "inv": v((1, NQ), f32),
        "shift": v((1, NQ), f32),
        "acc": v((LANES, NQ), f32),
        "attf": v((HEAD_DIM, NQ), f32),
        "atts": v((H, HEAD_DIM, tl), bf16),
        "attT": v((H, HEAD_DIM, tl), bf16),
        "att": v((tl, HF), bf16),
        "rs_send": v((4, M, rm, D), bf16),
        "rs_recv": v((4, M - 1, rm, D), bf16),
        "mid": v((rm, D), f32),
        "n2": v((rm, D), f32),
        "r2": v((rm, LANES), f32),
        "h2": v((M, rm, D), bf16),
        "active": v((tl, U), bf16),
        "il": v((tl, U), bf16),
        "gm": v((rm, D), f32),
        "ml": v((M, rm, D), bf16),
        "ln2g": v((1, D), f32),
        "ln2b": v((1, D), f32),
        "lnrow": v((D // LANES, 8, LANES), f32),
        "lnr_in": v((R, 8, LANES), f32),
        "lnx": v((M, 8, LANES), f32),
        "G": v((R, rb, p.WC), bf16),
        "gs": v((H, half, LANES), bf16),
        "gin": v((H, half, LANES), bf16),
        "gall": v((NQ, LANES), bf16),
        "dkvs": v((g, H, tl, LANES), bf16),
        "dkvx": v((max(g - 1, 1), H, tl, LANES), bf16),
        "dkv_in": v((H, tl, LANES), bf16),
        "dqs": v((H, HEAD_DIM, tl), bf16),
        "dqT": v((H, HEAD_DIM, tl), bf16),
        "gmix": v((tl, 3 * HF), bf16),
        "res": v((M, rm, D), bf16),
        "gt": v((M, rm, D), bf16),
    }
    if p.keep:
        scratch["prob"] = v((R, tl, NQ), bf16)
    if p.whole_lanes:
        scratch["raw_out"] = v((HF, rb), bf16)
        scratch["raw_down"] = v((U, rb), bf16)
        scratch["lnall"] = v((R, 16, rb), bf16)
    for n, (_, _, width, _, hops) in enumerate(p.streams):
        scratch["came%d" % n] = v((hops, rb, width), bf16)
    sems = {
        "wg": (len(p.streams), p.far),
        "gg": (len(p.streams), p.far),
        "lg": (2, p.far),
        "lr": (R - 1,),
        "kv": (H,),
        "q": (H,),
        "kvx": (H, max(g - 1, 1)),
        "att": (H,),
        "rs": (4, M - 1),
        "ag": (4, M - 1),
        "ga": (H,),
        "dkv": (H,),
        "dkvx": (max(g - 1, 1), H),
        "dq": (H,),
        "ln": (M - 1,),
    }
    for name, shape in sems.items():
        scratch[name + "_s"] = pltpu.SemaphoreType.DMA(shape)
        scratch[name + "_r"] = pltpu.SemaphoreType.DMA(shape)
    scratch["out"] = pltpu.SemaphoreType.DMA((10,))
    scratch["loc"] = pltpu.SemaphoreType.DMA((6,))
    names = (*ins, *outs, *scratch)
    any_spec = pl.BlockSpec(memory_space=pltpu.HBM)
    flops = 6 * tl * D * p.WC + 14 * NQ * R * tl * HEAD_DIM
    return pl.pallas_call(
        functools.partial(kernel, p, names),
        out_shape=[jax.ShapeDtypeStruct(*one) for one in outs.values()],
        in_specs=[any_spec] * 6 + [pl.BlockSpec(memory_space=pltpu.VMEM), pl.BlockSpec(memory_space=pltpu.SMEM)],
        out_specs=out_specs,
        scratch_shapes=list(scratch.values()),
        compiler_params=pltpu.CompilerParams(
            collective_id=0, has_side_effects=True, vmem_limit_bytes=60 << 20
        ),
        cost_estimate=pl.CostEstimate(flops=flops, bytes_accessed=8 << 20, transcendentals=NQ * R * tl),
        name="layer",
    )(*ins.values())


def finish_kernel(*refs):
    hbm, outs, held, made, sem, done = refs[:7], refs[7:17], refs[17:24], refs[24:28], refs[28], refs[29]
    reads = [pltpu.make_async_copy(hbm[k], held[k], sem.at[k]) for k in range(7)]
    order = (5, 4, 2, 3, 0, 1, 6)
    for k in order:
        reads[k].start()
    writes = []
    forms = {
        0: (made[0], lambda v: v.reshape(-1, v.shape[-1]).astype(f32)),
        1: (made[1], lambda v: v.reshape(-1, v.shape[-1]).astype(f32)),
        3: (made[2], lambda v: v.T),
        5: (made[3], lambda v: v.T),
    }
    for k in order:
        reads[k].wait()
        if k == 6:
            for n in range(4):
                outs[6 + n][...] = held[6][n, :]
            break
        value = held[k]
        if k in forms:
            value, form = forms[k]
            value[...] = form(held[k][...])
        one = pltpu.make_async_copy(value, outs[k], done.at[k])
        one.start()
        writes.append(one)
    for one in writes:
        one.wait()


def finish(p, parts):
    tl, D, rb, U, HF = p.tl, p.D, p.rb, p.U, p.HF
    shapes = [(tl, D), (tl, D), (rb, 3 * HF), (HF, rb), (rb, U), (U, rb)] + [(rb,)] * 4
    held = [pltpu.VMEM(one.shape, one.dtype) for one in parts]
    made = [pltpu.VMEM(shapes[k], f32) for k in (0, 1, 3, 5)]
    return pl.pallas_call(
        finish_kernel,
        out_shape=[jax.ShapeDtypeStruct(shape, f32) for shape in shapes],
        in_specs=[pl.BlockSpec(memory_space=pltpu.HBM)] * 7,
        out_specs=[pl.BlockSpec(memory_space=pltpu.HBM)] * 6
        + [pl.BlockSpec(memory_space=pltpu.VMEM)] * 4,
        scratch_shapes=[*held, *made, pltpu.SemaphoreType.DMA((7,)), pltpu.SemaphoreType.DMA((6,))],
        compiler_params=pltpu.CompilerParams(vmem_limit_bytes=62 << 20),
        cost_estimate=pl.CostEstimate(flops=0, bytes_accessed=6 << 20, transcendentals=0),
        name="finish",
    )(*parts)


def on_device(
    tokens,
    w_qkv,
    w_out,
    w_up,
    w_down,
    ln1_gain,
    ln1_bias,
    ln2_gain,
    ln2_bias,
    scene_lengths,
    grad_out,
):
    p = Plan(tokens, w_qkv, w_up, scene_lengths, lax.axis_size("dp"), lax.axis_size("mp"))
    rb, D, tl = p.rb, p.D, p.tl
    vectors = jnp.stack([ln1_gain, ln1_bias, ln2_gain, ln2_bias])
    if not p.whole_lanes:
        vectors = lax.all_gather(vectors, "dp", axis=1, tiled=True)
        w_out, w_down = w_out.T, w_down.T
    vectors = jnp.pad(vectors, ((0, 12), (0, 0)))
    parts = layer(p, tokens, grad_out, w_qkv, w_out, w_up, w_down, vectors, scene_lengths)
    if p.whole_lanes:
        return finish(p, parts)
    result, grad_tokens, qkv, out, up, down, ln = parts
    first = lax.axis_index("dp") * rb % LANES
    ln = lax.dynamic_slice_in_dim(ln, first, rb, 1)
    return (
        result.reshape(tl, D).astype(f32),
        grad_tokens.reshape(tl, D).astype(f32),
        qkv,
        out.T,
        up,
        down.T,
        ln[0],
        ln[1],
        ln[2],
        ln[3],
    )


def solution(mesh):
    weights = (P("dp", "mp"), P("mp", "dp"), P("dp", "mp"), P("mp", "dp"))
    rows = P("dp", None)
    vector = P("dp")
    return jax.shard_map(
        on_device,
        mesh=mesh,
        in_specs=(rows, *weights, vector, vector, vector, vector, P(), rows),
        out_specs=(rows, rows, *weights, vector, vector, vector, vector),
        check_vma=False,
    )
```

```python
import functools

import jax
import jax.numpy as jnp
from jax import lax
from jax.experimental import pallas as pl
from jax.experimental.pallas import tpu as pltpu
from jax.sharding import PartitionSpec as P

HEAD_DIM = 64
LANES = 128
FAR = -1e30
MESH = pl.DeviceIdType.MESH
PT = {
    "g1b": -4.6,
    "g0": 2.5,
    "o0": 1.8,
    "op": 0.96,
    "u0": 1.3,
    "d0": 4.5,
    "g1": 2.8,
    "g2": 4.3,
    "g3": -1.5,
    "g4": [1.7, 4.5, 1.8, 3.1, 3.6, 1.3, 4.6, 5.2],
    "g5": [4.9, 5.4, 4.0, 5.1, 4.8, 4.5, 2.2, 5.4],
    "g6": -11.4,
    "g7": -10.9,
    "g8": 7.2,
    "g9": 8.3,
    "su": 0.3,
    "s1": -1.5,
    "s2": 3.0,
    "s3": 2.5,
    "so": 2.1,
    "sop": 1.6,
    "s4": 3.2,
    "s4b": [-13.5, -8.0, -5.3, -8.1],
    "s5": -2.7,
    "s5b": [-11.3, -5.4, -4.8, -6.8],
    "s6": 5.2,
    "s7": 5.3,
    "sq": 9.5,
    "sqp": 0.5,
    "up": 1.44,
    "dp": 0.98,
    "sdp": 1.54,
    "sup": 1.42,
    "s8": 6.7,
    "s9": -4.0,
    "s10": 7.3,
}
bf16 = jnp.bfloat16
f32 = jnp.float32


def nn(a, b):
    return lax.dot_general(a, b, (((1,), (0,)), ((), ())), preferred_element_type=f32)


def nt(a, b):
    return lax.dot_general(a, b, (((1,), (1,)), ((), ())), preferred_element_type=f32)


def tn(a, b):
    return lax.dot_general(a, b, (((0,), (0,)), ((), ())), preferred_element_type=f32)


class Plan:
    def __init__(self, tokens, w_qkv, w_up, scenes, dp, mp):
        self.R, self.M = dp, mp
        self.tl, self.D = tokens.shape
        self.rb = self.D // dp
        self.L = dp // 2
        self.H = w_qkv.shape[1] // (3 * HEAD_DIM)
        self.g = dp // self.H
        self.U = w_up.shape[1]
        self.rm = self.tl // mp
        self.HF = self.H * HEAD_DIM
        self.scenes = scenes.shape[0]
        self.NQ = self.H * self.tl
        self.keep = dp * self.tl <= 4096
        self.whole_lanes = self.rb % LANES == 0
        widths = (0, self.HF, self.U, self.U)
        self.cols = []
        start = 0
        for width in widths:
            self.cols.append((start, width))
            start += width
        self.WC = start
        far, near = dp // 2, dp - 1 - dp // 2
        self.far = far
        self.streams = []
        for s, width in enumerate(widths):
            half = width // 2
            if not width:
                continue
            for first, way in ((0, 1), (half, -1)):
                self.streams.append((s, first, half, way, far))
                self.streams.append((s, first, half, -way, near))


def kernel(p, names, *refs):
    r = dict(zip(names, refs))
    R, M, L, H, g = p.R, p.M, p.L, p.H, p.g
    tl, D, rb, rm, U, HF, NQ = p.tl, p.D, p.rb, p.rm, p.U, p.HF, p.NQ
    half = tl // 2
    d = lax.axis_index("dp")
    m = lax.axis_index("mp")
    z, x = d // 2, lax.rem(d, 2)
    dh, di = d // g, lax.rem(d, g)
    sent = []

    def add(a, k, n):
        return lax.rem(a + k, n)

    def copy(src, dst, name, index, peer):
        return pltpu.make_async_remote_copy(
            src_ref=src,
            dst_ref=dst,
            send_sem=r[name + "_s"].at[index],
            recv_sem=r[name + "_r"].at[index],
            device_id=peer,
            device_id_type=MESH,
        )

    def send(src, dst, name, index, peer):
        one = copy(src, dst, name, index, peer)
        one.start()
        sent.append(one)

    def arrive(dst, name, index, peer):
        copy(dst, dst, name, index, peer).wait_recv()

    def head_dev(h, member):
        return (h * g + member, m)

    m_side, m_core = lax.rem(m + 2, M), m + 1 - 2 * lax.rem(m, 2)
    m_both = lax.rem(m_core + 2, M)
    side, core = (d, m_side), (d, m_core)

    def row_peer(k):
        return (d, add(m, k, M))

    pos = z + x * (R - 1 - 2 * z)

    def ring(q):
        q = lax.rem(q + 2 * R, R)
        far = q // L
        return 2 * q * (1 - far) + (2 * (R - 1 - q) + 1) * far

    W = r["W"]

    def wcols(b, c0, width):
        return W.at[b, :, pl.ds(c0, width)]

    local = []
    for n, (src, dst) in enumerate(
        [
            (r["w_qkv"], r["raw_qkv"]),
            (r["tokens"], r["tok"]),
            (r["w_up"], wcols(d, *p.cols[2])),
            (r["w_out"], r["raw_out"] if p.whole_lanes else wcols(d, *p.cols[1])),
            (r["w_down"], r["raw_down"] if p.whole_lanes else wcols(d, *p.cols[3])),
            (r["grad_out"], r["go"]),
        ]
    ):
        one = pltpu.make_async_copy(src, dst, r["loc"].at[n])
        one.start()
        local.append(one)

    barrier = pltpu.get_barrier_semaphore()
    greeted = [head_dev(add(dh, k, H), di) for k in range(1, H)]
    greeted += [head_dev(dh, add(di, q, g)) for q in range(1, g)]
    greeted += [row_peer(k) for k in range(1, M)]
    if g != 2:
        greeted += [(ring(pos + 1), m), (ring(pos - 1), m)]
    for peer in greeted:
        pl.semaphore_signal(barrier, 1, device_id=peer, device_id_type=MESH)

    def norm(values):
        center = values - jnp.mean(values, axis=-1, keepdims=True)
        inverse = lax.rsqrt(jnp.mean(center * center, axis=-1, keepdims=True) + 1e-05)
        return center * inverse, inverse

    lane = lax.broadcasted_iota(jnp.int32, (1, LANES), 1)
    low = lane < HEAD_DIM

    def swap(v):
        return pltpu.roll(v, HEAD_DIM, 1)

    N, ws, Win = r["N"], r["ws"], r["Win"]
    local[0].wait()
    vectors = 0.0
    if p.whole_lanes:
        before = jnp.zeros((HEAD_DIM, rb), f32)
        after = jnp.zeros((HEAD_DIM - 16, rb), f32)
        vectors = jnp.concatenate([before, r["ln_in"][...].astype(f32), after], axis=0).T
    for t in range(H // 2):
        t0, t1, t2 = (
            r["raw_qkv"][:, pl.ds((3 * t + k) * LANES, LANES)].astype(f32) for k in range(3)
        )
        ws[2 * t, :, pl.ds(0, LANES)] = t0.astype(bf16)
        ws[2 * t, :, pl.ds(LANES, LANES)] = jnp.where(low, t1, vectors).astype(bf16)
        ws[2 * t + 1, :, pl.ds(0, LANES)] = jnp.where(low, swap(t1), swap(t2)).astype(bf16)
        ws[2 * t + 1, :, pl.ds(LANES, LANES)] = jnp.where(low, swap(t2), vectors).astype(bf16)
    local[1].wait()

    def norm_quarter(b):
        for c in range(rm // 32):
            first = pl.multiple_of(b * rm + c * 32, 32)
            N[dh, b, pl.ds(c * 32, 32), :] = norm(r["tok"][pl.ds(first, 32), :])[0].astype(bf16)

    norm_quarter(m)
    pl.semaphore_wait(barrier, len(greeted))
    for k in range(1, H):
        h = add(dh, k, H)
        send(N.at[dh, m], N.at[dh, m], "na", k, head_dev(h, di))
        send(ws.at[h], Win.at[d], "wa", k, head_dev(h, di))
    Win[d] = ws[dh]
    for q in range(1, g):
        send(Win.at[d], Win.at[d], "wax", (0, q - 1), head_dev(dh, add(di, q, g)))

    class Queue:
        def __init__(self):
            self.steps = []

        def add(self, tag, streams, start, pace=1.0):
            for stream in streams:
                self.steps += [(start + pace * t, tag, run) for t, run in enumerate(stream)]
            self.steps.sort(key=lambda one: one[0])

        def run(self, place):
            while self.steps and self.steps[0][0] <= place:
                self.steps.pop(0)[2]()

        def need(self, tag):
            while any(one[1] == tag for one in self.steps):
                self.steps.pop(0)[2]()

    def gather_steps(block, name, index, way, hops):
        onward, before = (ring(pos + way), m), (ring(pos - way), m)

        def step(t):
            def run():
                here = block(ring(pos - way * t))
                if t:
                    arrive(here, name, (*index, t - 1), before)
                if t < hops:
                    send(here, here, name, (*index, t), onward)

            return run

        return [step(t) for t in range(hops + 1)]

    def gather_streams(segment):
        return [
            gather_steps(
                lambda b, s=s, first=first, width=width: wcols(b, p.cols[s][0] + first, width),
                "wg",
                (n,),
                way,
                hops,
            )
            for n, (s, first, width, way, hops) in enumerate(p.streams)
            if s == segment
        ]

    def weight(s, first=0, width=None):
        c0, full = p.cols[s]
        width = full if width is None else width
        return W[:, :, pl.ds(c0 + first, width)].reshape(D, width)

    gathers = Queue()
    lnp = r["lnp"]
    if not p.whole_lanes:
        lnp[...] = r["ln_in"][...].astype(f32)[0:8, :]
    gathers.add(1, gather_streams(1), PT["o0"], PT["op"])
    gathers.add(2, gather_streams(2), PT["u0"], PT["up"])
    gathers.add(3, gather_streams(3), PT["d0"], PT["dp"])
    gathers.run(0)
    for k in range(1, M):
        norm_quarter(add(m, k, M))
    for n in range(2, 6):
        local[n].wait()
    if p.whole_lanes:
        for raw, (c0, width) in ((r["raw_out"], p.cols[1]), (r["raw_down"], p.cols[3])):
            W[d, :, pl.ds(c0, width)] = raw[...].astype(f32).T.astype(bf16)

    outlow = r["outlow"]
    outlow[...] = r["go"][...].astype(bf16)

    for k in range(1, H):
        j = add(dh, H - k, H)
        own = j * g + di
        arrive(N.at[j, m], "na", k, head_dev(j, di))
        send(N.at[j, m], N.at[j, m], "ny", k, side)
        send(N.at[j, m], N.at[j, m], "nc", k, core)
        arrive(Win.at[own], "wa", k, head_dev(j, di))
        for q in range(1, g):
            send(Win.at[own], Win.at[own], "wax", (k, q - 1), head_dev(dh, add(di, q, g)))
        gathers.run(PT["g0"])
    for k in range(1, H):
        j = add(dh, H - k, H)
        arrive(N.at[j, m_side], "ny", k, side)
        send(N.at[j, m_side], N.at[j, m_side], "nd", k, core)
    for k in range(H):
        j = add(dh, H - k, H)
        for q in range(1, g):
            member = add(di, g - q, g)
            arrive(Win.at[j * g + member], "wax", (k, q - 1), head_dev(dh, member))
    if p.whole_lanes:
        columns = Win[:, :, pl.ds(LANES, LANES)].reshape(D, LANES).astype(f32)
        lnp[...] = columns.T[HEAD_DIM : HEAD_DIM + 8, :]
    gain1, bias1, gain2, bias2 = (lnp[pl.ds(k, 1), :] for k in range(4))

    def norm_back(upstream, normed, inverse, gain):
        scaled = upstream * gain
        return inverse * (
            scaled
            - jnp.mean(scaled, axis=-1, keepdims=True)
            - normed * jnp.mean(scaled * normed, axis=-1, keepdims=True)
        )

    h1 = r["h1"]

    def hidden(j):
        part = N[j].reshape(tl, D).astype(f32) * gain1 + bias1
        h1[pl.ds(pl.multiple_of(j * tl, tl), tl), :] = part.astype(bf16)

    hidden(dh)
    gathers.run(PT["g1"])
    for k in range(1, H):
        j = add(dh, H - k, H)
        arrive(N.at[j, m_core], "nc", k, core)
        arrive(N.at[j, m_both], "nd", k, core)
        hidden(j)
        gathers.run(PT["g1b"])

    KV, qall, KVT = r["KV"], r["qall"], r["KVT"]
    head_weight = Win[...].reshape(D, 2 * LANES)
    for k in range(H):
        j = add(dh, H - k, H)
        rows = pl.ds(pl.multiple_of(j * tl, tl), tl)
        mixed = nn(h1[rows, :], head_weight)
        t0, t1 = mixed[:, :LANES], mixed[:, LANES:]
        qall[rows, :] = jnp.where(low, t0 * 0.125, 0.0).astype(bf16)
        KV[j * g + di] = jnp.where(low, swap(t0), swap(t1)).astype(bf16)
        for q in range(1, g):
            own = j * g + di
            send(KV.at[own], KV.at[own], "kvx", (k, q - 1), head_dev(dh, add(di, q, g)))
    gathers.run(PT["g2"])
    for k in range(H):
        j = add(dh, H - k, H)
        for q in range(1, g):
            member = add(di, g - q, g)
            arrive(KV.at[j * g + member], "kvx", (k, q - 1), head_dev(dh, member))

    gathers.run(PT["g3"])

    ends = []
    total = 0
    for k in range(p.scenes):
        total = total + r["scene"][k]
        ends.append(total)

    def scene_of(pos):
        count = jnp.zeros(pos.shape, jnp.int32)
        for end in ends:
            count = count + (pos >= end).astype(jnp.int32)
        return count

    token_lane = lax.broadcasted_iota(jnp.int32, (1, tl), 1)
    q_scene = jnp.concatenate(
        [scene_of((j * g + di) * tl + token_lane) for j in range(H)], axis=1
    )
    token_row = lax.broadcasted_iota(jnp.int32, (tl, 1), 0)

    def masked_scores(o):
        scores = nt(KV[o], qall[...])
        return jnp.where(scene_of(o * tl + token_row) == q_scene, scores, FAR)

    unit = (
        lax.broadcasted_iota(jnp.int32, (LANES, LANES), 0)
        == lax.broadcasted_iota(jnp.int32, (LANES, LANES), 1)
    ).astype(bf16)

    top8, sum8, acc = r["top8"], r["sum8"], r["acc"]
    top8[...] = jnp.full((8, NQ), FAR, f32)
    sum8[...] = jnp.zeros((8, NQ), f32)
    acc[...] = jnp.zeros((LANES, NQ), f32)

    def maxima(o):
        KVT[o] = nt(unit, KV[o]).astype(bf16)
        top8[...] = jnp.maximum(
            top8[...], jnp.max(masked_scores(o).reshape(tl // 8, 8, NQ), axis=0)
        )

    pieces = 8 if R % 8 == 0 else 1

    def in_pieces(body, places):
        for c in range(pieces):
            pl.loop(c * R // pieces, (c + 1) * R // pieces)(body)
            gathers.run(places[c * len(places) // pieces])

    in_pieces(maxima, PT["g4"])

    top = r["top"]
    top[...] = jnp.max(top8[...], axis=0, keepdims=True)

    def exponentials(o):
        expo = jnp.exp(masked_scores(o) - top[...])
        sum8[...] += jnp.sum(expo.reshape(tl // 8, 8, NQ), axis=0)
        low_expo = expo.astype(bf16)
        if p.keep:
            r["prob"][o] = low_expo
        acc[...] += nn(KVT[o], low_expo)

    in_pieces(exponentials, PT["g5"])

    scale_row = 1.0 / jnp.sum(sum8[...], axis=0, keepdims=True)
    inv = r["inv"]
    inv[...] = scale_row
    attf, atts, attT = r["attf"], r["atts"], r["attT"]
    attf[...] = acc[pl.ds(HEAD_DIM, HEAD_DIM), :] * scale_row
    for j in range(H):
        atts[j] = attf[:, pl.ds(j * tl, tl)].astype(bf16)
    for k in range(1, H):
        j = add(dh, k, H)
        send(atts.at[j], attT.at[dh], "att", k, head_dev(j, di))
    attT[dh] = atts[dh]
    gathers.run(PT["g6"])
    for k in range(1, H):
        h = add(dh, H - k, H)
        arrive(attT.at[h], "att", k, head_dev(h, di))
    att = r["att"]
    att[...] = attT[...].reshape(HF, tl).astype(f32).T.astype(bf16)

    rs_send, rs_recv = r["rs_send"], r["rs_recv"]

    def rows_send(n, values):
        rs_send[n] = values.astype(bf16).reshape(M, rm, D)
        for k in range(1, M):
            send(rs_send.at[n, add(m, k, M)], rs_recv.at[n, k - 1], "rs", (n, k - 1), row_peer(k))

    def rows_sum(n):
        value = rs_send[n, m].astype(f32)
        for k in range(1, M):
            arrive(rs_recv.at[n, k - 1], "rs", (n, k - 1), row_peer(M - k))
            value = value + rs_recv[n, k - 1].astype(f32)
        return value

    def gather_send(n, ref):
        for k in range(1, M):
            send(ref.at[m], ref.at[m], "ag", (n, k - 1), row_peer(k))

    def gather_end(n, ref):
        for k in range(1, M):
            b = add(m, M - k, M)
            arrive(ref.at[b], "ag", (n, k - 1), row_peer(M - k))

    gathers.run(PT["g7"])
    gathers.need(1)
    rows_send(0, nt(att[...], weight(1)))
    gathers.run(PT["g8"])
    own_rows = pl.ds(pl.multiple_of(m * rm, rm), rm)
    mid, n2, r2, h2 = r["mid"], r["n2"], r["r2"], r["h2"]
    middle = r["tok"][own_rows, :] + rows_sum(0)
    mid[...] = middle
    normed, inverse = norm(middle)
    n2[...] = normed
    r2[...] = jnp.broadcast_to(inverse, (rm, LANES))
    h2[m] = (normed * gain2 + bias2).astype(bf16)
    gather_send(0, h2)
    gathers.run(PT["g9"])
    gathers.need(2)
    gather_end(0, h2)

    active, il, slope = r["active"], r["il"], r["slope"]
    c_one, c_two = 0.7978845608028654, 0.044715
    step = 256
    for c in range(U // step):
        inner = nn(h2[...].reshape(tl, D), weight(2, c * step, step))
        square = inner * inner
        t = jnp.tanh(c_one * inner * (1.0 + c_two * square))
        cdf = 0.5 * (1.0 + t)
        active[:, pl.ds(c * step, step)] = (inner * cdf).astype(bf16)
        slope[:, pl.ds(c * step, step)] = cdf + 0.5 * inner * (1.0 - t * t) * (
            c_one + 3.0 * c_one * c_two * square
        )
    sums = Queue()

    def grad_part(s, lhs, rhs):
        c0, width = p.cols[s]
        G = r["G"]
        piece = 256 if width % 256 == 0 else LANES
        for c in range(width // piece):
            value = tn(lhs, rhs[:, pl.ds(c * piece, piece)]).astype(bf16)
            G[:, :, pl.ds(c0 + c * piece, piece)] = value.reshape(R, rb, piece)

    leaving = []

    def leave(value, out):
        one = pltpu.make_async_copy(value, out, r["out"].at[len(leaving)])
        one.start()
        leaving.append(one)

    def sum_steps(n, stream, name):
        held, out = r["v" + name], r[name]
        s, first, width, way, hops = stream
        columns = pl.ds(p.cols[s][0] + first, width)
        G, came = r["G"], r["came%d" % n]
        onward, before = (ring(pos + way), m), (ring(pos - way), m)

        def step(t):
            def run():
                b = ring(pos + way * (hops - t))
                if t:
                    arrive(came.at[t - 1], "gg", (n, t - 1), before)
                if t == hops:
                    mine = pl.ds(first, width)
                    rest = G[b, :, columns] if hops < p.far else held[:, mine]
                    held[:, mine] = rest.astype(f32) + came[t - 1].astype(f32)
                    if hops == p.far:
                        if p.whole_lanes:
                            leave(held.at[:, mine], out.at[:, mine])
                        elif way < 0:
                            leave(held, out)
                    return
                if t:
                    value = G[b, :, columns].astype(f32) + came[t - 1].astype(f32)
                    G[b, :, columns] = value.astype(bf16)
                send(G.at[b, :, columns], came.at[t], "gg", (n, t), onward)

            return run

        return [step(t) for t in range(hops + 1)]

    def sum_streams(segment, name):
        return [
            sum_steps(n, stream, name) for n, stream in enumerate(p.streams) if stream[0] == segment
        ]

    grad_part(3, outlow[...], active)
    sums.add(3, sum_streams(3, "o_down"), 0, PT["sdp"])
    sums.run(0)
    gathers.need(3)
    for c in range(U // step):
        dact = nn(outlow[...], weight(3, c * step, step))
        il[:, pl.ds(c * step, step)] = (dact * slope[:, pl.ds(c * step, step)]).astype(bf16)
    rows_send(1, nt(il[...], weight(2)))

    grad_part(2, h2[...].reshape(tl, D), il)
    sums.add(2, sum_streams(2, "o_up"), PT["su"], PT["sup"])
    sums.run(PT["s1"])
    rows_send(2, nt(active[...], weight(3)))
    sums.run(PT["s2"])
    back2 = rows_sum(1)
    gm, ml = r["gm"], r["ml"]
    grad_middle = r["go"][own_rows, :] + norm_back(back2, n2[...], r2[:, 0:1], gain2)
    gm[...] = grad_middle
    ml[m] = grad_middle.astype(bf16)
    gather_send(1, ml)

    sums.run(PT["s3"])
    ln2g, ln2b = r["ln2g"], r["ln2b"]
    ln2g[...] = jnp.sum(back2 * n2[...], axis=0, keepdims=True)
    ln2b[...] = jnp.sum(back2, axis=0, keepdims=True)

    gather_end(1, ml)
    midlow = ml[...].reshape(tl, D)

    gs, gin, gall = r["gs"], r["gin"], r["gall"]
    gatt = nn(midlow, weight(1))
    for h in range(H):
        tile = gatt[:, (h // 2) * LANES : (h // 2 + 1) * LANES]
        even = h % 2 == 0
        first = tile[:half] if even else swap(tile[:half])
        second = swap(tile[half:]) if even else tile[half:]
        gs[h] = jnp.where(low, first, second).astype(bf16)
    for k in range(1, H):
        h = add(dh, k, H)
        send(gs.at[h], gin.at[dh], "ga", k, head_dev(h, di))
    gin[dh] = gs[dh]

    grad_part(1, midlow, att)
    sums.add(1, sum_streams(1, "o_out"), PT["so"], PT["sop"])
    sums.run(PT["s4"])
    for k in range(1, H):
        j = add(dh, H - k, H)
        arrive(gin.at[j], "ga", k, head_dev(j, di))

    inv_col = jnp.broadcast_to(inv[...], (LANES, NQ)).T
    shift_parts = []
    for j in range(H):
        packed = gin[j].astype(f32)
        top_half = jnp.where(low, 0.0, swap(packed))
        bottom = jnp.where(low, 0.0, packed)
        ga = jnp.concatenate([top_half, bottom], axis=0)
        gaT = ga.T[HEAD_DIM:, :]
        shift_parts.append(
            jnp.sum(gaT * attf[:, pl.ds(j * tl, tl)], axis=0, keepdims=True)
            * inv[:, pl.ds(j * tl, tl)]
        )
        gall[pl.ds(j * tl, tl), :] = (ga * inv_col[j * tl : (j + 1) * tl]).astype(bf16)
    shift = r["shift"]
    shift[...] = jnp.concatenate(shift_parts, axis=1)

    acc[...] = jnp.zeros((LANES, NQ), f32)
    dkvs, dkvx, dkvf = r["dkvs"], r["dkvx"], r["dkvf"]

    def key_grads(o):
        prob = r["prob"][o] if p.keep else jnp.exp(masked_scores(o) - top[...]).astype(bf16)
        dprob = nt(KV[o], gall[...])
        dscore = (prob.astype(f32) * (dprob - shift[...])).astype(bf16)
        acc[...] += nn(KVT[o], dscore)
        return nn(dscore, qall[...]) + nn(prob, gall[...])

    for q in range(1, g):
        member = add(di, q, g)
        for k in range(H):
            j = add(dh, k, H)
            dkvs[q, k] = key_grads(j * g + member).astype(bf16)
            send(dkvs.at[q, k], dkvx.at[q - 1, k], "dkvx", (q - 1, k), head_dev(dh, member))
            sums.run(PT["s4b"][k * len(PT["s4b"]) // H])
        sums.run(PT["s5"])
    for k in [*range(1, H), 0]:
        j = add(dh, k, H)
        dkv = key_grads(j * g + di)
        for q in range(1, g):
            arrive(dkvx.at[q - 1, k], "dkvx", (q - 1, k), head_dev(dh, add(di, g - q, g)))
            dkv = dkv + dkvx[q - 1, k].astype(f32)
        dkvf[pl.ds(pl.multiple_of(j * tl, tl), tl), :] = dkv
        sums.run(PT["s5b"][k * len(PT["s5b"]) // H])

    gmix = r["gmix"]
    dkv = swap(dkvf[...])
    gmix[:, pl.ds(0, LANES)] = jnp.where(low, acc[...].T * 0.125, dkv).astype(bf16)
    gmix[:, pl.ds(LANES, LANES)] = jnp.where(low, dkv, 0.0).astype(bf16)
    bps, bcx, byx, bzx = r["bps"], r["bcx"], r["byx"], r["bzx"]
    for k in [*range(1, H), 0]:
        j = add(dh, k, H)
        part = nt(gmix[pl.ds(pl.multiple_of(j * tl, tl), tl), :], head_weight)
        bps[j] = part.astype(bf16).reshape(M, rm, D)
        send(bps.at[j, m_both], bcx.at[j, 1], "bc", (k, 1), core)
        send(bps.at[j, m_core], bcx.at[j, 0], "bc", (k, 0), core)
    sums.run(PT["s6"])
    dws, dwx, dwin = r["dws"], r["dwx"], r["dwin"]
    dws[...] = tn(h1[...], gmix[...]).astype(bf16).reshape(R, rb, 2 * LANES)
    for q in range(1, g):
        member = add(di, q, g)
        for k in [*range(1, H), 0]:
            j = add(dh, k, H)
            send(dws.at[j * g + member], dwx.at[q - 1, k], "dwx", (q - 1, k), head_dev(dh, member))
    for k in [*range(1, H), 0]:
        j = add(dh, k, H)
        arrive(bcx.at[j, 1], "bc", (k, 1), core)
        value = bps[j, m_side].astype(f32) + bcx[j, 1].astype(f32)
        bps[j, m_side] = value.astype(bf16)
        send(bps.at[j, m_side], byx.at[j], "by", k, side)
    sums.run(PT["s7"])
    for k in [*range(1, H), 0]:
        j = add(dh, k, H)
        arrive(bcx.at[j, 0], "bc", (k, 0), core)
        arrive(byx.at[j], "by", k, side)
        value = bps[j, m].astype(f32) + bcx[j, 0].astype(f32) + byx[j].astype(f32)
        if k:
            bps[j, m] = value.astype(bf16)
            send(bps.at[j, m], bzx.at[dh], "bz", k, head_dev(j, di))
        else:
            back1 = value
    for k in [*range(1, H), 0]:
        j = add(dh, k, H)
        value = dws[j * g + di].astype(f32)
        for q in range(1, g):
            arrive(dwx.at[q - 1, k], "dwx", (q - 1, k), head_dev(dh, add(di, g - q, g)))
            value = value + dwx[q - 1, k].astype(f32)
        if k:
            dws[j * g + di] = value.astype(bf16)
            send(dws.at[j * g + di], dwin.at[dh], "dwz", k, head_dev(j, di))
        else:
            dwin[dh] = value.astype(bf16)
    sums.run(PT["s8"])

    res = r["res"]
    res[m] = (mid[...] + rows_sum(2)).astype(bf16)
    gather_send(2, res)

    sums.run(PT["s9"])
    for k in range(1, H):
        h = add(dh, H - k, H)
        arrive(bzx.at[h], "bz", k, head_dev(h, di))
        back1 = back1 + bzx[h].astype(f32)
    n1, r1 = norm(r["tok"][own_rows, :])
    gt = r["gt"]
    gt[m] = (gm[...] + norm_back(back1, n1, r1, gain1)).astype(bf16)
    gather_send(3, gt)
    ln_rows = jnp.concatenate(
        [
            jnp.sum(back1 * n1, axis=0, keepdims=True),
            jnp.sum(back1, axis=0, keepdims=True),
            ln2g[...],
            ln2b[...],
            jnp.zeros((4, D), f32),
        ],
        axis=0,
    )
    lnrow, lnr_in = r["lnrow"], r["lnr_in"]
    for b in range(D // LANES):
        lnrow[b] = ln_rows[:, b * LANES : (b + 1) * LANES]

    def lane_block(b):
        return b * rb // LANES

    for k in range(1, R):
        o = add(d, k, R)
        send(lnrow.at[lane_block(o)], lnr_in.at[d], "lr", k - 1, (o, m))
    lnr_in[d] = lnrow[lane_block(d)]
    sums.run(PT["s10"])
    for k in range(1, R):
        o = add(d, R - k, R)
        arrive(lnr_in.at[o], "lr", k - 1, (o, m))
    value = lnr_in[0]
    for b in range(1, R):
        value = value + lnr_in[b]
    gather_end(2, res)
    leave(res, r["o_result"])
    lnx = r["lnx"]
    lnx[m] = value
    for k in range(1, M):
        send(lnx.at[m], lnx.at[m], "ln", k - 1, row_peer(k))
    sums.run(100)
    for k in range(1, H):
        h = add(dh, H - k, H)
        arrive(dwin.at[h], "dwz", k, head_dev(h, di))
    vqkv = r["vo_qkv"]
    for t in range(H // 2):
        even0, even1, odd0, odd1 = (
            dwin[2 * t + b, :, pl.ds(c * LANES, LANES)].astype(f32) for b in (0, 1) for c in (0, 1)
        )
        vqkv[:, pl.ds(3 * t * LANES, LANES)] = even0
        vqkv[:, pl.ds((3 * t + 1) * LANES, LANES)] = jnp.where(low, even1, swap(odd0))
        vqkv[:, pl.ds((3 * t + 2) * LANES, LANES)] = jnp.where(low, swap(odd0), swap(odd1))
    leave(vqkv, r["o_qkv"])

    gather_end(3, gt)
    leave(gt, r["o_tokens"])
    for k in range(1, M):
        arrive(lnx.at[add(m, M - k, M)], "ln", k - 1, row_peer(M - k))
    value = lnx[0]
    for k in range(1, M):
        value = value + lnx[k]
    r["o_ln"][...] = value
    for one in leaving:
        one.wait()
    for one in sent:
        one.wait_send()


def layer(p, tokens, grad_out, w_qkv, w_out, w_up, w_down, ln_in, scene):
    R, M, L, H, g = p.R, p.M, p.L, p.H, p.g
    tl, D, rb, rm, U, HF, NQ = p.tl, p.D, p.rb, p.rm, p.U, p.HF, p.NQ
    half = tl // 2
    ins = {
        "tokens": tokens,
        "grad_out": grad_out,
        "w_qkv": w_qkv,
        "w_out": w_out,
        "w_up": w_up,
        "w_down": w_down,
        "ln_in": ln_in,
        "scene": scene,
    }
    outs = {
        "o_result": ((M, rm, D), bf16),
        "o_tokens": ((M, rm, D), bf16),
        "o_qkv": ((rb, 3 * HF), f32),
        "o_out": ((rb, HF), f32),
        "o_up": ((rb, U), f32),
        "o_down": ((rb, U), f32),
        "o_ln": ((8, LANES), f32),
    }
    v = pltpu.VMEM
    space = pl.BlockSpec(memory_space=pltpu.HBM)
    out_specs = [space] * 6 + [pl.BlockSpec(memory_space=pltpu.VMEM)]
    scratch = {
        "vo_qkv": v((rb, 3 * HF), f32),
        "vo_out": v((rb, HF), f32),
        "vo_up": v((rb, U), f32),
        "vo_down": v((rb, U), f32),
        "W": v((R, rb, p.WC), bf16),
        "tok": v((tl, D), f32),
        "go": v((tl, D), f32),
        "outlow": v((tl, D), bf16),
        "lnp": v((8, D), f32),
        "raw_qkv": v((rb, 3 * HF), bf16),
        "N": v((H, M, rm, D), bf16),
        "ws": v((H, rb, 2 * LANES), bf16),
        "Win": v((R, rb, 2 * LANES), bf16),
        "h1": v((NQ, D), bf16),
        "slope": v((tl, U), f32),
        "KV": v((R, tl, LANES), bf16),
        "KVT": v((R, LANES, tl), bf16),
        "qall": v((NQ, LANES), bf16),
        "top8": v((8, NQ), f32),
        "sum8": v((8, NQ), f32),
        "top": v((1, NQ), f32),
        "inv": v((1, NQ), f32),
        "shift": v((1, NQ), f32),
        "acc": v((LANES, NQ), f32),
        "attf": v((HEAD_DIM, NQ), f32),
        "atts": v((H, HEAD_DIM, tl), bf16),
        "attT": v((H, HEAD_DIM, tl), bf16),
        "att": v((tl, HF), bf16),
        "rs_send": v((3, M, rm, D), bf16),
        "rs_recv": v((3, M - 1, rm, D), bf16),
        "mid": v((rm, D), f32),
        "n2": v((rm, D), f32),
        "r2": v((rm, LANES), f32),
        "h2": v((M, rm, D), bf16),
        "active": v((tl, U), bf16),
        "il": v((tl, U), bf16),
        "gm": v((rm, D), f32),
        "ml": v((M, rm, D), bf16),
        "ln2g": v((1, D), f32),
        "ln2b": v((1, D), f32),
        "lnrow": v((D // LANES, 8, LANES), f32),
        "lnr_in": v((R, 8, LANES), f32),
        "lnx": v((M, 8, LANES), f32),
        "G": v((R, rb, p.WC), bf16),
        "gs": v((H, half, LANES), bf16),
        "gin": v((H, half, LANES), bf16),
        "gall": v((NQ, LANES), bf16),
        "dkvs": v((g, H, tl, LANES), bf16),
        "dkvx": v((max(g - 1, 1), H, tl, LANES), bf16),
        "dkvf": v((NQ, LANES), f32),
        "gmix": v((NQ, 2 * LANES), bf16),
        "bps": v((H, M, rm, D), bf16),
        "bcx": v((H, 2, rm, D), bf16),
        "byx": v((H, rm, D), bf16),
        "bzx": v((H, rm, D), bf16),
        "dws": v((R, rb, 2 * LANES), bf16),
        "dwx": v((max(g - 1, 1), H, rb, 2 * LANES), bf16),
        "dwin": v((H, rb, 2 * LANES), bf16),
        "res": v((M, rm, D), bf16),
        "gt": v((M, rm, D), bf16),
    }
    if p.keep:
        scratch["prob"] = v((R, tl, NQ), bf16)
    if p.whole_lanes:
        scratch["raw_out"] = v((HF, rb), bf16)
        scratch["raw_down"] = v((U, rb), bf16)
    for n, (_, _, width, _, hops) in enumerate(p.streams):
        scratch["came%d" % n] = v((hops, rb, width), bf16)
    sems = {
        "wg": (len(p.streams), p.far),
        "gg": (len(p.streams), p.far),
        "lr": (R - 1,),
        "na": (H,),
        "ny": (H,),
        "nc": (H,),
        "nd": (H,),
        "wa": (H,),
        "wax": (H, max(g - 1, 1)),
        "bc": (H, 2),
        "by": (H,),
        "bz": (H,),
        "dwz": (H,),
        "kvx": (H, max(g - 1, 1)),
        "att": (H,),
        "rs": (3, M - 1),
        "ag": (4, M - 1),
        "ga": (H,),
        "dkvx": (max(g - 1, 1), H),
        "dwx": (max(g - 1, 1), H),
        "ln": (M - 1,),
    }
    for name, shape in sems.items():
        scratch[name + "_s"] = pltpu.SemaphoreType.DMA(shape)
        scratch[name + "_r"] = pltpu.SemaphoreType.DMA(shape)
    scratch["out"] = pltpu.SemaphoreType.DMA((10,))
    scratch["loc"] = pltpu.SemaphoreType.DMA((6,))
    names = (*ins, *outs, *scratch)
    any_spec = pl.BlockSpec(memory_space=pltpu.HBM)
    flops = 6 * tl * D * p.WC + 14 * NQ * R * tl * HEAD_DIM
    return pl.pallas_call(
        functools.partial(kernel, p, names),
        out_shape=[jax.ShapeDtypeStruct(*one) for one in outs.values()],
        in_specs=[any_spec] * 6 + [pl.BlockSpec(memory_space=pltpu.VMEM), pl.BlockSpec(memory_space=pltpu.SMEM)],
        out_specs=out_specs,
        scratch_shapes=list(scratch.values()),
        compiler_params=pltpu.CompilerParams(
            collective_id=0, has_side_effects=True, vmem_limit_bytes=60 << 20
        ),
        cost_estimate=pl.CostEstimate(flops=flops, bytes_accessed=8 << 20, transcendentals=NQ * R * tl),
        name="layer",
    )(*ins.values())


def finish_kernel(*refs):
    hbm, outs, held, made, sem, done = refs[:7], refs[7:17], refs[17:24], refs[24:28], refs[28], refs[29]
    reads = [pltpu.make_async_copy(hbm[k], held[k], sem.at[k]) for k in range(7)]
    order = (5, 4, 2, 3, 0, 1, 6)
    for k in order:
        reads[k].start()
    writes = []
    forms = {
        0: (made[0], lambda v: v.reshape(-1, v.shape[-1]).astype(f32)),
        1: (made[1], lambda v: v.reshape(-1, v.shape[-1]).astype(f32)),
        3: (made[2], lambda v: v.T),
        5: (made[3], lambda v: v.T),
    }
    for k in order:
        reads[k].wait()
        if k == 6:
            for n in range(4):
                outs[6 + n][...] = held[6][n, :]
            break
        value = held[k]
        if k in forms:
            value, form = forms[k]
            value[...] = form(held[k][...])
        one = pltpu.make_async_copy(value, outs[k], done.at[k])
        one.start()
        writes.append(one)
    for one in writes:
        one.wait()


def finish(p, parts):
    tl, D, rb, U, HF = p.tl, p.D, p.rb, p.U, p.HF
    shapes = [(tl, D), (tl, D), (rb, 3 * HF), (HF, rb), (rb, U), (U, rb)] + [(rb,)] * 4
    held = [pltpu.VMEM(one.shape, one.dtype) for one in parts]
    made = [pltpu.VMEM(shapes[k], f32) for k in (0, 1, 3, 5)]
    return pl.pallas_call(
        finish_kernel,
        out_shape=[jax.ShapeDtypeStruct(shape, f32) for shape in shapes],
        in_specs=[pl.BlockSpec(memory_space=pltpu.HBM)] * 7,
        out_specs=[pl.BlockSpec(memory_space=pltpu.HBM)] * 6
        + [pl.BlockSpec(memory_space=pltpu.VMEM)] * 4,
        scratch_shapes=[*held, *made, pltpu.SemaphoreType.DMA((7,)), pltpu.SemaphoreType.DMA((6,))],
        compiler_params=pltpu.CompilerParams(vmem_limit_bytes=62 << 20),
        cost_estimate=pl.CostEstimate(flops=0, bytes_accessed=6 << 20, transcendentals=0),
        name="finish",
    )(*parts)


def on_device(
    tokens,
    w_qkv,
    w_out,
    w_up,
    w_down,
    ln1_gain,
    ln1_bias,
    ln2_gain,
    ln2_bias,
    scene_lengths,
    grad_out,
):
    p = Plan(tokens, w_qkv, w_up, scene_lengths, lax.axis_size("dp"), lax.axis_size("mp"))
    rb, D, tl = p.rb, p.D, p.tl
    vectors = jnp.stack([ln1_gain, ln1_bias, ln2_gain, ln2_bias])
    if not p.whole_lanes:
        vectors = lax.all_gather(vectors, "dp", axis=1, tiled=True)
        w_out, w_down = w_out.T, w_down.T
    vectors = jnp.pad(vectors, ((0, 12), (0, 0)))
    parts = layer(p, tokens, grad_out, w_qkv, w_out, w_up, w_down, vectors, scene_lengths)
    if p.whole_lanes:
        return finish(p, parts)
    result, grad_tokens, qkv, out, up, down, ln = parts
    first = lax.axis_index("dp") * rb % LANES
    ln = lax.dynamic_slice_in_dim(ln, first, rb, 1)
    return (
        result.reshape(tl, D).astype(f32),
        grad_tokens.reshape(tl, D).astype(f32),
        qkv,
        out.T,
        up,
        down.T,
        ln[0],
        ln[1],
        ln[2],
        ln[3],
    )


def solution(mesh):
    weights = (P("dp", "mp"), P("mp", "dp"), P("dp", "mp"), P("mp", "dp"))
    rows = P("dp", None)
    vector = P("dp")
    return jax.shard_map(
        on_device,
        mesh=mesh,
        in_specs=(rows, *weights, vector, vector, vector, vector, P(), rows),
        out_specs=(rows, rows, *weights, vector, vector, vector, vector),
        check_vma=False,
    )
```

```python
import functools
import types

import jax
import jax.numpy as jnp
from jax import lax
from jax.experimental import pallas as pl
from jax.experimental.pallas import tpu as pltpu
from jax.sharding import PartitionSpec as P

HEAD_DIM = 64
LANES = 128
FAR = -1e30
MESH = pl.DeviceIdType.MESH
class PT:
    g1b = -4.6
    g0 = 2.5
    o0 = 1.8
    op = 0.96
    u0 = 1.3
    d0 = 4.6
    g1 = 2.8
    g2 = 4.4
    g3 = -2.5
    g4 = [0.7, 3.5, 2.8, 1.2, 3.9, 1.3, 4.6, 5.2]
    g5 = [4.9, 5.2, 4.2, 5.1, 4.9, 5.1, 2.2, 4.4]
    g6 = -11.7
    g7 = -11.2
    g8 = 6.9
    g9 = 8.0
    su = 0.25
    s1 = -1.5
    s2 = 2.6
    s3 = 2.5
    so = 2.7
    sop = 1.6
    s4 = 4.2
    s4b = [-13.5, -6.9, -6.2, -7.4]
    s5 = -2.6
    s5b = [-11.2, -5.3, -2.7, -4.7]
    s6 = 5.3
    s7 = 6.0
    sq = 9.5
    sqp = 0.44
    up = 1.44
    dp = 1.0
    sdp = 1.56
    sup = 1.48
    s8 = 5.1
    s9 = -3.7
    s10 = 8.3


TWO_STEPS = (3,)
bf16 = jnp.bfloat16
f32 = jnp.float32


def nn(a, b):
    return lax.dot_general(a, b, (((1,), (0,)), ((), ())), preferred_element_type=f32)


def nt(a, b):
    return lax.dot_general(a, b, (((1,), (1,)), ((), ())), preferred_element_type=f32)


def tn(a, b):
    return lax.dot_general(a, b, (((0,), (0,)), ((), ())), preferred_element_type=f32)


class Plan:
    def __init__(self, tokens, w_qkv, w_up, scenes, dp, mp):
        self.R, self.M = dp, mp
        self.tl, self.D = tokens.shape
        self.rb = self.D // dp
        self.L = dp // 2
        self.H = w_qkv.shape[1] // (3 * HEAD_DIM)
        self.g = dp // self.H
        self.U = w_up.shape[1]
        self.rm = self.tl // mp
        self.HF = self.H * HEAD_DIM
        self.scenes = scenes.shape[0]
        self.NQ = self.H * self.tl
        self.keep = dp * self.tl <= 4096
        self.whole_lanes = self.rb % LANES == 0
        widths = (0, self.HF, self.U, self.U)
        self.cols = []
        start = 0
        for width in widths:
            self.cols.append((start, width))
            start += width
        self.WC = start
        far, near = dp // 2, dp - 1 - dp // 2
        self.far = far
        self.streams = []
        for s, width in enumerate(widths):
            half = width // 2
            if not width:
                continue
            for first, way in ((0, 1), (half, -1)):
                self.streams.append((s, first, half, way, far))
                self.streams.append((s, first, half, -way, near))


def kernel(p, names, *refs):
    r = types.SimpleNamespace(**dict(zip(names, refs)))
    R, M, L, H, g = p.R, p.M, p.L, p.H, p.g
    tl, D, rb, rm, U, HF, NQ = p.tl, p.D, p.rb, p.rm, p.U, p.HF, p.NQ
    half = tl // 2
    d = lax.axis_index("dp")
    m = lax.axis_index("mp")
    z, x = d // 2, lax.rem(d, 2)
    dh, di = d // g, lax.rem(d, g)
    sent = []

    def add(a, k, n):
        return lax.rem(a + k, n)

    def copy(src, dst, name, index, peer):
        return pltpu.make_async_remote_copy(
            src_ref=src,
            dst_ref=dst,
            send_sem=getattr(r, name + "_s").at[index],
            recv_sem=getattr(r, name + "_r").at[index],
            device_id=peer,
            device_id_type=MESH,
        )

    def send(src, dst, name, index, peer):
        one = copy(src, dst, name, index, peer)
        one.start()
        sent.append(one)

    def arrive(dst, name, index, peer):
        copy(dst, dst, name, index, peer).wait_recv()

    def head_dev(h, member):
        return (h * g + member, m)

    h_near, h_far = dh + 1 - 2 * lax.rem(dh, 2), lax.rem(dh + 2, H)
    h_both = lax.rem(h_near + 2, H)
    m_side, m_core = lax.rem(m + 2, M), m + 1 - 2 * lax.rem(m, 2)
    m_both = lax.rem(m_core + 2, M)
    side, core = (d, m_side), (d, m_core)

    def row_peer(k):
        return (d, add(m, k, M))

    pos = z + x * (R - 1 - 2 * z)

    def ring(q):
        q = lax.rem(q + 2 * R, R)
        far = q // L
        return 2 * q * (1 - far) + (2 * (R - 1 - q) + 1) * far

    W = r.W

    def wcols(b, c0, width):
        return W.at[b, :, pl.ds(c0, width)]

    local = []
    for n, (src, dst) in enumerate(
        [
            (r.w_qkv, r.raw_qkv),
            (r.tokens, r.tok),
            (r.w_up, wcols(d, *p.cols[2])),
            (r.w_out, r.raw_out if p.whole_lanes else wcols(d, *p.cols[1])),
            (r.w_down, r.raw_down if p.whole_lanes else wcols(d, *p.cols[3])),
            (r.grad_out, r.go),
        ]
    ):
        one = pltpu.make_async_copy(src, dst, r.loc.at[n])
        one.start()
        local.append(one)

    barrier = pltpu.get_barrier_semaphore()
    greeted = [head_dev(add(dh, k, H), di) for k in range(1, H)]
    greeted += [head_dev(dh, add(di, q, g)) for q in range(1, g)]
    greeted += [row_peer(k) for k in range(1, M)]
    if g != 2:
        greeted += [(ring(pos + 1), m), (ring(pos - 1), m)]
    for peer in greeted:
        pl.semaphore_signal(barrier, 1, device_id=peer, device_id_type=MESH)

    def norm(values):
        center = values - jnp.mean(values, axis=-1, keepdims=True)
        inverse = lax.rsqrt(jnp.mean(center * center, axis=-1, keepdims=True) + 1e-05)
        return center * inverse, inverse

    lane = lax.broadcasted_iota(jnp.int32, (1, LANES), 1)
    low = lane < HEAD_DIM

    def swap(v):
        return pltpu.roll(v, HEAD_DIM, 1)

    N, ws, Win = r.N, r.ws, r.Win
    local[0].wait()
    vectors = 0.0
    if p.whole_lanes:
        before = jnp.zeros((HEAD_DIM, rb), f32)
        after = jnp.zeros((HEAD_DIM - 16, rb), f32)
        vectors = jnp.concatenate([before, r.ln_in[...].astype(f32), after], axis=0).T
    for t in range(H // 2):
        t0, t1, t2 = (
            r.raw_qkv[:, pl.ds((3 * t + k) * LANES, LANES)].astype(f32) for k in range(3)
        )
        ws[2 * t, :, pl.ds(0, LANES)] = t0.astype(bf16)
        ws[2 * t, :, pl.ds(LANES, LANES)] = jnp.where(low, t1, vectors).astype(bf16)
        ws[2 * t + 1, :, pl.ds(0, LANES)] = jnp.where(low, swap(t1), swap(t2)).astype(bf16)
        ws[2 * t + 1, :, pl.ds(LANES, LANES)] = jnp.where(low, swap(t2), vectors).astype(bf16)
    local[1].wait()

    def norm_quarter(b):
        for c in range(rm // 32):
            first = pl.multiple_of(b * rm + c * 32, 32)
            N[dh, b, pl.ds(c * 32, 32), :] = norm(r.tok[pl.ds(first, 32), :])[0].astype(bf16)

    norm_quarter(m)
    pl.semaphore_wait(barrier, len(greeted))
    send(N.at[dh, m], N.at[dh, m], "na", 2, head_dev(h_far, di))
    send(N.at[dh, m], N.at[dh, m], "na", 1, head_dev(h_near, di))
    for k in range(1, H):
        h = add(dh, k, H)
        send(ws.at[h], Win.at[d], "wa", k, head_dev(h, di))
    Win[d] = ws[dh]
    for q in range(1, g):
        send(Win.at[d], Win.at[d], "wax", (0, q - 1), head_dev(dh, add(di, q, g)))

    class Queue:
        def __init__(self):
            self.steps = []

        def add(self, tag, streams, start, pace=1.0):
            for stream in streams:
                self.steps += [(start + pace * t, tag, run) for t, run in enumerate(stream)]
            self.steps.sort(key=lambda one: one[0])

        def run(self, place):
            while self.steps and self.steps[0][0] <= place:
                self.steps.pop(0)[2]()

        def need(self, tag):
            while any(one[1] == tag for one in self.steps):
                self.steps.pop(0)[2]()

    def gather_steps(block, name, index, way, hops):
        onward, before = (ring(pos + way), m), (ring(pos - way), m)

        def step(t):
            def run():
                here = block(ring(pos - way * t))
                if t:
                    arrive(here, name, (*index, t - 1), before)
                if t < hops:
                    send(here, here, name, (*index, t), onward)

            return run

        return [step(t) for t in range(hops + 1)]

    def gather_streams(segment):
        return [
            gather_steps(
                lambda b, s=s, first=first, width=width: wcols(b, p.cols[s][0] + first, width),
                "wg",
                (n,),
                way,
                hops,
            )
            for n, (s, first, width, way, hops) in enumerate(p.streams)
            if s == segment
        ]

    def weight(s, first=0, width=None):
        c0, full = p.cols[s]
        width = full if width is None else width
        return W[:, :, pl.ds(c0 + first, width)].reshape(D, width)

    gathers = Queue()
    lnp = r.lnp
    if not p.whole_lanes:
        lnp[...] = r.ln_in[...].astype(f32)[0:8, :]
    gathers.add(1, gather_streams(1), PT.o0, PT.op)
    gathers.add(2, gather_streams(2), PT.u0, PT.up)
    gathers.add(3, gather_streams(3), PT.d0, PT.dp)
    gathers.run(0)
    for k in range(1, M):
        norm_quarter(add(m, k, M))
    for n in range(2, 6):
        local[n].wait()
    if p.whole_lanes:
        for raw, (c0, width) in ((r.raw_out, p.cols[1]), (r.raw_down, p.cols[3])):
            W[d, :, pl.ds(c0, width)] = raw[...].astype(f32).T.astype(bf16)

    outlow = r.outlow
    outlow[...] = r.go[...].astype(bf16)

    passed = {1: (2, h_far, h_far), 2: (1, h_near, h_near), 3: (3, h_both, h_near)}
    for k in range(1, H):
        n, j, giver = passed[k]
        arrive(N.at[j, m], "na", n, head_dev(giver, di))
        if k == 1:
            send(N.at[j, m], N.at[j, m], "na", 3, head_dev(h_near, di))
        send(N.at[j, m], N.at[j, m], "ny", k, side)
        send(N.at[j, m], N.at[j, m], "nc", k, core)
        j = add(dh, H - k, H)
        own = j * g + di
        arrive(Win.at[own], "wa", k, head_dev(j, di))
        for q in range(1, g):
            send(Win.at[own], Win.at[own], "wax", (k, q - 1), head_dev(dh, add(di, q, g)))
        gathers.run(PT.g0)
    for k in range(1, H):
        j = passed[k][1]
        arrive(N.at[j, m_side], "ny", k, side)
        send(N.at[j, m_side], N.at[j, m_side], "nd", k, core)
    for k in range(H):
        j = add(dh, H - k, H)
        for q in range(1, g):
            member = add(di, g - q, g)
            arrive(Win.at[j * g + member], "wax", (k, q - 1), head_dev(dh, member))
    if p.whole_lanes:
        columns = Win[:, :, pl.ds(LANES, LANES)].reshape(D, LANES).astype(f32)
        lnp[...] = columns.T[HEAD_DIM : HEAD_DIM + 8, :]
    gain1, bias1, gain2, bias2 = (lnp[pl.ds(k, 1), :] for k in range(4))

    def norm_back(upstream, normed, inverse, gain):
        scaled = upstream * gain
        return inverse * (
            scaled
            - jnp.mean(scaled, axis=-1, keepdims=True)
            - normed * jnp.mean(scaled * normed, axis=-1, keepdims=True)
        )

    h1 = r.h1

    def hidden(j):
        part = N[j].reshape(tl, D).astype(f32) * gain1 + bias1
        h1[pl.ds(pl.multiple_of(j * tl, tl), tl), :] = part.astype(bf16)

    hidden(dh)
    gathers.run(PT.g1)
    for k in range(1, H):
        j = passed[k][1]
        arrive(N.at[j, m_core], "nc", k, core)
        arrive(N.at[j, m_both], "nd", k, core)
        hidden(j)
        gathers.run(PT.g1b)

    KV, qall, KVT = r.KV, r.qall, r.KVT
    head_weight = Win[...].reshape(D, 2 * LANES)
    for k in range(H):
        j = add(dh, H - k, H)
        rows = pl.ds(pl.multiple_of(j * tl, tl), tl)
        mixed = nn(h1[rows, :], head_weight)
        t0, t1 = mixed[:, :LANES], mixed[:, LANES:]
        qall[rows, :] = jnp.where(low, t0 * 0.125, 0.0).astype(bf16)
        KV[j * g + di] = jnp.where(low, swap(t0), swap(t1)).astype(bf16)
        for q in range(1, g):
            own = j * g + di
            send(KV.at[own], KV.at[own], "kvx", (k, q - 1), head_dev(dh, add(di, q, g)))
    gathers.run(PT.g2)
    for k in range(H):
        j = add(dh, H - k, H)
        for q in range(1, g):
            member = add(di, g - q, g)
            arrive(KV.at[j * g + member], "kvx", (k, q - 1), head_dev(dh, member))

    gathers.run(PT.g3)

    ends = []
    total = 0
    for k in range(p.scenes):
        total = total + r.scene[k]
        ends.append(total)

    def scene_of(pos):
        count = jnp.zeros(pos.shape, jnp.int32)
        for end in ends:
            count = count + (pos >= end).astype(jnp.int32)
        return count

    token_lane = lax.broadcasted_iota(jnp.int32, (1, tl), 1)
    q_scene = jnp.concatenate(
        [scene_of((j * g + di) * tl + token_lane) for j in range(H)], axis=1
    )
    token_row = lax.broadcasted_iota(jnp.int32, (tl, 1), 0)

    def masked_scores(o):
        scores = nt(KV[o], qall[...])
        return jnp.where(scene_of(o * tl + token_row) == q_scene, scores, FAR)

    unit = (
        lax.broadcasted_iota(jnp.int32, (LANES, LANES), 0)
        == lax.broadcasted_iota(jnp.int32, (LANES, LANES), 1)
    ).astype(bf16)

    top8, sum8, acc = r.top8, r.sum8, r.acc
    top8[...] = jnp.full((8, NQ), FAR, f32)
    sum8[...] = jnp.zeros((8, NQ), f32)
    acc[...] = jnp.zeros((LANES, NQ), f32)

    def maxima(o):
        KVT[o] = nt(unit, KV[o]).astype(bf16)
        top8[...] = jnp.maximum(
            top8[...], jnp.max(masked_scores(o).reshape(tl // 8, 8, NQ), axis=0)
        )

    pieces = 8 if R % 8 == 0 else 1

    def in_pieces(body, places):
        for c in range(pieces):
            pl.loop(c * R // pieces, (c + 1) * R // pieces)(body)
            gathers.run(places[c * len(places) // pieces])

    in_pieces(maxima, PT.g4)

    top = r.top
    top[...] = jnp.max(top8[...], axis=0, keepdims=True)

    def exponentials(o):
        expo = jnp.exp(masked_scores(o) - top[...])
        sum8[...] += jnp.sum(expo.reshape(tl // 8, 8, NQ), axis=0)
        low_expo = expo.astype(bf16)
        if p.keep:
            r.prob[o] = low_expo
        acc[...] += nn(KVT[o], low_expo)

    in_pieces(exponentials, PT.g5)

    scale_row = 1.0 / jnp.sum(sum8[...], axis=0, keepdims=True)
    inv = r.inv
    inv[...] = scale_row
    attf, atts, attT = r.attf, r.atts, r.attT
    attf[...] = acc[pl.ds(HEAD_DIM, HEAD_DIM), :] * scale_row
    for j in range(H):
        atts[j] = attf[:, pl.ds(j * tl, tl)].astype(bf16)
    for k in range(1, H):
        j = add(dh, k, H)
        send(atts.at[j], attT.at[dh], "att", k, head_dev(j, di))
    attT[dh] = atts[dh]
    gathers.run(PT.g6)
    for k in range(1, H):
        h = add(dh, H - k, H)
        arrive(attT.at[h], "att", k, head_dev(h, di))
    att = r.att
    att[...] = attT[...].reshape(HF, tl).astype(f32).T.astype(bf16)

    rs_send, rs_recv = r.rs_send, r.rs_recv

    def rows_send(n, values):
        rs_send[n] = values.astype(bf16).reshape(M, rm, D)
        for k in range(1, M):
            send(rs_send.at[n, add(m, k, M)], rs_recv.at[n, k - 1], "rs", (n, k - 1), row_peer(k))

    def rows_sum(n):
        value = rs_send[n, m].astype(f32)
        for k in range(1, M):
            arrive(rs_recv.at[n, k - 1], "rs", (n, k - 1), row_peer(M - k))
            value = value + rs_recv[n, k - 1].astype(f32)
        return value

    def gather_send(n, ref):
        if n in TWO_STEPS:
            send(ref.at[m], ref.at[m], "ah", (n, 0), side)
            send(ref.at[m], ref.at[m], "ah", (n, 1), core)
            return
        for k in range(1, M):
            send(ref.at[m], ref.at[m], "ag", (n, k - 1), row_peer(k))

    def gather_end(n, ref):
        if n in TWO_STEPS:
            arrive(ref.at[m_side], "ah", (n, 0), side)
            send(ref.at[m_side], ref.at[m_side], "ah", (n, 2), core)
            arrive(ref.at[m_core], "ah", (n, 1), core)
            arrive(ref.at[m_both], "ah", (n, 2), core)
            return
        for k in range(1, M):
            b = add(m, M - k, M)
            arrive(ref.at[b], "ag", (n, k - 1), row_peer(M - k))

    gathers.run(PT.g7)
    gathers.need(1)
    rows_send(0, nt(att[...], weight(1)))
    gathers.run(PT.g8)
    own_rows = pl.ds(pl.multiple_of(m * rm, rm), rm)
    mid, n2, r2, h2 = r.mid, r.n2, r.r2, r.h2
    middle = r.tok[own_rows, :] + rows_sum(0)
    mid[...] = middle
    normed, inverse = norm(middle)
    n2[...] = normed
    r2[...] = jnp.broadcast_to(inverse, (rm, LANES))
    h2[m] = (normed * gain2 + bias2).astype(bf16)
    gather_send(0, h2)
    gathers.run(PT.g9)
    gathers.need(2)
    gather_end(0, h2)

    active, il, slope = r.active, r.il, r.slope
    c_one, c_two = 0.7978845608028654, 0.044715
    step = 256
    for c in range(U // step):
        inner = nn(h2[...].reshape(tl, D), weight(2, c * step, step))
        square = inner * inner
        t = jnp.tanh(c_one * inner * (1.0 + c_two * square))
        cdf = 0.5 * (1.0 + t)
        active[:, pl.ds(c * step, step)] = (inner * cdf).astype(bf16)
        slope[:, pl.ds(c * step, step)] = cdf + 0.5 * inner * (1.0 - t * t) * (
            c_one + 3.0 * c_one * c_two * square
        )
    sums = Queue()

    def grad_part(s, lhs, rhs):
        c0, width = p.cols[s]
        G = r.G
        piece = 256 if width % 256 == 0 else LANES
        for c in range(width // piece):
            value = tn(lhs, rhs[:, pl.ds(c * piece, piece)]).astype(bf16)
            G[:, :, pl.ds(c0 + c * piece, piece)] = value.reshape(R, rb, piece)

    leaving = []

    def leave(value, out):
        one = pltpu.make_async_copy(value, out, r.out.at[len(leaving)])
        one.start()
        leaving.append(one)

    def sum_steps(n, stream, name):
        held, out = getattr(r, "v" + name), getattr(r, name)
        s, first, width, way, hops = stream
        columns = pl.ds(p.cols[s][0] + first, width)
        G, came = r.G, getattr(r, "came%d" % n)
        onward, before = (ring(pos + way), m), (ring(pos - way), m)

        def step(t):
            def run():
                b = ring(pos + way * (hops - t))
                if t:
                    arrive(came.at[t - 1], "gg", (n, t - 1), before)
                if t == hops:
                    mine = pl.ds(first, width)
                    rest = G[b, :, columns] if hops < p.far else held[:, mine]
                    held[:, mine] = rest.astype(f32) + came[t - 1].astype(f32)
                    if hops == p.far:
                        if p.whole_lanes:
                            leave(held.at[:, mine], out.at[:, mine])
                        elif way < 0:
                            leave(held, out)
                    return
                if t:
                    value = G[b, :, columns].astype(f32) + came[t - 1].astype(f32)
                    G[b, :, columns] = value.astype(bf16)
                send(G.at[b, :, columns], came.at[t], "gg", (n, t), onward)

            return run

        return [step(t) for t in range(hops + 1)]

    def sum_streams(segment, name):
        return [
            sum_steps(n, stream, name) for n, stream in enumerate(p.streams) if stream[0] == segment
        ]

    grad_part(3, outlow[...], active)
    sums.add(3, sum_streams(3, "o_down"), 0, PT.sdp)
    sums.run(0)
    gathers.need(3)
    for c in range(U // step):
        dact = nn(outlow[...], weight(3, c * step, step))
        il[:, pl.ds(c * step, step)] = (dact * slope[:, pl.ds(c * step, step)]).astype(bf16)
    rows_send(1, nt(il[...], weight(2)))

    grad_part(2, h2[...].reshape(tl, D), il)
    sums.add(2, sum_streams(2, "o_up"), PT.su, PT.sup)
    sums.run(PT.s1)
    rows_send(2, nt(active[...], weight(3)))
    sums.run(PT.s2)
    back2 = rows_sum(1)
    gm, ml = r.gm, r.ml
    grad_middle = r.go[own_rows, :] + norm_back(back2, n2[...], r2[:, 0:1], gain2)
    gm[...] = grad_middle
    ml[m] = grad_middle.astype(bf16)
    gather_send(1, ml)

    sums.run(PT.s3)
    ln2g, ln2b = r.ln2g, r.ln2b
    ln2g[...] = jnp.sum(back2 * n2[...], axis=0, keepdims=True)
    ln2b[...] = jnp.sum(back2, axis=0, keepdims=True)

    gather_end(1, ml)
    midlow = ml[...].reshape(tl, D)

    gs, gin, gall = r.gs, r.gin, r.gall
    gatt = nn(midlow, weight(1))
    for h in range(H):
        tile = gatt[:, (h // 2) * LANES : (h // 2 + 1) * LANES]
        even = h % 2 == 0
        first = tile[:half] if even else swap(tile[:half])
        second = swap(tile[half:]) if even else tile[half:]
        gs[h] = jnp.where(low, first, second).astype(bf16)
    for k in range(1, H):
        h = add(dh, k, H)
        send(gs.at[h], gin.at[dh], "ga", k, head_dev(h, di))
    gin[dh] = gs[dh]

    grad_part(1, midlow, att)
    sums.add(1, sum_streams(1, "o_out"), PT.so, PT.sop)
    sums.run(PT.s4)
    for k in range(1, H):
        j = add(dh, H - k, H)
        arrive(gin.at[j], "ga", k, head_dev(j, di))

    res = r.res
    res[m] = (mid[...] + rows_sum(2)).astype(bf16)
    gather_send(2, res)

    inv_col = jnp.broadcast_to(inv[...], (LANES, NQ)).T
    shift_parts = []
    for j in range(H):
        packed = gin[j].astype(f32)
        top_half = jnp.where(low, 0.0, swap(packed))
        bottom = jnp.where(low, 0.0, packed)
        ga = jnp.concatenate([top_half, bottom], axis=0)
        gaT = ga.T[HEAD_DIM:, :]
        shift_parts.append(
            jnp.sum(gaT * attf[:, pl.ds(j * tl, tl)], axis=0, keepdims=True)
            * inv[:, pl.ds(j * tl, tl)]
        )
        gall[pl.ds(j * tl, tl), :] = (ga * inv_col[j * tl : (j + 1) * tl]).astype(bf16)
    shift = r.shift
    shift[...] = jnp.concatenate(shift_parts, axis=1)

    acc[...] = jnp.zeros((LANES, NQ), f32)
    dkvs, dkvx, dkvf = r.dkvs, r.dkvx, r.dkvf

    def key_grads(o):
        prob = r.prob[o] if p.keep else jnp.exp(masked_scores(o) - top[...]).astype(bf16)
        dprob = nt(KV[o], gall[...])
        dscore = (prob.astype(f32) * (dprob - shift[...])).astype(bf16)
        acc[...] += nn(KVT[o], dscore)
        return nn(dscore, qall[...]) + nn(prob, gall[...])

    for q in range(1, g):
        member = add(di, q, g)
        for k in range(H):
            j = add(dh, k, H)
            dkvs[q, k] = key_grads(j * g + member).astype(bf16)
            send(dkvs.at[q, k], dkvx.at[q - 1, k], "dkvx", (q - 1, k), head_dev(dh, member))
            sums.run(PT.s4b[k * len(PT.s4b) // H])
        sums.run(PT.s5)
    for k in [*range(1, H), 0]:
        j = add(dh, k, H)
        dkv = key_grads(j * g + di)
        for q in range(1, g):
            arrive(dkvx.at[q - 1, k], "dkvx", (q - 1, k), head_dev(dh, add(di, g - q, g)))
            dkv = dkv + dkvx[q - 1, k].astype(f32)
        dkvf[pl.ds(pl.multiple_of(j * tl, tl), tl), :] = dkv
        sums.run(PT.s5b[k * len(PT.s5b) // H])

    gmix = r.gmix
    dkv = swap(dkvf[...])
    gmix[:, pl.ds(0, LANES)] = jnp.where(low, acc[...].T * 0.125, dkv).astype(bf16)
    gmix[:, pl.ds(LANES, LANES)] = jnp.where(low, dkv, 0.0).astype(bf16)
    bps, bcx, byx, bzx = r.bps, r.bcx, r.byx, r.bzx
    for k in [*range(1, H), 0]:
        j = add(dh, k, H)
        part = nt(gmix[pl.ds(pl.multiple_of(j * tl, tl), tl), :], head_weight)
        bps[j] = part.astype(bf16).reshape(M, rm, D)
        send(bps.at[j, m_both], bcx.at[j, 1], "bc", (k, 1), core)
        send(bps.at[j, m_core], bcx.at[j, 0], "bc", (k, 0), core)
    sums.run(PT.s6)
    dws, dwx, dwin = r.dws, r.dwx, r.dwin
    dws[...] = tn(h1[...], gmix[...]).astype(bf16).reshape(R, rb, 2 * LANES)
    for q in range(1, g):
        member = add(di, q, g)
        for k in [*range(1, H), 0]:
            j = add(dh, k, H)
            send(dws.at[j * g + member], dwx.at[q - 1, k], "dwx", (q - 1, k), head_dev(dh, member))
    for k in [*range(1, H), 0]:
        j = add(dh, k, H)
        arrive(bcx.at[j, 1], "bc", (k, 1), core)
        value = bps[j, m_side].astype(f32) + bcx[j, 1].astype(f32)
        bps[j, m_side] = value.astype(bf16)
        send(bps.at[j, m_side], byx.at[j], "by", k, side)
    sums.run(PT.s7)
    for k in [*range(1, H), 0]:
        j = add(dh, k, H)
        arrive(bcx.at[j, 0], "bc", (k, 0), core)
        arrive(byx.at[j], "by", k, side)
        value = bps[j, m].astype(f32) + bcx[j, 0].astype(f32) + byx[j].astype(f32)
        if k:
            bps[j, m] = value.astype(bf16)
            send(bps.at[j, m], bzx.at[dh], "bz", k, head_dev(j, di))
        else:
            back1 = value
    for k in [*range(1, H), 0]:
        j = add(dh, k, H)
        value = dws[j * g + di].astype(f32)
        for q in range(1, g):
            arrive(dwx.at[q - 1, k], "dwx", (q - 1, k), head_dev(dh, add(di, g - q, g)))
            value = value + dwx[q - 1, k].astype(f32)
        if k:
            dws[j * g + di] = value.astype(bf16)
            send(dws.at[j * g + di], dwin.at[dh], "dwz", k, head_dev(j, di))
        else:
            dwin[dh] = value.astype(bf16)
    sums.run(PT.s8)


    sums.run(PT.s9)
    for k in range(1, H):
        h = add(dh, H - k, H)
        arrive(bzx.at[h], "bz", k, head_dev(h, di))
        back1 = back1 + bzx[h].astype(f32)
    n1, r1 = norm(r.tok[own_rows, :])
    gt = r.gt
    gt[m] = (gm[...] + norm_back(back1, n1, r1, gain1)).astype(bf16)
    gather_send(3, gt)
    ln_rows = jnp.concatenate(
        [
            jnp.sum(back1 * n1, axis=0, keepdims=True),
            jnp.sum(back1, axis=0, keepdims=True),
            ln2g[...],
            ln2b[...],
            jnp.zeros((4, D), f32),
        ],
        axis=0,
    )
    lnrow, lnr_in = r.lnrow, r.lnr_in
    for b in range(D // LANES):
        lnrow[b] = ln_rows[:, b * LANES : (b + 1) * LANES]

    def lane_block(b):
        return b * rb // LANES

    for k in range(1, R):
        o = add(d, k, R)
        send(lnrow.at[lane_block(o)], lnr_in.at[d], "lr", k - 1, (o, m))
    lnr_in[d] = lnrow[lane_block(d)]
    sums.run(PT.s10)
    for k in range(1, R):
        o = add(d, R - k, R)
        arrive(lnr_in.at[o], "lr", k - 1, (o, m))
    value = lnr_in[0]
    for b in range(1, R):
        value = value + lnr_in[b]
    gather_end(2, res)
    leave(res, r.o_result)
    lnx = r.lnx
    lnx[m] = value
    for k in range(1, M):
        send(lnx.at[m], lnx.at[m], "ln", k - 1, row_peer(k))
    sums.run(100)
    for k in range(1, H):
        h = add(dh, H - k, H)
        arrive(dwin.at[h], "dwz", k, head_dev(h, di))
    vqkv = r.vo_qkv
    for t in range(H // 2):
        even0, even1, odd0, odd1 = (
            dwin[2 * t + b, :, pl.ds(c * LANES, LANES)].astype(f32) for b in (0, 1) for c in (0, 1)
        )
        vqkv[:, pl.ds(3 * t * LANES, LANES)] = even0
        vqkv[:, pl.ds((3 * t + 1) * LANES, LANES)] = jnp.where(low, even1, swap(odd0))
        vqkv[:, pl.ds((3 * t + 2) * LANES, LANES)] = jnp.where(low, swap(odd0), swap(odd1))
    leave(vqkv, r.o_qkv)

    gather_end(3, gt)
    leave(gt, r.o_tokens)
    for k in range(1, M):
        arrive(lnx.at[add(m, M - k, M)], "ln", k - 1, row_peer(M - k))
    value = lnx[0]
    for k in range(1, M):
        value = value + lnx[k]
    r.o_ln[...] = value
    for one in leaving:
        one.wait()
    for one in sent:
        one.wait_send()


def layer(p, tokens, grad_out, w_qkv, w_out, w_up, w_down, ln_in, scene):
    R, M, L, H, g = p.R, p.M, p.L, p.H, p.g
    tl, D, rb, rm, U, HF, NQ = p.tl, p.D, p.rb, p.rm, p.U, p.HF, p.NQ
    half = tl // 2
    ins = dict(
        tokens=tokens,
        grad_out=grad_out,
        w_qkv=w_qkv,
        w_out=w_out,
        w_up=w_up,
        w_down=w_down,
        ln_in=ln_in,
        scene=scene,
    )
    outs = dict(
        o_result=((M, rm, D), bf16),
        o_tokens=((M, rm, D), bf16),
        o_qkv=((rb, 3 * HF), f32),
        o_out=((rb, HF), f32),
        o_up=((rb, U), f32),
        o_down=((rb, U), f32),
        o_ln=((8, LANES), f32),
    )
    v = pltpu.VMEM
    space = pl.BlockSpec(memory_space=pltpu.HBM)
    out_specs = [space] * 6 + [pl.BlockSpec(memory_space=pltpu.VMEM)]
    scratch = dict(
        vo_qkv=v((rb, 3 * HF), f32),
        vo_out=v((rb, HF), f32),
        vo_up=v((rb, U), f32),
        vo_down=v((rb, U), f32),
        W=v((R, rb, p.WC), bf16),
        tok=v((tl, D), f32),
        go=v((tl, D), f32),
        outlow=v((tl, D), bf16),
        lnp=v((8, D), f32),
        raw_qkv=v((rb, 3 * HF), bf16),
        N=v((H, M, rm, D), bf16),
        ws=v((H, rb, 2 * LANES), bf16),
        Win=v((R, rb, 2 * LANES), bf16),
        h1=v((NQ, D), bf16),
        slope=v((tl, U), f32),
        KV=v((R, tl, LANES), bf16),
        KVT=v((R, LANES, tl), bf16),
        qall=v((NQ, LANES), bf16),
        top8=v((8, NQ), f32),
        sum8=v((8, NQ), f32),
        top=v((1, NQ), f32),
        inv=v((1, NQ), f32),
        shift=v((1, NQ), f32),
        acc=v((LANES, NQ), f32),
        attf=v((HEAD_DIM, NQ), f32),
        atts=v((H, HEAD_DIM, tl), bf16),
        attT=v((H, HEAD_DIM, tl), bf16),
        att=v((tl, HF), bf16),
        rs_send=v((3, M, rm, D), bf16),
        rs_recv=v((3, M - 1, rm, D), bf16),
        mid=v((rm, D), f32),
        n2=v((rm, D), f32),
        r2=v((rm, LANES), f32),
        h2=v((M, rm, D), bf16),
        active=v((tl, U), bf16),
        il=v((tl, U), bf16),
        gm=v((rm, D), f32),
        ml=v((M, rm, D), bf16),
        ln2g=v((1, D), f32),
        ln2b=v((1, D), f32),
        lnrow=v((D // LANES, 8, LANES), f32),
        lnr_in=v((R, 8, LANES), f32),
        lnx=v((M, 8, LANES), f32),
        G=v((R, rb, p.WC), bf16),
        gs=v((H, half, LANES), bf16),
        gin=v((H, half, LANES), bf16),
        gall=v((NQ, LANES), bf16),
        dkvs=v((g, H, tl, LANES), bf16),
        dkvx=v((max(g - 1, 1), H, tl, LANES), bf16),
        dkvf=v((NQ, LANES), f32),
        gmix=v((NQ, 2 * LANES), bf16),
        bps=v((H, M, rm, D), bf16),
        bcx=v((H, 2, rm, D), bf16),
        byx=v((H, rm, D), bf16),
        bzx=v((H, rm, D), bf16),
        dws=v((R, rb, 2 * LANES), bf16),
        dwx=v((max(g - 1, 1), H, rb, 2 * LANES), bf16),
        dwin=v((H, rb, 2 * LANES), bf16),
        res=v((M, rm, D), bf16),
        gt=v((M, rm, D), bf16),
    )
    if p.keep:
        scratch.update(prob=v((R, tl, NQ), bf16))
    if p.whole_lanes:
        scratch.update(raw_out=v((HF, rb), bf16))
        scratch.update(raw_down=v((U, rb), bf16))
    for n, (_, _, width, _, hops) in enumerate(p.streams):
        scratch["came%d" % n] = v((hops, rb, width), bf16)
    sems = dict(
        wg=(len(p.streams), p.far),
        gg=(len(p.streams), p.far),
        lr=(R - 1,),
        na=(H,),
        ny=(H,),
        nc=(H,),
        nd=(H,),
        wa=(H,),
        wax=(H, max(g - 1, 1)),
        bc=(H, 2),
        by=(H,),
        bz=(H,),
        dwz=(H,),
        kvx=(H, max(g - 1, 1)),
        att=(H,),
        rs=(3, M - 1),
        ag=(4, M - 1),
        ah=(4, 3),
        ga=(H,),
        dkvx=(max(g - 1, 1), H),
        dwx=(max(g - 1, 1), H),
        ln=(M - 1,),
    )
    for name, shape in sems.items():
        scratch[name + "_s"] = pltpu.SemaphoreType.DMA(shape)
        scratch[name + "_r"] = pltpu.SemaphoreType.DMA(shape)
    scratch.update(out=pltpu.SemaphoreType.DMA((10,)))
    scratch.update(loc=pltpu.SemaphoreType.DMA((6,)))
    names = (*ins, *outs, *scratch)
    any_spec = pl.BlockSpec(memory_space=pltpu.HBM)
    flops = 6 * tl * D * p.WC + 14 * NQ * R * tl * HEAD_DIM
    return pl.pallas_call(
        functools.partial(kernel, p, names),
        out_shape=[jax.ShapeDtypeStruct(*one) for one in outs.values()],
        in_specs=[any_spec] * 6 + [pl.BlockSpec(memory_space=pltpu.VMEM), pl.BlockSpec(memory_space=pltpu.SMEM)],
        out_specs=out_specs,
        scratch_shapes=list(scratch.values()),
        compiler_params=pltpu.CompilerParams(
            collective_id=0, has_side_effects=True, vmem_limit_bytes=60 << 20
        ),
        cost_estimate=pl.CostEstimate(flops=flops, bytes_accessed=8 << 20, transcendentals=NQ * R * tl),
        name="layer",
    )(*ins.values())


def finish_kernel(*refs):
    hbm, outs, held, made, sem, done = refs[:7], refs[7:17], refs[17:24], refs[24:28], refs[28], refs[29]
    reads = [pltpu.make_async_copy(hbm[k], held[k], sem.at[k]) for k in range(7)]
    order = (5, 4, 2, 3, 0, 1, 6)
    for k in order:
        reads[k].start()
    writes = []
    forms = {
        0: (made[0], lambda v: v.reshape(-1, v.shape[-1]).astype(f32)),
        1: (made[1], lambda v: v.reshape(-1, v.shape[-1]).astype(f32)),
        3: (made[2], lambda v: v.T),
        5: (made[3], lambda v: v.T),
    }
    for k in order:
        reads[k].wait()
        if k == 6:
            for n in range(4):
                outs[6 + n][...] = held[6][n, :]
            break
        value = held[k]
        if k in forms:
            value, form = forms[k]
            value[...] = form(held[k][...])
        one = pltpu.make_async_copy(value, outs[k], done.at[k])
        one.start()
        writes.append(one)
    for one in writes:
        one.wait()


def finish(p, parts):
    tl, D, rb, U, HF = p.tl, p.D, p.rb, p.U, p.HF
    shapes = [(tl, D), (tl, D), (rb, 3 * HF), (HF, rb), (rb, U), (U, rb)] + [(rb,)] * 4
    held = [pltpu.VMEM(one.shape, one.dtype) for one in parts]
    made = [pltpu.VMEM(shapes[k], f32) for k in (0, 1, 3, 5)]
    return pl.pallas_call(
        finish_kernel,
        out_shape=[jax.ShapeDtypeStruct(shape, f32) for shape in shapes],
        in_specs=[pl.BlockSpec(memory_space=pltpu.HBM)] * 7,
        out_specs=[pl.BlockSpec(memory_space=pltpu.HBM)] * 6
        + [pl.BlockSpec(memory_space=pltpu.VMEM)] * 4,
        scratch_shapes=[*held, *made, pltpu.SemaphoreType.DMA((7,)), pltpu.SemaphoreType.DMA((6,))],
        compiler_params=pltpu.CompilerParams(vmem_limit_bytes=62 << 20),
        cost_estimate=pl.CostEstimate(flops=0, bytes_accessed=6 << 20, transcendentals=0),
        name="finish",
    )(*parts)


def on_device(
    tokens,
    w_qkv,
    w_out,
    w_up,
    w_down,
    ln1_gain,
    ln1_bias,
    ln2_gain,
    ln2_bias,
    scene_lengths,
    grad_out,
):
    p = Plan(tokens, w_qkv, w_up, scene_lengths, lax.axis_size("dp"), lax.axis_size("mp"))
    rb, D, tl = p.rb, p.D, p.tl
    vectors = jnp.stack([ln1_gain, ln1_bias, ln2_gain, ln2_bias])
    if not p.whole_lanes:
        vectors = lax.all_gather(vectors, "dp", axis=1, tiled=True)
        w_out, w_down = w_out.T, w_down.T
    vectors = jnp.pad(vectors, ((0, 12), (0, 0)))
    parts = layer(p, tokens, grad_out, w_qkv, w_out, w_up, w_down, vectors, scene_lengths)
    if p.whole_lanes:
        return finish(p, parts)
    result, grad_tokens, qkv, out, up, down, ln = parts
    first = lax.axis_index("dp") * rb % LANES
    ln = lax.dynamic_slice_in_dim(ln, first, rb, 1)
    return (
        result.reshape(tl, D).astype(f32),
        grad_tokens.reshape(tl, D).astype(f32),
        qkv,
        out.T,
        up,
        down.T,
        ln[0],
        ln[1],
        ln[2],
        ln[3],
    )


def solution(mesh):
    weights = (P("dp", "mp"), P("mp", "dp"), P("dp", "mp"), P("mp", "dp"))
    rows = P("dp", None)
    vector = P("dp")
    return jax.shard_map(
        on_device,
        mesh=mesh,
        in_specs=(rows, *weights, vector, vector, vector, vector, P(), rows),
        out_specs=(rows, rows, *weights, vector, vector, vector, vector),
        check_vma=False,
    )
```

```python
import functools
import types

import jax
import jax.numpy as jnp
from jax import lax
from jax.experimental import pallas as pl
from jax.experimental.pallas import tpu as pltpu
from jax.sharding import PartitionSpec as P

HEAD_DIM = 64
LANES = 128
FAR = -1e30
MESH = pl.DeviceIdType.MESH
class PT:
    g1b = -4.6
    g0 = 2.5
    o0 = 1.8
    op = 0.96
    u0 = 1.3
    d0 = 4.6
    g1 = 2.8
    g2 = 4.4
    g3 = -2.5
    g4 = [0.7, 3.5, 2.8, 1.2, 3.9, 1.3, 4.6, 5.2]
    g5 = [4.9, 5.2, 4.2, 5.1, 4.9, 5.1, 2.2, 4.4]
    g6 = -11.7
    g7 = -11.2
    g8 = 6.9
    g9 = 8.0
    su = 0.25
    s1 = -1.5
    s2 = 2.6
    s3 = 2.5
    so = 2.7
    sop = 1.6
    s4 = 4.2
    s4b = [-13.5, -6.9, -6.2, -7.4]
    s5 = -2.6
    s5b = [-11.2, -5.3, -2.7, -4.7]
    s6 = 5.3
    s7 = 6.0
    sq = 9.5
    sqp = 0.44
    up = 1.44
    dp = 1.0
    sdp = 1.56
    sup = 1.48
    s8 = 5.1
    s9 = -3.7
    s10 = 8.3


TWO_STEPS = (0, 1, 3)
bf16 = jnp.bfloat16
f32 = jnp.float32


def nn(a, b):
    return lax.dot_general(a, b, (((1,), (0,)), ((), ())), preferred_element_type=f32)


def nt(a, b):
    return lax.dot_general(a, b, (((1,), (1,)), ((), ())), preferred_element_type=f32)


def tn(a, b):
    return lax.dot_general(a, b, (((0,), (0,)), ((), ())), preferred_element_type=f32)


class Plan:
    def __init__(self, tokens, w_qkv, w_up, scenes, dp, mp):
        self.R, self.M = dp, mp
        self.tl, self.D = tokens.shape
        self.rb = self.D // dp
        self.L = dp // 2
        self.H = w_qkv.shape[1] // (3 * HEAD_DIM)
        self.g = dp // self.H
        self.U = w_up.shape[1]
        self.rm = self.tl // mp
        self.HF = self.H * HEAD_DIM
        self.scenes = scenes.shape[0]
        self.NQ = self.H * self.tl
        self.keep = dp * self.tl <= 4096
        self.whole_lanes = self.rb % LANES == 0
        widths = (0, self.HF, self.U, self.U)
        self.cols = []
        start = 0
        for width in widths:
            self.cols.append((start, width))
            start += width
        self.WC = start
        far, near = dp // 2, dp - 1 - dp // 2
        self.far = far
        self.streams = []
        for s, width in enumerate(widths):
            half = width // 2
            if not width:
                continue
            for first, way in ((0, 1), (half, -1)):
                self.streams.append((s, first, half, way, far))
                self.streams.append((s, first, half, -way, near))


def kernel(p, names, *refs):
    r = types.SimpleNamespace(**dict(zip(names, refs)))
    R, M, L, H, g = p.R, p.M, p.L, p.H, p.g
    tl, D, rb, rm, U, HF, NQ = p.tl, p.D, p.rb, p.rm, p.U, p.HF, p.NQ
    half = tl // 2
    d = lax.axis_index("dp")
    m = lax.axis_index("mp")
    z, x = d // 2, lax.rem(d, 2)
    dh, di = d // g, lax.rem(d, g)
    sent = []

    def add(a, k, n):
        return lax.rem(a + k, n)

    def copy(src, dst, name, index, peer):
        return pltpu.make_async_remote_copy(
            src_ref=src,
            dst_ref=dst,
            send_sem=getattr(r, name + "_s").at[index],
            recv_sem=getattr(r, name + "_r").at[index],
            device_id=peer,
            device_id_type=MESH,
        )

    def send(src, dst, name, index, peer):
        one = copy(src, dst, name, index, peer)
        one.start()
        sent.append(one)

    def arrive(dst, name, index, peer):
        copy(dst, dst, name, index, peer).wait_recv()

    def head_dev(h, member):
        return (h * g + member, m)

    h_near, h_far = dh + 1 - 2 * lax.rem(dh, 2), lax.rem(dh + 2, H)
    h_both = lax.rem(h_near + 2, H)
    m_side, m_core = lax.rem(m + 2, M), m + 1 - 2 * lax.rem(m, 2)
    m_both = lax.rem(m_core + 2, M)
    side, core = (d, m_side), (d, m_core)

    def row_peer(k):
        return (d, add(m, k, M))

    pos = z + x * (R - 1 - 2 * z)

    def ring(q):
        q = lax.rem(q + 2 * R, R)
        far = q // L
        return 2 * q * (1 - far) + (2 * (R - 1 - q) + 1) * far

    W = r.W

    def wcols(b, c0, width):
        return W.at[b, :, pl.ds(c0, width)]

    local = []
    for n, (src, dst) in enumerate(
        [
            (r.w_qkv, r.raw_qkv),
            (r.tokens, r.tok),
            (r.w_up, wcols(d, *p.cols[2])),
            (r.w_out, r.raw_out if p.whole_lanes else wcols(d, *p.cols[1])),
            (r.w_down, r.raw_down if p.whole_lanes else wcols(d, *p.cols[3])),
            (r.grad_out, r.go),
        ]
    ):
        one = pltpu.make_async_copy(src, dst, r.loc.at[n])
        one.start()
        local.append(one)

    barrier = pltpu.get_barrier_semaphore()
    greeted = [head_dev(add(dh, k, H), di) for k in range(1, H)]
    greeted += [head_dev(dh, add(di, q, g)) for q in range(1, g)]
    greeted += [row_peer(k) for k in range(1, M)]
    if g != 2:
        greeted += [(ring(pos + 1), m), (ring(pos - 1), m)]
    for peer in greeted:
        pl.semaphore_signal(barrier, 1, device_id=peer, device_id_type=MESH)

    def norm(values):
        center = values - jnp.mean(values, axis=-1, keepdims=True)
        inverse = lax.rsqrt(jnp.mean(center * center, axis=-1, keepdims=True) + 1e-05)
        return center * inverse, inverse

    lane = lax.broadcasted_iota(jnp.int32, (1, LANES), 1)
    low = lane < HEAD_DIM

    def swap(v):
        return pltpu.roll(v, HEAD_DIM, 1)

    N, ws, Win = r.N, r.ws, r.Win
    local[0].wait()
    vectors = 0.0
    if p.whole_lanes:
        before = jnp.zeros((HEAD_DIM, rb), f32)
        after = jnp.zeros((HEAD_DIM - 8, rb), f32)
        row = lax.broadcasted_iota(jnp.int32, (8, rb), 0)
        eight = jnp.zeros((8, rb), f32)
        for k, one in enumerate((r.ln_a, r.ln_b, r.ln_c, r.ln_d)):
            eight = jnp.where(row == k, one[...].astype(f32), eight)
        vectors = jnp.concatenate([before, eight, after], axis=0).T
    for t in range(H // 2):
        t0, t1, t2 = (
            r.raw_qkv[:, pl.ds((3 * t + k) * LANES, LANES)].astype(f32) for k in range(3)
        )
        ws[2 * t, :, pl.ds(0, LANES)] = t0.astype(bf16)
        ws[2 * t, :, pl.ds(LANES, LANES)] = jnp.where(low, t1, vectors).astype(bf16)
        ws[2 * t + 1, :, pl.ds(0, LANES)] = jnp.where(low, swap(t1), swap(t2)).astype(bf16)
        ws[2 * t + 1, :, pl.ds(LANES, LANES)] = jnp.where(low, swap(t2), vectors).astype(bf16)
    local[1].wait()

    def norm_quarter(b):
        for c in range(rm // 32):
            first = pl.multiple_of(b * rm + c * 32, 32)
            N[dh, b, pl.ds(c * 32, 32), :] = norm(r.tok[pl.ds(first, 32), :])[0].astype(bf16)

    norm_quarter(m)
    pl.semaphore_wait(barrier, len(greeted))
    send(N.at[dh, m], N.at[dh, m], "na", 2, head_dev(h_far, di))
    send(N.at[dh, m], N.at[dh, m], "na", 1, head_dev(h_near, di))
    for k in range(1, H):
        h = add(dh, k, H)
        send(ws.at[h], Win.at[d], "wa", k, head_dev(h, di))
    Win[d] = ws[dh]
    for q in range(1, g):
        send(Win.at[d], Win.at[d], "wax", (0, q - 1), head_dev(dh, add(di, q, g)))

    class Queue:
        def __init__(self):
            self.steps = []

        def add(self, tag, streams, start, pace=1.0):
            for stream in streams:
                self.steps += [(start + pace * t, tag, run) for t, run in enumerate(stream)]
            self.steps.sort(key=lambda one: one[0])

        def run(self, place):
            while self.steps and self.steps[0][0] <= place:
                self.steps.pop(0)[2]()

        def need(self, tag):
            while any(one[1] == tag for one in self.steps):
                self.steps.pop(0)[2]()

    def gather_steps(block, name, index, way, hops):
        onward, before = (ring(pos + way), m), (ring(pos - way), m)

        def step(t):
            def run():
                here = block(ring(pos - way * t))
                if t:
                    arrive(here, name, (*index, t - 1), before)
                if t < hops:
                    send(here, here, name, (*index, t), onward)

            return run

        return [step(t) for t in range(hops + 1)]

    def gather_streams(segment):
        return [
            gather_steps(
                lambda b, s=s, first=first, width=width: wcols(b, p.cols[s][0] + first, width),
                "wg",
                (n,),
                way,
                hops,
            )
            for n, (s, first, width, way, hops) in enumerate(p.streams)
            if s == segment
        ]

    def weight(s, first=0, width=None):
        c0, full = p.cols[s]
        width = full if width is None else width
        return W[:, :, pl.ds(c0 + first, width)].reshape(D, width)

    gathers = Queue()
    lnp = r.lnp
    if not p.whole_lanes:
        lnp[...] = r.ln_in[...].astype(f32)[0:8, :]
    gathers.add(1, gather_streams(1), PT.o0, PT.op)
    gathers.add(2, gather_streams(2), PT.u0, PT.up)
    gathers.add(3, gather_streams(3), PT.d0, PT.dp)
    gathers.run(0)
    for k in range(1, M):
        norm_quarter(add(m, k, M))
    for n in range(2, 6):
        local[n].wait()
    if p.whole_lanes:
        for raw, (c0, width) in ((r.raw_out, p.cols[1]), (r.raw_down, p.cols[3])):
            W[d, :, pl.ds(c0, width)] = raw[...].astype(f32).T.astype(bf16)

    outlow = r.outlow
    outlow[...] = r.go[...].astype(bf16)

    passed = {1: (2, h_far, h_far), 2: (1, h_near, h_near), 3: (3, h_both, h_near)}
    for k in range(1, H):
        n, j, giver = passed[k]
        arrive(N.at[j, m], "na", n, head_dev(giver, di))
        if k == 1:
            send(N.at[j, m], N.at[j, m], "na", 3, head_dev(h_near, di))
        send(N.at[j, m], N.at[j, m], "ny", k, side)
        send(N.at[j, m], N.at[j, m], "nc", k, core)
        j = add(dh, H - k, H)
        own = j * g + di
        arrive(Win.at[own], "wa", k, head_dev(j, di))
        for q in range(1, g):
            send(Win.at[own], Win.at[own], "wax", (k, q - 1), head_dev(dh, add(di, q, g)))
        gathers.run(PT.g0)
    for k in range(1, H):
        j = passed[k][1]
        arrive(N.at[j, m_side], "ny", k, side)
        send(N.at[j, m_side], N.at[j, m_side], "nd", k, core)
    for k in range(H):
        j = add(dh, H - k, H)
        for q in range(1, g):
            member = add(di, g - q, g)
            arrive(Win.at[j * g + member], "wax", (k, q - 1), head_dev(dh, member))
    if p.whole_lanes:
        columns = Win[:, :, pl.ds(LANES, LANES)].reshape(D, LANES).astype(f32)
        lnp[...] = columns.T[HEAD_DIM : HEAD_DIM + 8, :]
    gain1, bias1, gain2, bias2 = (lnp[pl.ds(k, 1), :] for k in range(4))

    def norm_back(upstream, normed, inverse, gain):
        scaled = upstream * gain
        return inverse * (
            scaled
            - jnp.mean(scaled, axis=-1, keepdims=True)
            - normed * jnp.mean(scaled * normed, axis=-1, keepdims=True)
        )

    h1 = r.h1

    def hidden(j):
        part = N[j].reshape(tl, D).astype(f32) * gain1 + bias1
        h1[pl.ds(pl.multiple_of(j * tl, tl), tl), :] = part.astype(bf16)

    hidden(dh)
    gathers.run(PT.g1)
    for k in range(1, H):
        j = passed[k][1]
        arrive(N.at[j, m_core], "nc", k, core)
        arrive(N.at[j, m_both], "nd", k, core)
        hidden(j)
        gathers.run(PT.g1b)

    KV, qall, KVT = r.KV, r.qall, r.KVT
    head_weight = Win[...].reshape(D, 2 * LANES)
    for k in range(H):
        j = add(dh, H - k, H)
        rows = pl.ds(pl.multiple_of(j * tl, tl), tl)
        mixed = nn(h1[rows, :], head_weight)
        t0, t1 = mixed[:, :LANES], mixed[:, LANES:]
        qall[rows, :] = jnp.where(low, t0 * 0.125, 0.0).astype(bf16)
        KV[j * g + di] = jnp.where(low, swap(t0), swap(t1)).astype(bf16)
        for q in range(1, g):
            own = j * g + di
            send(KV.at[own], KV.at[own], "kvx", (k, q - 1), head_dev(dh, add(di, q, g)))
    gathers.run(PT.g2)
    for k in range(H):
        j = add(dh, H - k, H)
        for q in range(1, g):
            member = add(di, g - q, g)
            arrive(KV.at[j * g + member], "kvx", (k, q - 1), head_dev(dh, member))

    gathers.run(PT.g3)

    ends = []
    total = 0
    for k in range(p.scenes):
        total = total + r.scene[k]
        ends.append(total)

    def scene_of(pos):
        count = jnp.zeros(pos.shape, jnp.int32)
        for end in ends:
            count = count + (pos >= end).astype(jnp.int32)
        return count

    token_lane = lax.broadcasted_iota(jnp.int32, (1, tl), 1)
    q_scene = jnp.concatenate(
        [scene_of((j * g + di) * tl + token_lane) for j in range(H)], axis=1
    )
    token_row = lax.broadcasted_iota(jnp.int32, (tl, 1), 0)

    def masked_scores(o):
        scores = nt(KV[o], qall[...])
        return jnp.where(scene_of(o * tl + token_row) == q_scene, scores, FAR)

    unit = (
        lax.broadcasted_iota(jnp.int32, (LANES, LANES), 0)
        == lax.broadcasted_iota(jnp.int32, (LANES, LANES), 1)
    ).astype(bf16)

    top8, sum8, acc = r.top8, r.sum8, r.acc
    top8[...] = jnp.full((8, NQ), FAR, f32)
    sum8[...] = jnp.zeros((8, NQ), f32)
    acc[...] = jnp.zeros((LANES, NQ), f32)

    def maxima(o):
        KVT[o] = nt(unit, KV[o]).astype(bf16)
        top8[...] = jnp.maximum(
            top8[...], jnp.max(masked_scores(o).reshape(tl // 8, 8, NQ), axis=0)
        )

    pieces = 8 if R % 8 == 0 else 1

    def in_pieces(body, places):
        for c in range(pieces):
            pl.loop(c * R // pieces, (c + 1) * R // pieces)(body)
            gathers.run(places[c * len(places) // pieces])

    in_pieces(maxima, PT.g4)

    top = r.top
    top[...] = jnp.max(top8[...], axis=0, keepdims=True)

    def exponentials(o):
        expo = jnp.exp(masked_scores(o) - top[...])
        sum8[...] += jnp.sum(expo.reshape(tl // 8, 8, NQ), axis=0)
        low_expo = expo.astype(bf16)
        if p.keep:
            r.prob[o] = low_expo
        acc[...] += nn(KVT[o], low_expo)

    in_pieces(exponentials, PT.g5)

    scale_row = 1.0 / jnp.sum(sum8[...], axis=0, keepdims=True)
    inv = r.inv
    inv[...] = scale_row
    attf, atts, attT = r.attf, r.atts, r.attT
    attf[...] = acc[pl.ds(HEAD_DIM, HEAD_DIM), :] * scale_row
    for j in range(H):
        atts[j] = attf[:, pl.ds(j * tl, tl)].astype(bf16)
    for k in range(1, H):
        j = add(dh, k, H)
        send(atts.at[j], attT.at[dh], "att", k, head_dev(j, di))
    attT[dh] = atts[dh]
    gathers.run(PT.g6)
    for k in range(1, H):
        h = add(dh, H - k, H)
        arrive(attT.at[h], "att", k, head_dev(h, di))
    att = r.att
    att[...] = attT[...].reshape(HF, tl).astype(f32).T.astype(bf16)

    rs_send, rs_recv = r.rs_send, r.rs_recv

    def rows_send(n, values):
        rs_send[n] = values.astype(bf16).reshape(M, rm, D)
        for k in range(1, M):
            send(rs_send.at[n, add(m, k, M)], rs_recv.at[n, k - 1], "rs", (n, k - 1), row_peer(k))

    def rows_sum(n):
        value = rs_send[n, m].astype(f32)
        for k in range(1, M):
            arrive(rs_recv.at[n, k - 1], "rs", (n, k - 1), row_peer(M - k))
            value = value + rs_recv[n, k - 1].astype(f32)
        return value

    def gather_send(n, ref):
        if n in TWO_STEPS:
            send(ref.at[m], ref.at[m], "ah", (n, 0), side)
            send(ref.at[m], ref.at[m], "ah", (n, 1), core)
            return
        for k in range(1, M):
            send(ref.at[m], ref.at[m], "ag", (n, k - 1), row_peer(k))

    def gather_end(n, ref):
        if n in TWO_STEPS:
            arrive(ref.at[m_side], "ah", (n, 0), side)
            send(ref.at[m_side], ref.at[m_side], "ah", (n, 2), core)
            arrive(ref.at[m_core], "ah", (n, 1), core)
            arrive(ref.at[m_both], "ah", (n, 2), core)
            return
        for k in range(1, M):
            b = add(m, M - k, M)
            arrive(ref.at[b], "ag", (n, k - 1), row_peer(M - k))

    gathers.run(PT.g7)
    gathers.need(1)
    rows_send(0, nt(att[...], weight(1)))
    gathers.run(PT.g8)
    own_rows = pl.ds(pl.multiple_of(m * rm, rm), rm)
    mid, n2, r2, h2 = r.mid, r.n2, r.r2, r.h2
    middle = r.tok[own_rows, :] + rows_sum(0)
    mid[...] = middle
    normed, inverse = norm(middle)
    n2[...] = normed
    r2[...] = jnp.broadcast_to(inverse, (rm, LANES))
    h2[m] = (normed * gain2 + bias2).astype(bf16)
    gather_send(0, h2)
    gathers.run(PT.g9)
    gathers.need(2)
    gather_end(0, h2)

    active, il, slope = r.active, r.il, r.slope
    c_one, c_two = 0.7978845608028654, 0.044715
    step = 256
    for c in range(U // step):
        inner = nn(h2[...].reshape(tl, D), weight(2, c * step, step))
        square = inner * inner
        t = jnp.tanh(c_one * inner * (1.0 + c_two * square))
        cdf = 0.5 * (1.0 + t)
        active[:, pl.ds(c * step, step)] = (inner * cdf).astype(bf16)
        slope[:, pl.ds(c * step, step)] = cdf + 0.5 * inner * (1.0 - t * t) * (
            c_one + 3.0 * c_one * c_two * square
        )
    sums = Queue()

    def grad_part(s, lhs, rhs):
        c0, width = p.cols[s]
        G = r.G
        piece = 256 if width % 256 == 0 else LANES
        for c in range(width // piece):
            value = tn(lhs, rhs[:, pl.ds(c * piece, piece)]).astype(bf16)
            G[:, :, pl.ds(c0 + c * piece, piece)] = value.reshape(R, rb, piece)

    leaving = []

    def leave(value, out):
        one = pltpu.make_async_copy(value, out, r.out.at[len(leaving)])
        one.start()
        leaving.append(one)

    def sum_steps(n, stream, name):
        held, out = getattr(r, "v" + name), getattr(r, name)
        s, first, width, way, hops = stream
        columns = pl.ds(p.cols[s][0] + first, width)
        G, came = r.G, getattr(r, "came%d" % n)
        onward, before = (ring(pos + way), m), (ring(pos - way), m)

        def step(t):
            def run():
                b = ring(pos + way * (hops - t))
                if t:
                    arrive(came.at[t - 1], "gg", (n, t - 1), before)
                if t == hops:
                    mine = pl.ds(first, width)
                    rest = G[b, :, columns] if hops < p.far else held[:, mine]
                    held[:, mine] = rest.astype(f32) + came[t - 1].astype(f32)
                    if hops == p.far:
                        if p.whole_lanes:
                            leave(held.at[:, mine], out.at[:, mine])
                        elif way < 0:
                            leave(held, out)
                    return
                if t:
                    value = G[b, :, columns].astype(f32) + came[t - 1].astype(f32)
                    G[b, :, columns] = value.astype(bf16)
                send(G.at[b, :, columns], came.at[t], "gg", (n, t), onward)

            return run

        return [step(t) for t in range(hops + 1)]

    def sum_streams(segment, name):
        return [
            sum_steps(n, stream, name) for n, stream in enumerate(p.streams) if stream[0] == segment
        ]

    grad_part(3, outlow[...], active)
    sums.add(3, sum_streams(3, "o_down"), 0, PT.sdp)
    sums.run(0)
    gathers.need(3)
    for c in range(U // step):
        dact = nn(outlow[...], weight(3, c * step, step))
        il[:, pl.ds(c * step, step)] = (dact * slope[:, pl.ds(c * step, step)]).astype(bf16)
    rows_send(1, nt(il[...], weight(2)))

    grad_part(2, h2[...].reshape(tl, D), il)
    sums.add(2, sum_streams(2, "o_up"), PT.su, PT.sup)
    sums.run(PT.s1)
    rows_send(2, nt(active[...], weight(3)))
    sums.run(PT.s2)
    back2 = rows_sum(1)
    gm, ml = r.gm, r.ml
    grad_middle = r.go[own_rows, :] + norm_back(back2, n2[...], r2[:, 0:1], gain2)
    gm[...] = grad_middle
    ml[m] = grad_middle.astype(bf16)
    gather_send(1, ml)

    sums.run(PT.s3)
    ln2g, ln2b = r.ln2g, r.ln2b
    ln2g[...] = jnp.sum(back2 * n2[...], axis=0, keepdims=True)
    ln2b[...] = jnp.sum(back2, axis=0, keepdims=True)

    gather_end(1, ml)
    midlow = ml[...].reshape(tl, D)

    gs, gin, gall = r.gs, r.gin, r.gall
    gatt = nn(midlow, weight(1))
    for h in range(H):
        tile = gatt[:, (h // 2) * LANES : (h // 2 + 1) * LANES]
        even = h % 2 == 0
        first = tile[:half] if even else swap(tile[:half])
        second = swap(tile[half:]) if even else tile[half:]
        gs[h] = jnp.where(low, first, second).astype(bf16)
    for k in range(1, H):
        h = add(dh, k, H)
        send(gs.at[h], gin.at[dh], "ga", k, head_dev(h, di))
    gin[dh] = gs[dh]

    grad_part(1, midlow, att)
    sums.add(1, sum_streams(1, "o_out"), PT.so, PT.sop)
    sums.run(PT.s4)
    for k in range(1, H):
        j = add(dh, H - k, H)
        arrive(gin.at[j], "ga", k, head_dev(j, di))

    res = r.res
    res[m] = (mid[...] + rows_sum(2)).astype(bf16)
    gather_send(2, res)

    inv_col = jnp.broadcast_to(inv[...], (LANES, NQ)).T
    shift_parts = []
    for j in range(H):
        packed = gin[j].astype(f32)
        top_half = jnp.where(low, 0.0, swap(packed))
        bottom = jnp.where(low, 0.0, packed)
        ga = jnp.concatenate([top_half, bottom], axis=0)
        gaT = ga.T[HEAD_DIM:, :]
        shift_parts.append(
            jnp.sum(gaT * attf[:, pl.ds(j * tl, tl)], axis=0, keepdims=True)
            * inv[:, pl.ds(j * tl, tl)]
        )
        gall[pl.ds(j * tl, tl), :] = (ga * inv_col[j * tl : (j + 1) * tl]).astype(bf16)
    shift = r.shift
    shift[...] = jnp.concatenate(shift_parts, axis=1)

    acc[...] = jnp.zeros((LANES, NQ), f32)
    dkvs, dkvx, dkvf = r.dkvs, r.dkvx, r.dkvf

    def key_grads(o):
        prob = r.prob[o] if p.keep else jnp.exp(masked_scores(o) - top[...]).astype(bf16)
        dprob = nt(KV[o], gall[...])
        dscore = (prob.astype(f32) * (dprob - shift[...])).astype(bf16)
        acc[...] += nn(KVT[o], dscore)
        return nn(dscore, qall[...]) + nn(prob, gall[...])

    for q in range(1, g):
        member = add(di, q, g)
        for k in range(H):
            j = add(dh, k, H)
            dkvs[q, k] = key_grads(j * g + member).astype(bf16)
            send(dkvs.at[q, k], dkvx.at[q - 1, k], "dkvx", (q - 1, k), head_dev(dh, member))
            sums.run(PT.s4b[k * len(PT.s4b) // H])
        sums.run(PT.s5)
    for k in [*range(1, H), 0]:
        j = add(dh, k, H)
        dkv = key_grads(j * g + di)
        for q in range(1, g):
            arrive(dkvx.at[q - 1, k], "dkvx", (q - 1, k), head_dev(dh, add(di, g - q, g)))
            dkv = dkv + dkvx[q - 1, k].astype(f32)
        dkvf[pl.ds(pl.multiple_of(j * tl, tl), tl), :] = dkv
        sums.run(PT.s5b[k * len(PT.s5b) // H])

    gmix = r.gmix
    dkv = swap(dkvf[...])
    gmix[:, pl.ds(0, LANES)] = jnp.where(low, acc[...].T * 0.125, dkv).astype(bf16)
    gmix[:, pl.ds(LANES, LANES)] = jnp.where(low, dkv, 0.0).astype(bf16)
    bps, bcx, byx, bzx = r.bps, r.bcx, r.byx, r.bzx
    for k in [*range(1, H), 0]:
        j = add(dh, k, H)
        part = nt(gmix[pl.ds(pl.multiple_of(j * tl, tl), tl), :], head_weight)
        bps[j] = part.astype(bf16).reshape(M, rm, D)
        send(bps.at[j, m_both], bcx.at[j, 1], "bc", (k, 1), core)
        send(bps.at[j, m_core], bcx.at[j, 0], "bc", (k, 0), core)
    sums.run(PT.s6)
    dws, dwx, dwin = r.dws, r.dwx, r.dwin
    dws[...] = tn(h1[...], gmix[...]).astype(bf16).reshape(R, rb, 2 * LANES)
    for q in range(1, g):
        member = add(di, q, g)
        for k in [*range(1, H), 0]:
            j = add(dh, k, H)
            send(dws.at[j * g + member], dwx.at[q - 1, k], "dwx", (q - 1, k), head_dev(dh, member))
    for k in [*range(1, H), 0]:
        j = add(dh, k, H)
        arrive(bcx.at[j, 1], "bc", (k, 1), core)
        value = bps[j, m_side].astype(f32) + bcx[j, 1].astype(f32)
        bps[j, m_side] = value.astype(bf16)
        send(bps.at[j, m_side], byx.at[j], "by", k, side)
    sums.run(PT.s7)
    for k in [*range(1, H), 0]:
        j = add(dh, k, H)
        arrive(bcx.at[j, 0], "bc", (k, 0), core)
        arrive(byx.at[j], "by", k, side)
        value = bps[j, m].astype(f32) + bcx[j, 0].astype(f32) + byx[j].astype(f32)
        if k:
            bps[j, m] = value.astype(bf16)
            send(bps.at[j, m], bzx.at[dh], "bz", k, head_dev(j, di))
        else:
            back1 = value
    for k in [*range(1, H), 0]:
        j = add(dh, k, H)
        value = dws[j * g + di].astype(f32)
        for q in range(1, g):
            arrive(dwx.at[q - 1, k], "dwx", (q - 1, k), head_dev(dh, add(di, g - q, g)))
            value = value + dwx[q - 1, k].astype(f32)
        if k:
            dws[j * g + di] = value.astype(bf16)
            send(dws.at[j * g + di], dwin.at[dh], "dwz", k, head_dev(j, di))
        else:
            dwin[dh] = value.astype(bf16)
    sums.run(PT.s8)


    sums.run(PT.s9)
    for k in range(1, H):
        h = add(dh, H - k, H)
        arrive(bzx.at[h], "bz", k, head_dev(h, di))
        back1 = back1 + bzx[h].astype(f32)
    n1, r1 = norm(r.tok[own_rows, :])
    gt = r.gt
    gt[m] = (gm[...] + norm_back(back1, n1, r1, gain1)).astype(bf16)
    gather_send(3, gt)
    ln_rows = jnp.concatenate(
        [
            jnp.sum(back1 * n1, axis=0, keepdims=True),
            jnp.sum(back1, axis=0, keepdims=True),
            ln2g[...],
            ln2b[...],
            jnp.zeros((4, D), f32),
        ],
        axis=0,
    )
    lnrow, lnr_in = r.lnrow, r.lnr_in
    for b in range(D // LANES):
        lnrow[b] = ln_rows[:, b * LANES : (b + 1) * LANES]

    def lane_block(b):
        return b * rb // LANES

    for k in range(1, R):
        o = add(d, k, R)
        send(lnrow.at[lane_block(o)], lnr_in.at[d], "lr", k - 1, (o, m))
    lnr_in[d] = lnrow[lane_block(d)]
    sums.run(PT.s10)
    for k in range(1, R):
        o = add(d, R - k, R)
        arrive(lnr_in.at[o], "lr", k - 1, (o, m))
    value = lnr_in[0]
    for b in range(1, R):
        value = value + lnr_in[b]
    gather_end(2, res)
    leave(res, r.o_result)
    lnx = r.lnx
    lnx[m] = value
    for k in range(1, M):
        send(lnx.at[m], lnx.at[m], "ln", k - 1, row_peer(k))
    sums.run(100)
    for k in range(1, H):
        h = add(dh, H - k, H)
        arrive(dwin.at[h], "dwz", k, head_dev(h, di))
    vqkv = r.vo_qkv
    for t in range(H // 2):
        even0, even1, odd0, odd1 = (
            dwin[2 * t + b, :, pl.ds(c * LANES, LANES)].astype(f32) for b in (0, 1) for c in (0, 1)
        )
        vqkv[:, pl.ds(3 * t * LANES, LANES)] = even0
        vqkv[:, pl.ds((3 * t + 1) * LANES, LANES)] = jnp.where(low, even1, swap(odd0))
        vqkv[:, pl.ds((3 * t + 2) * LANES, LANES)] = jnp.where(low, swap(odd0), swap(odd1))
    leave(vqkv, r.o_qkv)

    gather_end(3, gt)
    leave(gt, r.o_tokens)
    for k in range(1, M):
        arrive(lnx.at[add(m, M - k, M)], "ln", k - 1, row_peer(M - k))
    value = lnx[0]
    for k in range(1, M):
        value = value + lnx[k]
    r.o_ln[...] = value
    for one in leaving:
        one.wait()
    for one in sent:
        one.wait_send()


def layer(p, tokens, grad_out, w_qkv, w_out, w_up, w_down, ln_in, scene):
    R, M, L, H, g = p.R, p.M, p.L, p.H, p.g
    tl, D, rb, rm, U, HF, NQ = p.tl, p.D, p.rb, p.rm, p.U, p.HF, p.NQ
    half = tl // 2
    ins = dict(
        tokens=tokens,
        grad_out=grad_out,
        w_qkv=w_qkv,
        w_out=w_out,
        w_up=w_up,
        w_down=w_down,
        **dict(zip(("ln_a", "ln_b", "ln_c", "ln_d") if p.whole_lanes else ("ln_in",), ln_in)),
        scene=scene,
    )
    outs = dict(
        o_result=((M, rm, D), bf16),
        o_tokens=((M, rm, D), bf16),
        o_qkv=((rb, 3 * HF), f32),
        o_out=((rb, HF), f32),
        o_up=((rb, U), f32),
        o_down=((rb, U), f32),
        o_ln=((8, LANES), f32),
    )
    v = pltpu.VMEM
    space = pl.BlockSpec(memory_space=pltpu.HBM)
    out_specs = [space] * 6 + [pl.BlockSpec(memory_space=pltpu.VMEM)]
    scratch = dict(
        vo_qkv=v((rb, 3 * HF), f32),
        vo_out=v((rb, HF), f32),
        vo_up=v((rb, U), f32),
        vo_down=v((rb, U), f32),
        W=v((R, rb, p.WC), bf16),
        tok=v((tl, D), f32),
        go=v((tl, D), f32),
        outlow=v((tl, D), bf16),
        lnp=v((8, D), f32),
        raw_qkv=v((rb, 3 * HF), bf16),
        N=v((H, M, rm, D), bf16),
        ws=v((H, rb, 2 * LANES), bf16),
        Win=v((R, rb, 2 * LANES), bf16),
        h1=v((NQ, D), bf16),
        slope=v((tl, U), f32),
        KV=v((R, tl, LANES), bf16),
        KVT=v((R, LANES, tl), bf16),
        qall=v((NQ, LANES), bf16),
        top8=v((8, NQ), f32),
        sum8=v((8, NQ), f32),
        top=v((1, NQ), f32),
        inv=v((1, NQ), f32),
        shift=v((1, NQ), f32),
        acc=v((LANES, NQ), f32),
        attf=v((HEAD_DIM, NQ), f32),
        atts=v((H, HEAD_DIM, tl), bf16),
        attT=v((H, HEAD_DIM, tl), bf16),
        att=v((tl, HF), bf16),
        rs_send=v((3, M, rm, D), bf16),
        rs_recv=v((3, M - 1, rm, D), bf16),
        mid=v((rm, D), f32),
        n2=v((rm, D), f32),
        r2=v((rm, LANES), f32),
        h2=v((M, rm, D), bf16),
        active=v((tl, U), bf16),
        il=v((tl, U), bf16),
        gm=v((rm, D), f32),
        ml=v((M, rm, D), bf16),
        ln2g=v((1, D), f32),
        ln2b=v((1, D), f32),
        lnrow=v((D // LANES, 8, LANES), f32),
        lnr_in=v((R, 8, LANES), f32),
        lnx=v((M, 8, LANES), f32),
        G=v((R, rb, p.WC), bf16),
        gs=v((H, half, LANES), bf16),
        gin=v((H, half, LANES), bf16),
        gall=v((NQ, LANES), bf16),
        dkvs=v((g, H, tl, LANES), bf16),
        dkvx=v((max(g - 1, 1), H, tl, LANES), bf16),
        dkvf=v((NQ, LANES), f32),
        gmix=v((NQ, 2 * LANES), bf16),
        bps=v((H, M, rm, D), bf16),
        bcx=v((H, 2, rm, D), bf16),
        byx=v((H, rm, D), bf16),
        bzx=v((H, rm, D), bf16),
        dws=v((R, rb, 2 * LANES), bf16),
        dwx=v((max(g - 1, 1), H, rb, 2 * LANES), bf16),
        dwin=v((H, rb, 2 * LANES), bf16),
        res=v((M, rm, D), bf16),
        gt=v((M, rm, D), bf16),
    )
    if p.keep:
        scratch.update(prob=v((R, tl, NQ), bf16))
    if p.whole_lanes:
        scratch.update(raw_out=v((HF, rb), bf16))
        scratch.update(raw_down=v((U, rb), bf16))
    for n, (_, _, width, _, hops) in enumerate(p.streams):
        scratch["came%d" % n] = v((hops, rb, width), bf16)
    sems = dict(
        wg=(len(p.streams), p.far),
        gg=(len(p.streams), p.far),
        lr=(R - 1,),
        na=(H,),
        ny=(H,),
        nc=(H,),
        nd=(H,),
        wa=(H,),
        wax=(H, max(g - 1, 1)),
        bc=(H, 2),
        by=(H,),
        bz=(H,),
        dwz=(H,),
        kvx=(H, max(g - 1, 1)),
        att=(H,),
        rs=(3, M - 1),
        ag=(4, M - 1),
        ah=(4, 3),
        ga=(H,),
        dkvx=(max(g - 1, 1), H),
        dwx=(max(g - 1, 1), H),
        ln=(M - 1,),
    )
    for name, shape in sems.items():
        scratch[name + "_s"] = pltpu.SemaphoreType.DMA(shape)
        scratch[name + "_r"] = pltpu.SemaphoreType.DMA(shape)
    scratch.update(out=pltpu.SemaphoreType.DMA((10,)))
    scratch.update(loc=pltpu.SemaphoreType.DMA((6,)))
    names = (*ins, *outs, *scratch)
    any_spec = pl.BlockSpec(memory_space=pltpu.HBM)
    flops = 6 * tl * D * p.WC + 14 * NQ * R * tl * HEAD_DIM
    return pl.pallas_call(
        functools.partial(kernel, p, names),
        out_shape=[jax.ShapeDtypeStruct(*one) for one in outs.values()],
        in_specs=[any_spec] * 6
        + [pl.BlockSpec(memory_space=pltpu.VMEM)] * len(ln_in)
        + [pl.BlockSpec(memory_space=pltpu.SMEM)],
        out_specs=out_specs,
        scratch_shapes=list(scratch.values()),
        compiler_params=pltpu.CompilerParams(
            collective_id=0, has_side_effects=True, vmem_limit_bytes=60 << 20
        ),
        cost_estimate=pl.CostEstimate(flops=flops, bytes_accessed=8 << 20, transcendentals=NQ * R * tl),
        name="layer",
    )(*ins.values())


def finish_kernel(*refs):
    hbm, outs, held, made, sem, done = refs[:7], refs[7:17], refs[17:24], refs[24:28], refs[28], refs[29]
    reads = [pltpu.make_async_copy(hbm[k], held[k], sem.at[k]) for k in range(7)]
    order = (5, 4, 2, 3, 0, 1, 6)
    for k in order:
        reads[k].start()
    writes = []
    forms = {
        0: (made[0], lambda v: v.reshape(-1, v.shape[-1]).astype(f32)),
        1: (made[1], lambda v: v.reshape(-1, v.shape[-1]).astype(f32)),
        3: (made[2], lambda v: v.T),
        5: (made[3], lambda v: v.T),
    }
    for k in order:
        reads[k].wait()
        if k == 6:
            for n in range(4):
                outs[6 + n][...] = held[6][n, :]
            break
        value = held[k]
        if k in forms:
            value, form = forms[k]
            value[...] = form(held[k][...])
        one = pltpu.make_async_copy(value, outs[k], done.at[k])
        one.start()
        writes.append(one)
    for one in writes:
        one.wait()


def finish(p, parts):
    tl, D, rb, U, HF = p.tl, p.D, p.rb, p.U, p.HF
    shapes = [(tl, D), (tl, D), (rb, 3 * HF), (HF, rb), (rb, U), (U, rb)] + [(rb,)] * 4
    held = [pltpu.VMEM(one.shape, one.dtype) for one in parts]
    made = [pltpu.VMEM(shapes[k], f32) for k in (0, 1, 3, 5)]
    return pl.pallas_call(
        finish_kernel,
        out_shape=[jax.ShapeDtypeStruct(shape, f32) for shape in shapes],
        in_specs=[pl.BlockSpec(memory_space=pltpu.HBM)] * 7,
        out_specs=[pl.BlockSpec(memory_space=pltpu.HBM)] * 6
        + [pl.BlockSpec(memory_space=pltpu.VMEM)] * 4,
        scratch_shapes=[*held, *made, pltpu.SemaphoreType.DMA((7,)), pltpu.SemaphoreType.DMA((6,))],
        compiler_params=pltpu.CompilerParams(vmem_limit_bytes=62 << 20),
        cost_estimate=pl.CostEstimate(flops=0, bytes_accessed=6 << 20, transcendentals=0),
        name="finish",
    )(*parts)


def on_device(
    tokens,
    w_qkv,
    w_out,
    w_up,
    w_down,
    ln1_gain,
    ln1_bias,
    ln2_gain,
    ln2_bias,
    scene_lengths,
    grad_out,
):
    p = Plan(tokens, w_qkv, w_up, scene_lengths, lax.axis_size("dp"), lax.axis_size("mp"))
    rb, D, tl = p.rb, p.D, p.tl
    vectors = [ln1_gain, ln1_bias, ln2_gain, ln2_bias]
    if p.whole_lanes:
        vectors = [one.reshape(1, rb) for one in vectors]
    else:
        vectors = lax.all_gather(jnp.stack(vectors), "dp", axis=1, tiled=True)
        vectors = [jnp.pad(vectors, ((0, 12), (0, 0)))]
        w_out, w_down = w_out.T, w_down.T
    parts = layer(p, tokens, grad_out, w_qkv, w_out, w_up, w_down, vectors, scene_lengths)
    if p.whole_lanes:
        return finish(p, parts)
    result, grad_tokens, qkv, out, up, down, ln = parts
    first = lax.axis_index("dp") * rb % LANES
    ln = lax.dynamic_slice_in_dim(ln, first, rb, 1)
    return (
        result.reshape(tl, D).astype(f32),
        grad_tokens.reshape(tl, D).astype(f32),
        qkv,
        out.T,
        up,
        down.T,
        ln[0],
        ln[1],
        ln[2],
        ln[3],
    )


def solution(mesh):
    weights = (P("dp", "mp"), P("mp", "dp"), P("dp", "mp"), P("mp", "dp"))
    rows = P("dp", None)
    vector = P("dp")
    return jax.shard_map(
        on_device,
        mesh=mesh,
        in_specs=(rows, *weights, vector, vector, vector, vector, P(), rows),
        out_specs=(rows, rows, *weights, vector, vector, vector, vector),
        check_vma=False,
    )
```
